32 devices in a mesh: gx: 8 (over z, x), gy: 4 (over y, core).
Axes of the slice: x: 2, y: 2, z: 4, core: 2. Of those that a mesh axis runs over, the one named last changes fastest.
Arguments:
- guess: float32 [128, 128, 256], P('gx', 'gy'), may hold values from -6 to 6
- right_side: float32 [128, 128, 256], P('gx', 'gy'), may hold values from -6 to 6
- coefficient: float32 [128, 128, 256], P('gx', 'gy'), may hold values from 0.3 to 3
Outputs:
- solution: float32 [128, 128, 256], P('gx', 'gy')
The draws below stay inside these ranges and needn't reach their ends.
All inputs are finite; a program needn't handle non-finite values.
Results may differ from the reference program's by a relative error of at most 0.0001.
Values sent between devices are 32-bit elements; how exact they have to be, the bound alone decides.
No kernel may reach another device: no remote copies, remote signals or barrier semaphores. Data moves between devices by JAX's collectives and lax.ppermute only.
A program may use at most 128 MiB of HBM per device.

```python
import math
import jax
import jax.numpy as jnp

LEVELS = 4
SWEEPS = 3
CHEB = 8
NX = 128
NY = 128
NZ = 256


def draw_right_side(key, part):
    result = jnp.clip(jax.random.normal(key, (NX, NY, NZ), jnp.float32), -6.0, 6.0)
    return result


def levels(rng, dims, pieces, smallest, top_value):
    factor_of, own = 1.0, jax.random.fold_in(rng, 6)
    for axis_at, parts in pieces:
        steps = jnp.exp(jax.random.uniform(jax.random.fold_in(own, axis_at), (parts,), jnp.float32, smallest / len(pieces), top_value / len(pieces)))
        factor_of = factor_of * jnp.repeat(steps, dims[axis_at] // parts).reshape([-1 if axis == axis_at else 1 for axis in range(len(dims))])
    return factor_of


def noise(stream_key, shape, width, reach, cuts=(), held_as=jnp.bfloat16):
    gain = levels(stream_key, shape, cuts, -0.22, 0.18) if cuts else 1.0
    drawn = jax.random.normal(stream_key, shape, jnp.float32) * width * gain
    return jnp.minimum(jnp.maximum(drawn, -reach), reach).astype(held_as)


def setup_inputs(seed: int = 0) -> dict:
    arg_keys = jax.random.split(jax.random.key(seed), 4)
    return {
        "guess": noise(arg_keys[0], (NX, NY, NZ), 1.0, 6.0, ((0, 8), (1, 4)), jnp.float32),
        "right_side": draw_right_side(jax.random.fold_in(arg_keys[3], 71), 0),
        "coefficient": jnp.clip(jnp.exp(math.log(3.0) - 2.3025851 * jax.random.uniform(arg_keys[2], (NX, NY, NZ), jnp.float32) ** levels(arg_keys[2], (NX, NY, NZ), ((0, 8), (1, 4)), -0.2, 0.2)), 0.3, 3.0),
    }


RELAX_WEIGHT = 0.7
CHEBY_LOWER = 0.08
CHEBY_UPPER = 2.0


def offset_view(array, direction, offset):
    selector = [slice(1, -1), slice(1, -1), slice(1, -1)]
    selector[direction] = slice(1 + offset, array.shape[direction] - 1 + offset)
    return array[tuple(selector)]


def apply_operator(padded_field, padded_coef, factor):
    center_coef = padded_coef[1:-1, 1:-1, 1:-1]
    center_value = padded_field[1:-1, 1:-1, 1:-1]
    summed = jnp.zeros(center_value.shape, jnp.float32)
    for direction in range(3):
        for offset in (-1, 1):
            near_coef = offset_view(padded_coef, direction, offset)
            near_value = offset_view(padded_field, direction, offset)
            summed = summed + 0.5 * (center_coef + near_coef) * (center_value - near_value)
    return factor * summed


def diagonal_of(padded_coef, factor):
    center_coef = padded_coef[1:-1, 1:-1, 1:-1]
    summed = jnp.zeros(center_coef.shape, jnp.float32)
    for direction in range(3):
        for offset in (-1, 1):
            summed = summed + 0.5 * (center_coef + offset_view(padded_coef, direction, offset))
    return factor * summed


def zero_pad(array):
    return jnp.pad(array, 1)


def smooth(iterate, source, padded_coef, diagonal, factor, pad_field, zero_start):
    for sweep_index in range(SWEEPS):
        if sweep_index == 0 and zero_start:
            iterate = RELAX_WEIGHT * source / diagonal
        else:
            image = apply_operator(pad_field(iterate), padded_coef, factor)
            iterate = iterate + RELAX_WEIGHT * (source - image) / diagonal
    return iterate


def restrict(array):
    extent = array.shape
    blocks = array.reshape(extent[0] // 2, 2, extent[1] // 2, 2, extent[2] // 2, 2)
    return blocks.mean(axis=(1, 3, 5))


def prolong(array):
    return jnp.repeat(jnp.repeat(jnp.repeat(array, 2, 0), 2, 1), 2, 2)


def chebyshev(source, padded_coef, diagonal, factor):
    center_value = (CHEBY_UPPER + CHEBY_LOWER) / 2.0
    half_width = (CHEBY_UPPER - CHEBY_LOWER) / 2.0
    ratio_sigma = center_value / half_width
    weight_old = 1.0 / ratio_sigma
    iterate = jnp.zeros(source.shape, jnp.float32)
    residual = source
    direction_field = residual / diagonal / center_value
    for step_index in range(CHEB):
        iterate = iterate + direction_field
        residual = residual - apply_operator(zero_pad(direction_field), padded_coef, factor)
        weight_new = 1.0 / (2.0 * ratio_sigma - weight_old)
        direction_field = weight_new * weight_old * direction_field + (2.0 * weight_new / half_width) * (residual / diagonal)
        weight_old = weight_new
    return iterate


def reference(guess, right_side, coefficient):
    padded_coef = zero_pad(coefficient)
    diagonal = diagonal_of(padded_coef, 1.0)
    iterate = smooth(guess, right_side, padded_coef, diagonal, 1.0, zero_pad, False)
    entries = [(iterate, right_side, padded_coef, diagonal, 1.0)]
    residual = right_side - apply_operator(zero_pad(iterate), padded_coef, 1.0)
    coarse_coef = coefficient
    for level_index in range(1, LEVELS):
        factor = 0.25 ** level_index
        source = restrict(residual)
        coarse_coef = restrict(coarse_coef)
        padded_coef = zero_pad(coarse_coef)
        diagonal = diagonal_of(padded_coef, factor)
        iterate = smooth(jnp.zeros_like(source), source, padded_coef, diagonal, factor, zero_pad, True)
        residual = source - apply_operator(zero_pad(iterate), padded_coef, factor)
        entries.append((iterate, source, padded_coef, diagonal, factor))
    factor = 0.25 ** LEVELS
    source = restrict(residual)
    coarse_coef = restrict(coarse_coef)
    padded_coef = zero_pad(coarse_coef)
    diagonal = diagonal_of(padded_coef, factor)
    correction = chebyshev(source, padded_coef, diagonal, factor)
    for entry in reversed(entries):
        iterate, source, padded_coef, diagonal, factor = entry
        iterate = iterate + prolong(correction)
        correction = smooth(iterate, source, padded_coef, diagonal, factor, zero_pad, False)
    return correction
```

```python
from functools import partial

import jax
import jax.numpy as jnp
from jax import lax
from jax.experimental import pallas as pl
from jax.experimental.pallas import tpu as pltpu
from jax.sharding import PartitionSpec as P

LEVELS = 4
SWEEPS = 3
CHEB = 8

RELAX_WEIGHT = 0.7
CHEBY_LOWER = 0.08
CHEBY_UPPER = 2.0

F32 = jnp.float32
LANES = 128
FINE = SWEEPS + 1
COARSE = 8
SOURCE = COARSE - 1
POST = SWEEPS
VMEM_LIMIT = 56 * 1024 * 1024


def dot(a, b):
    return jnp.dot(a, b, precision=lax.Precision.HIGHEST, preferred_element_type=F32)


def iota(shape, dim):
    return lax.broadcasted_iota(jnp.int32, shape, dim)


def vmem(*shape):
    return pltpu.VMEM(shape, F32)


def roll(x, by, axis):
    return pltpu.roll(x, by % x.shape[axis], axis)


def weigh(coef, weights, scaled, diag, source, first, last, depth, row_edges, scale, omega):
    rows, lanes = coef.shape[1:]
    lane = iota((1, lanes), 1) % depth
    front, back = lane == 0, lane == depth - 1
    row = iota((rows, 1), 0)

    def step(p, carry):
        c = coef[p]
        lower, upper = coef[p - 1], coef[p + 1]
        left, right = roll(c, 1, 0), roll(c, -1, 0)
        near, far = roll(c, 1, 1), roll(c, -1, 1)
        near, far = jnp.where(front, 0.0, near), jnp.where(back, 0.0, far)
        if row_edges:
            left, right = jnp.where(row == 0, 0.0, left), jnp.where(row == rows - 1, 0.0, right)
        total = 6.0 * c + ((lower + upper) + (left + right) + (near + far))
        inverse = jnp.where(c > 0.0, omega / total, 0.0)
        weights[0, p] = (c + lower) * inverse
        weights[1, p] = (c + upper) * inverse
        left, right = (c + left) * inverse, (c + right) * inverse
        if row_edges:
            left, right = jnp.where(row == 0, 0.0, left), jnp.where(row == rows - 1, 0.0, right)
        weights[2, p] = left
        weights[3, p] = right
        weights[4, p] = jnp.where(front, 0.0, (c + near) * inverse)
        weights[5, p] = jnp.where(back, 0.0, (c + far) * inverse)
        scaled[p] = source(p) * inverse * (2.0 / scale)
        if diag is not None:
            diag[p] = total * (0.5 * scale / omega)
        return carry

    lax.fori_loop(first, last, step, 0)


def neighbours(field, weights, p):
    v = field[p]
    total = weights[0, p] * field[p - 1] + weights[1, p] * field[p + 1]
    total += weights[2, p] * roll(v, 1, 0) + weights[3, p] * roll(v, -1, 0)
    return v, total + (weights[4, p] * roll(v, 1, 1) + weights[5, p] * roll(v, -1, 1))


def sweep(field, out, weights, scaled, first, last):
    def step(p, carry):
        v, total = neighbours(field, weights, p)
        out[p] = (1.0 - RELAX_WEIGHT) * v + (scaled[p] + total)
        return carry

    lax.fori_loop(first, last, step, 0)


def residual(field, weights, scaled, diag, p):
    v, total = neighbours(field, weights, p)
    return (scaled[p] + total - RELAX_WEIGHT * v) * diag[p]


def halve_lanes(lanes, width, offset=0):
    return jnp.where(iota((lanes, width), 0) // 2 + offset == iota((lanes, width), 1), 0.125, 0.0).astype(F32)


def pair_rows(ref, count):
    return ref[pl.ds(0, count, stride=2), :] + ref[pl.ds(1, count, stride=2), :]


def fine_pre_kernel(guess, source, coef, low, high, left, right,
                    out, weights, scaled, up, down, b1, c1, v, c, w, diag, pairs, halved):
    nx, ny, nz = guess.shape
    planes = nx + 2 * FINE

    def fill(target, own, base, width):
        at = FINE - width
        count = nx + 2 * width
        offset = sum(nx + 2 * k for k in base)
        message = sum(base)

        def rest(k, carry):
            target[at + k, ny:] = jnp.concatenate((right[offset + k], left[offset + k]), 0)
            return carry

        lax.fori_loop(0, count, rest, 0)

        def main(k, carry):
            target[FINE + k, :ny] = own[k]
            return carry

        lax.fori_loop(0, nx, main, 0)
        for k in range(width):
            target[at + k, :ny] = low[message + k]
            target[FINE + nx + k, :ny] = high[message + k]

    fill(v, guess, (), FINE)
    fill(scaled, source, (FINE,), FINE - 1)
    fill(c, coef, (FINE, FINE - 1), FINE)
    weigh(c, weights, scaled, diag, lambda p: scaled[p], 1, planes - 1, nz, False, 1.0, RELAX_WEIGHT)
    sweep(v, w, weights, scaled, 1, planes - 1)
    sweep(w, v, weights, scaled, 2, planes - 2)
    sweep(v, w, weights, scaled, 3, planes - 3)

    def copy(p, carry):
        out[p] = w[FINE + p, :ny]
        return carry

    lax.fori_loop(0, nx, copy, 0)

    matrix = halve_lanes(nz, nz // 2)

    def halve(fetch, out):
        def step(q, carry):
            pairs[pl.ds(pl.multiple_of(q * ny, ny), ny), :] = fetch(2 * q) + fetch(2 * q + 1)
            return carry

        lax.fori_loop(0, nx // 2, step, 0)
        halved[...] = dot(pairs[...], matrix)
        out[...] = pair_rows(halved, nx * ny // 4).reshape(out.shape)

    halve(lambda k: residual(w, weights, scaled, diag, FINE + k)[:ny], b1)
    halve(lambda k: coef[k], c1)

    n1 = nx // 2
    r1 = ny // 2
    up[:SOURCE] = b1[n1 - SOURCE:]
    down[:SOURCE] = b1[:SOURCE]
    up[SOURCE:SOURCE + COARSE] = c1[n1 - COARSE:]
    down[SOURCE:SOURCE + COARSE] = c1[:COARSE]
    at = SOURCE + COARSE
    for k in range(POST):
        for i in range(2):
            for j in range(2):
                rows, lanes = pl.ds(i * r1, r1), pl.ds(j * (nz // 2), nz // 2)
                up[at] = w[FINE + nx - POST + k, rows, lanes]
                down[at] = w[FINE + k, rows, lanes]
                at += 1


def rows_kernel(b1, c1, v, low, high, up, down):
    n1, r1, half = b1.shape
    nx, ny = 2 * n1, 2 * r1

    def edge(take, at):
        up[at] = take(r1 - COARSE, COARSE)
        down[at] = take(0, COARSE)

    at = 0
    for k in range(SOURCE):
        edge(lambda s, n: low[k, pl.ds(s, n), :], at)
        edge(lambda s, n: high[k, pl.ds(s, n), :], at + SOURCE + n1)
        at += 1
    for k in range(n1):
        edge(lambda s, n: b1[k, pl.ds(s, n), :], at)
        at += 1
    at += SOURCE
    for k in range(COARSE):
        edge(lambda s, n: low[SOURCE + k, pl.ds(s, n), :], at)
        edge(lambda s, n: high[SOURCE + k, pl.ds(s, n), :], at + COARSE + n1)
        at += 1
    for k in range(n1):
        edge(lambda s, n: c1[k, pl.ds(s, n), :], at)
        at += 1
    at += COARSE
    base = SOURCE + COARSE
    for k in range(POST):
        for j in range(2):
            rows = pl.ds(j * FINE, FINE)
            up[at, rows, :] = low[base + 4 * k + 2 + j, r1 - FINE:, :]
            down[at, rows, :] = low[base + 4 * k + j, :FINE, :]
            up[at + POST + nx, rows, :] = high[base + 4 * k + 2 + j, r1 - FINE:, :]
            down[at + POST + nx, rows, :] = high[base + 4 * k + j, :FINE, :]
        at += 1

    def own(k, carry):
        for j in range(2):
            rows, lanes = pl.ds(j * FINE, FINE), pl.ds(j * half, half)
            up[at + k, rows, :] = v[k, ny - FINE:, lanes]
            down[at + k, rows, :] = v[k, :FINE, lanes]
        return carry

    lax.fori_loop(0, nx, own, 0)


def coarse_pre_kernel(b1, c1, low, high, left, right,
                      v, weights, scaled, send, c, w, diag, halved, c2):
    n1, r1, lanes = b1.shape
    planes = n1 + 2 * COARSE
    scale = 0.25

    def fill(target, own, base, offset, width):
        at = COARSE - width

        def rest(k, carry):
            target[at + k, r1:] = jnp.concatenate((right[offset + k], left[offset + k]), 0)
            return carry

        lax.fori_loop(0, n1 + 2 * width, rest, 0)
        for k in range(n1):
            target[COARSE + k, :r1] = own[k]
        for k in range(width):
            target[at + k, :r1] = low[base + k]
            target[COARSE + n1 + k, :r1] = high[base + k]

    fill(scaled, b1, 0, 0, SOURCE)
    fill(c, c1, SOURCE, n1 + 2 * SOURCE, COARSE)
    weigh(c, weights, scaled, diag, lambda p: scaled[p], 1, planes - 1, lanes, False, scale, RELAX_WEIGHT)
    sweep(scaled, w, weights, scaled, 2, planes - 2)
    sweep(w, v, weights, scaled, 3, planes - 3)

    n2, r2 = n1 // 2, r1 // 2
    matrix = jnp.concatenate((halve_lanes(lanes, LANES), halve_lanes(lanes, LANES, lanes // 2)), 0)

    def halve(fetch):
        wide = jnp.concatenate(
            [
                jnp.concatenate(
                    [fetch(2 * (q + g * (n2 // 2))) + fetch(2 * (q + g * (n2 // 2)) + 1) for g in range(2)], 1
                )
                for q in range(n2 // 2)
            ],
            0,
        )
        halved[...] = dot(wide, matrix)
        return pair_rows(halved, n2 // 2 * r2).reshape(n2 // 2, r2, LANES)

    c2[...] = halve(lambda k: c1[k])
    b2 = halve(lambda k: residual(v, weights, scaled, diag, COARSE + k)[:r1])
    half = n2 // 2
    for d in range(send.shape[0]):
        send[d, :half] = b2
        send[d, half:] = c2[...]


def pads(ref, depth, count):
    lanes = ref.shape[2]
    lane = iota((1, lanes), 1)
    ref[0] = jnp.where(lane < depth, 0.0, roll(ref[count], depth, 1))
    ref[count + 1] = jnp.where(lane >= lanes - depth, 0.0, roll(ref[1], -depth, 1))


def regroup(depth):
    source, target = iota((2 * LANES, LANES), 0), iota((2 * LANES, LANES), 1)
    group, lane = source // LANES, source % LANES
    block, z = lane // depth, lane % depth
    return (2 * block + group) * (depth // 2) + z // 2 == target


def solve_kernel(place_ref, gathered, v1, w1, s1, v0, w0, s0, low, high, left, right, out,
                 c2, a2, y2, g2, s2, d2, c3, a3, y3, g3, s3, d3, c4, b4, y4, g4, s4,
                 wide2, thin2, wide3, thin3, spread, u1, t1, u0, t0, *, gx, gy):
    half = gathered.shape[1] // 2
    r2 = gathered.shape[2]
    n2, m2 = 2 * half, s2.shape[0] - 2
    rows2 = s2.shape[1]
    depth2 = LANES // 2
    lane = iota((1, LANES), 1)

    def unpack(i, carry):
        for j in range(gy):
            for k in range(half):
                for which, target in enumerate((s2, c2)):
                    one = gathered[i * gy + j, which * half + k]
                    two = gathered[(i + gx // 2) * gy + j, which * half + k]
                    rows = pl.ds(j * r2, r2)
                    target[1 + i * n2 + k, rows, :] = jnp.where(lane < depth2, one, roll(two, depth2, 1))
                    target[1 + i * n2 + half + k, rows, :] = jnp.where(lane < depth2, roll(one, depth2, 1), two)
        return carry

    lax.fori_loop(0, gx // 2, unpack, 0)

    def level_in(c, source, weights, scaled, diag, depth, scale, omega):
        count = c.shape[0] - 2
        pads(c, depth, count)
        weigh(c, weights, scaled, diag, source, 1, count + 1, depth, True, scale, omega)

    def smooth(first, other, weights, scaled, depth, count, sweeps):
        for _ in range(sweeps):
            pads(first, depth, count)
            sweep(first, other, weights, scaled, 1, count + 1)
            first, other = other, first
        return first, other

    def down(fetch, wide, thin, depth, out, count, scale=1.0):
        rows = wide.shape[0] // (count // 4)
        for m in range(count // 4):
            for g in range(2):
                at = g * (count // 2) + 2 * m + 1
                wide[m * rows:(m + 1) * rows, g * LANES:(g + 1) * LANES] = fetch(at) + fetch(at + 1)
        thin[...] = dot(wide[...], jnp.where(regroup(depth), 0.125, 0.0).astype(F32))
        total = pair_rows(thin, thin.shape[0] // 2)
        out[1:1 + count // 4] = total.reshape(count // 4, rows // 2, LANES)

    def up(coarse, wide, thin, depth, fine, count):
        rows = wide.shape[0] // (count // 4)
        matrix = jnp.where(regroup(depth), 1.0, 0.0).astype(F32)
        for g in range(2):
            part = matrix[g * LANES:(g + 1) * LANES]
            x = coarse[1:1 + count // 4].reshape(thin.shape[0] // 2, LANES)
            x = lax.dot_general(x, part, (((1,), (1,)), ((), ())), precision=lax.Precision.HIGHEST,
                                preferred_element_type=F32)
            thin[pl.ds(0, thin.shape[0] // 2, stride=2), :] = x
            thin[pl.ds(1, thin.shape[0] // 2, stride=2), :] = x
            for m in range(count // 4):
                value = thin[m * rows:(m + 1) * rows, :]
                for k in range(2):
                    at = g * (count // 2) + 2 * m + 1 + k
                    fine[at] = fine[at] + value

    m3, m4 = c3.shape[0] - 2, c4.shape[0] - 2
    level_in(c2, lambda p: s2[p], g2, s2, d2, depth2, 0.25**2, RELAX_WEIGHT)
    for p in range(1, m2 + 1):
        a2[p] = s2[p]
    x2, z2 = smooth(a2, y2, g2, s2, depth2, m2, SWEEPS - 1)
    pads(x2, depth2, m2)
    down(lambda p: residual(x2, g2, s2, d2, p), wide2, thin2, depth2, s3, m2)
    down(lambda p: c2[p], wide2, thin2, depth2, c3, m2)

    depth3, depth4 = depth2 // 2, depth2 // 4
    level_in(c3, lambda p: s3[p], g3, s3, d3, depth3, 0.25**3, RELAX_WEIGHT)
    for p in range(1, m3 + 1):
        a3[p] = s3[p]
    x3, z3 = smooth(a3, y3, g3, s3, depth3, m3, SWEEPS - 1)
    pads(x3, depth3, m3)
    down(lambda p: residual(x3, g3, s3, d3, p), wide3, thin3, depth3, s4, m3)
    down(lambda p: c3[p], wide3, thin3, depth3, c4, m3)

    level_in(c4, lambda p: s4[p], g4, s4, None, depth4, 0.25**4, 1.0)
    theta, delta = (CHEBY_UPPER + CHEBY_LOWER) / 2.0, (CHEBY_UPPER - CHEBY_LOWER) / 2.0
    sigma = theta / delta
    rho = 1.0 / sigma
    res = [s4[p] for p in range(1, m4 + 1)]
    direction = [r / theta for r in res]
    total = [jnp.zeros_like(r) for r in res]
    for _ in range(CHEB):
        for p in range(m4):
            total[p] = total[p] + direction[p]
            y4[1 + p] = direction[p]
        pads(y4, depth4, m4)
        for p in range(m4):
            _, near = neighbours(y4, g4, 1 + p)
            res[p] = res[p] - (direction[p] - near)
        rho_new = 1.0 / (2.0 * sigma - rho)
        direction = [rho_new * rho * d + (2.0 * rho_new / delta) * r for d, r in zip(direction, res)]
        rho = rho_new
    for p in range(m4):
        b4[1 + p] = total[p]

    up(b4, wide3, thin3, depth3, x3, m3)
    x3, z3 = smooth(x3, z3, g3, s3, depth3, m3, SWEEPS)
    up(x3, wide2, thin2, depth2, x2, m2)
    x2, z2 = smooth(x2, z2, g2, s2, depth2, m2, SWEEPS)

    at_x, at_y = place_ref[0], place_ref[1]
    planes1, rows1, lanes1 = v1.shape
    n1 = planes1 - 2 * COARSE
    r1 = rows1 - 2 * COARSE
    y = iota((rows1, rows2), 0)
    y = jnp.where(y < r1 + COARSE, y, y - rows1) + r1 * at_y
    pick = jnp.where((y >= 0) & (y // 2 == iota((rows1, rows2), 1)), 1.0, 0.0).astype(F32)
    for h in range(2):
        source, target = iota((LANES, lanes1), 0), iota((LANES, lanes1), 1)
        spread[h] = jnp.where(source == h * depth2 + target // 2, 1.0, 0.0).astype(F32)

    reach = SWEEPS + 2
    for t in range(-((reach + 1) // 2), (n1 + reach + 1) // 2):
        x = at_x * n2 + t
        inside = jnp.where((x >= 0) & (x < gx * n2), 1.0, 0.0).astype(F32)
        x = jnp.clip(x, 0, gx * n2 - 1)
        block = x // m2
        plane = x2[1 + x - block * m2]
        value = dot(dot(pick, plane), spread[block]) * inside
        for k in range(2):
            p = COARSE + 2 * t + k
            u1[p] = v1[p] + value
    sweep(u1, t1, w1, s1, COARSE - 4, COARSE + n1 + 4)
    sweep(t1, u1, w1, s1, COARSE - 3, COARSE + n1 + 3)
    sweep(u1, t1, w1, s1, COARSE - 2, COARSE + n1 + 2)

    nx, ny, nz = v0.shape
    rows0 = u0.shape[1]

    def own(k, carry):
        u0[FINE + k, :ny] = v0[k]
        return carry

    lax.fori_loop(0, nx, own, 0)
    base = SOURCE + COARSE
    for k in range(POST):
        for i in range(2):
            for j in range(2):
                rows, lanes = pl.ds(i * r1, r1), pl.ds(j * lanes1, lanes1)
                u0[FINE - POST + k, rows, lanes] = low[base + 4 * k + 2 * i + j]
                u0[FINE + nx + k, rows, lanes] = high[base + 4 * k + 2 * i + j]
    base = 2 * n1 + 2 * SOURCE + 2 * COARSE

    def sides(k, carry):
        for j in range(2):
            rows, lanes = pl.ds(j * FINE, FINE), pl.ds(j * lanes1, lanes1)
            u0[FINE - POST + k, ny:, lanes] = jnp.concatenate((right[base + k, rows, :], left[base + k, rows, :]), 0)
        return carry

    lax.fori_loop(0, nx + 2 * POST, sides, 0)

    y = iota((rows0, rows1), 0)
    y = jnp.where(y < ny + FINE, y, y - rows0)
    y = jnp.where(y >= 0, y // 2, rows1 - (1 - y) // 2)
    pick = jnp.where(y == iota((rows0, rows1), 1), 1.0, 0.0).astype(F32)
    source, target = iota((lanes1, nz), 0), iota((lanes1, nz), 1)
    widen = jnp.where(source == target // 2, 1.0, 0.0).astype(F32)

    def add(t, carry):
        value = dot(dot(pick, t1[COARSE - 2 + t]), widen)
        for k in range(2):
            p = FINE - 4 + 2 * t + k
            u0[p] = u0[p] + value
        return carry

    lax.fori_loop(0, n1 + 4, add, 0)
    sweep(u0, t0, w0, s0, FINE - 2, FINE + nx + 2)
    sweep(t0, u0, w0, s0, FINE - 1, FINE + nx + 1)

    def last(p, carry):
        v, total = neighbours(u0, w0, p)
        out[p - FINE] = ((1.0 - RELAX_WEIGHT) * v + (s0[p] + total))[:ny]
        return carry

    lax.fori_loop(FINE, FINE + nx, last, 0)


def call(kernel, outs, scratch, *args, scalars=0):
    specs = [pl.BlockSpec(memory_space=pltpu.SMEM if k < scalars else pltpu.VMEM) for k in range(len(args))]
    return pl.pallas_call(
        kernel,
        out_shape=outs,
        in_specs=specs,
        out_specs=[pl.BlockSpec(memory_space=pltpu.VMEM) for _ in outs],
        scratch_shapes=scratch,
        compiler_params=pltpu.CompilerParams(vmem_limit_bytes=VMEM_LIMIT),
    )(*args)


def shape(*dims):
    return jax.ShapeDtypeStruct(dims, F32)


def exchange(up, down, axis):
    count = lax.axis_size(axis)
    forward = [(i, i + 1) for i in range(count - 1)]
    backward = [(target, source) for source, target in forward]
    return lax.ppermute(up, axis, forward), lax.ppermute(down, axis, backward)


def body(guess, right_side, coefficient):
    gx, gy = lax.axis_size("gx"), lax.axis_size("gy")
    nx, ny, nz = guess.shape
    fields = ((guess, FINE), (right_side, FINE - 1), (coefficient, FINE))
    low, high = exchange(
        jnp.concatenate([f[nx - k:] for f, k in fields], 0), jnp.concatenate([f[:k] for f, k in fields], 0), "gx"
    )

    def rows(cut):
        parts, at = [], 0
        for f, k in fields:
            parts += [cut(low[at:at + k]), cut(f), cut(high[at:at + k])]
            at += k
        return jnp.concatenate(parts, 0)

    left, right = exchange(rows(lambda f: f[:, ny - FINE:]), rows(lambda f: f[:, :FINE]), "gy")

    planes0, rows0 = nx + 2 * FINE, ny + 2 * FINE
    block0 = (planes0, rows0, nz)
    n1, r1, z1 = nx // 2, ny // 2, nz // 2
    message = (SOURCE + COARSE + 4 * POST, r1, z1)
    v0, w0, s0, up, down, b1, c1 = call(
        fine_pre_kernel,
        (shape(nx, ny, nz), shape(6, *block0), shape(*block0), shape(*message), shape(*message),
         shape(n1, r1, z1), shape(n1, r1, z1)),
        (vmem(*block0), vmem(*block0), vmem(*block0), vmem(*block0), vmem(n1 * ny, nz), vmem(n1 * ny, z1)),
        guess, right_side, coefficient, low, high, left, right,
    )
    low, high = exchange(up, down, "gx")
    count = 3 * n1 + 2 * SOURCE + 2 * COARSE + 2 * POST + n1
    up, down = call(rows_kernel, (shape(count, COARSE, z1),) * 2, (), b1, c1, v0, low, high)
    left, right = exchange(up, down, "gy")

    block1 = (n1 + 2 * COARSE, r1 + 2 * COARSE, z1)
    n2, r2 = n1 // 2, r1 // 2
    chunk = (n2, r2, LANES)
    v1, w1, s1, send = call(
        coarse_pre_kernel,
        (shape(*block1), shape(6, *block1), shape(*block1), shape(gx * gy, *chunk)),
        (vmem(*block1), vmem(*block1), vmem(*block1), vmem(n2 // 2 * r1, LANES), vmem(n2 // 2, r2, LANES)),
        b1, c1, low, high, left, right,
    )
    gathered = lax.all_to_all(send, ("gx", "gy"), 0, 0)
    place_at = jnp.stack((lax.axis_index("gx"), lax.axis_index("gy"))).astype(jnp.int32)

    m2, rows2 = gx * n2 // 2, gy * r2
    m3, rows3 = m2 // 4, rows2 // 2
    m4, rows4 = m3 // 4, rows3 // 2
    level2, level3, level4 = (m2 + 2, rows2, LANES), (m3 + 2, rows3, LANES), (m4 + 2, rows4, LANES)
    scratch = [
        vmem(*level2), vmem(*level2), vmem(*level2), vmem(6, *level2), vmem(*level2), vmem(*level2),
        vmem(*level3), vmem(*level3), vmem(*level3), vmem(6, *level3), vmem(*level3), vmem(*level3),
        vmem(*level4), vmem(*level4), vmem(*level4), vmem(6, *level4), vmem(*level4),
        vmem(m3 * rows2, 2 * LANES), vmem(m3 * rows2, LANES),
        vmem(m4 * rows3, 2 * LANES), vmem(m4 * rows3, LANES),
        vmem(2, LANES, z1), vmem(*block1), vmem(*block1), vmem(*block0), vmem(*block0),
    ]
    (out,) = call(
        partial(solve_kernel, gx=gx, gy=gy), (shape(nx, ny, nz),), scratch,
        place_at, gathered, v1, w1, s1, v0, w0, s0, low, high, left, right, scalars=1,
    )
    return out


def solution(mesh):
    return jax.shard_map(
        body,
        mesh=mesh,
        in_specs=(P("gx", "gy", None), P("gx", "gy", None), P("gx", "gy", None)),
        out_specs=P("gx", "gy", None),
        check_vma=False,
    )
```

```python
from functools import partial

import jax
import jax.numpy as jnp
from jax import lax
from jax.experimental import pallas as pl
from jax.experimental.pallas import tpu as pltpu
from jax.sharding import PartitionSpec as P

LEVELS = 4
SWEEPS = 3
CHEB = 8

RELAX_WEIGHT = 0.7
CHEBY_LOWER = 0.08
CHEBY_UPPER = 2.0

F32 = jnp.float32
LANES = 128
FINE = SWEEPS + 1
COARSE = 8
SOURCE = COARSE - 1
POST = SWEEPS
BLOCK = 24
VMEM_LIMIT = 56 * 1024 * 1024


def dot(a, b):
    return jnp.dot(a, b, precision=lax.Precision.HIGHEST, preferred_element_type=F32)


def iota(shape, dim):
    return lax.broadcasted_iota(jnp.int32, shape, dim)


def vmem(*shape):
    return pltpu.VMEM(shape, F32)


def roll(x, by, axis):
    return pltpu.roll(x, by % x.shape[axis], axis)


def planes(first, last, step):
    if last - first <= BLOCK:
        for p in range(first, last):
            step(p)
    else:
        lax.fori_loop(first, last, lambda p, carry: (step(p), carry)[1], 0, unroll=4)


def lane_before(x, t, lane):
    moved = roll(x[t], 1, 1)
    return moved if len(x) == 1 else jnp.where(lane == 0, roll(x[t - 1], 1, 1), moved)


def lane_after(x, t, lane):
    moved = roll(x[t], -1, 1)
    return moved if len(x) == 1 else jnp.where(lane == LANES - 1, roll(x[(t + 1) % len(x)], -1, 1), moved)


def weigh(fetch, source, level, first, last, depth, row_edges, scale, omega):
    wx, wy, wz, gain, scaled, total = level
    count, pieces = wy.shape[1:3]
    lane = iota((8, LANES), 1)
    front, back = lane % depth == 0, lane % depth == depth - 1
    top, bottom = iota((8, LANES), 0) == 0, iota((8, LANES), 0) == 7

    def step(p):
        for j in range(count):
            c = [fetch(p, j, t) for t in range(pieces)]
            for t in range(pieces):
                x = c[t]
                lower, upper = fetch(p - 1, j, t), fetch(p + 1, j, t)
                left = fetch(p, j - 1, t) if j else roll(fetch(p, count - 1, t), 1, 0)
                right = fetch(p, j + 1, t) if j < count - 1 else roll(fetch(p, 0, t), -1, 0)
                if row_edges and j == 0:
                    left = jnp.where(top, 0.0, left)
                if row_edges and j == count - 1:
                    right = jnp.where(bottom, 0.0, right)
                near, far = lane_before(c, t, lane), lane_after(c, t, lane)
                if t == 0:
                    near = jnp.where(front, 0.0, near)
                if t == pieces - 1:
                    far = jnp.where(back, 0.0, far)
                below, beside, before = x + lower, x + left, x + near
                s = (below + beside + before) + (3.0 * x + (upper + right + far))
                wx[p, j, t] = below
                if last is not None:
                    wx[p + 1, j, t] = x + upper
                wy[p, j, t] = jnp.where(top, 0.0, beside) if row_edges and j == 0 else beside
                wz[p, j, t] = jnp.where(front, 0.0, before) if t == 0 else before
                gain[p, j, t] = jnp.where(x > 0.0, omega / s, 0.0)
                scaled[p, j, t] = source(p, j, t) * (2.0 / scale)
                if total is not None:
                    total[p, j, t] = s

    planes(first, last, step)


def around(fetch, level, p, finish):
    wx, wy, wz = level[:3]
    count, pieces = wy.shape[1:3]
    lane = iota((8, LANES), 1)
    v = [[fetch(p, j, t) for t in range(pieces)] for j in range(count)]
    beside = [wy[p, 0, t] for t in range(pieces)]
    wrap = [roll(beside[t] * v[0][t], -1, 0) for t in range(pieces)]
    for j in range(count):
        ahead = [wy[p, j + 1, t] for t in range(pieces)] if j < count - 1 else None
        before = [wz[p, j, t] for t in range(pieces)]
        flow = [before[t] * v[j][t] for t in range(pieces)]
        for t in range(pieces):
            total = wx[p, j, t] * fetch(p - 1, j, t) + wx[p + 1, j, t] * fetch(p + 1, j, t)
            total += beside[t] * (v[j - 1][t] if j else roll(v[count - 1][t], 1, 0))
            total += ahead[t] * v[j + 1][t] if j < count - 1 else wrap[t]
            total += before[t] * lane_before(v[j], t, lane) + lane_after(flow, t, lane)
            finish(j, t, v[j][t], total)
        beside = ahead


def reader(ref):
    return lambda p, j, t: ref[p, j, t]


def sweep(fetch, out, level, first, last):
    gain, scaled = level[3:5]

    def step(p):
        def finish(j, t, v, total):
            out[p, j, t] = (1.0 - RELAX_WEIGHT) * v + gain[p, j, t] * (scaled[p, j, t] + total)

        around(fetch, level, p, finish)

    planes(first, last, step)


def start(out, level, first, last):
    gain, scaled = level[3:5]

    def step(p):
        for j in range(out.shape[1]):
            for t in range(out.shape[2]):
                out[p, j, t] = gain[p, j, t] * scaled[p, j, t]

    planes(first, last, step)


def residual(fetch, level, p):
    scaled, total = level[4:6]
    found = {}

    def finish(j, t, v, near):
        found[j, t] = (scaled[p, j, t] + near) - v * total[p, j, t]

    around(fetch, level, p, finish)
    return found


def halve_lanes(lanes, width, value, offset=0):
    return jnp.where(iota((lanes, width), 0) // 2 + offset == iota((lanes, width), 1), value, 0.0).astype(F32)


def even_odd(ref, count):
    return ref[pl.ds(0, count, stride=2), :] + ref[pl.ds(1, count, stride=2), :]


def fine_pre_kernel(guess, source, coef, low, high, left, right,
                    out, wx, wy, wz, gain, scaled, up, down, b1, c1,
                    field, force, c, v, w, total, *pairs):
    nx, ny, nz = guess.shape
    pieces = nz // LANES
    rows = ny + 2 * FINE
    count = rows // 8
    planes0 = nx + 2 * FINE
    level = (wx, wy, wz, gain, scaled, total)

    def fill(target, own, base, width):
        at = FINE - width
        offset = sum(nx + 2 * k for k in base)
        message = sum(base)

        def rest(k):
            side = jnp.concatenate((right[offset + k], left[offset + k]), 0)
            for t in range(pieces):
                target[at + k, t, ny:] = side[:, t * LANES:(t + 1) * LANES]

        planes(0, nx + 2 * width, rest)

        def main(k):
            for t in range(pieces):
                target[FINE + k, t, :ny] = own[k, :, t * LANES:(t + 1) * LANES]

        planes(0, nx, main)
        for k in range(width):
            for t in range(pieces):
                lanes = slice(t * LANES, (t + 1) * LANES)
                target[at + k, t, :ny] = low[message + k, :, lanes]
                target[FINE + nx + k, t, :ny] = high[message + k, :, lanes]

    def spaced(ref):
        return lambda p, j, t: ref[p, t, pl.ds(j, 8, stride=count), :]

    fill(field, guess, (), FINE)
    fill(force, source, (FINE,), FINE - 1)
    fill(c, coef, (FINE, FINE - 1), FINE)
    def arrange(p):
        for j in range(count):
            for t in range(pieces):
                w[p, j, t] = spaced(c)(p, j, t)

    planes(0, planes0, arrange)
    weigh(reader(w), spaced(force), level, 1, planes0 - 1, LANES, False, 1.0, RELAX_WEIGHT)

    def arrange_field(p):
        for j in range(count):
            for t in range(pieces):
                v[p, j, t] = spaced(field)(p, j, t)

    planes(0, planes0, arrange_field)
    sweep(reader(v), w, level, 1, planes0 - 1)
    sweep(reader(w), v, level, 2, planes0 - 2)
    sweep(reader(v), w, level, 3, planes0 - 3)

    def put(k):
        for t in range(pieces):
            for j in range(count):
                field[k, t, pl.ds(j, 8, stride=count), :] = w[FINE + k, j, t]
            out[k, :, t * LANES:(t + 1) * LANES] = field[k, t, :ny]

    planes(0, nx, put)

    n1, r1 = nx // 2, ny // 2

    def coarsen(value):
        wide = jnp.concatenate(
            [jnp.concatenate([even_odd(pairs[t].at[pl.ds(q * rows, ny)], r1) for t in range(pieces)], 1) for q in range(n1)], 0
        )
        return dot(wide, halve_lanes(nz, nz // 2, value)).reshape(n1, r1, nz // 2)

    def halve(q):
        one, two = (residual(reader(w), level, FINE + 2 * q + k) for k in range(2))
        for j in range(count):
            for t in range(pieces):
                pairs[t][pl.ds(q * rows + j, 8, stride=count), :] = one[j, t] + two[j, t]

    planes(0, n1, halve)
    b1[...] = coarsen(0.125 * 0.5)
    for q in range(n1):
        for t in range(pieces):
            lanes = slice(t * LANES, (t + 1) * LANES)
            pairs[t][q * rows:q * rows + ny, :] = coef[2 * q, :, lanes] + coef[2 * q + 1, :, lanes]
    c1[...] = coarsen(0.125)

    up[:SOURCE] = b1[n1 - SOURCE:]
    down[:SOURCE] = b1[:SOURCE]
    up[SOURCE:SOURCE + COARSE] = c1[n1 - COARSE:]
    down[SOURCE:SOURCE + COARSE] = c1[:COARSE]
    at = SOURCE + COARSE
    for k in range(POST):
        for i in range(2):
            for j in range(2):
                here, lanes = pl.ds(i * r1, r1), pl.ds(j * (nz // 2), nz // 2)
                up[at] = out[nx - POST + k, here, lanes]
                down[at] = out[k, here, lanes]
                at += 1


def rows_kernel(b1, c1, v, low, high, up, down):
    n1, r1, half = b1.shape
    nx, ny = 2 * n1, 2 * r1

    def edge(take, at):
        up[at] = take(r1 - COARSE, COARSE)
        down[at] = take(0, COARSE)

    at = 0
    for k in range(SOURCE):
        edge(lambda s, n: low[k, pl.ds(s, n), :], at)
        edge(lambda s, n: high[k, pl.ds(s, n), :], at + SOURCE + n1)
        at += 1
    for k in range(n1):
        edge(lambda s, n: b1[k, pl.ds(s, n), :], at)
        at += 1
    at += SOURCE
    for k in range(COARSE):
        edge(lambda s, n: low[SOURCE + k, pl.ds(s, n), :], at)
        edge(lambda s, n: high[SOURCE + k, pl.ds(s, n), :], at + COARSE + n1)
        at += 1
    for k in range(n1):
        edge(lambda s, n: c1[k, pl.ds(s, n), :], at)
        at += 1
    at += COARSE
    base = SOURCE + COARSE
    for k in range(POST):
        for j in range(2):
            rows = pl.ds(j * FINE, FINE)
            up[at, rows, :] = low[base + 4 * k + 2 + j, r1 - FINE:, :]
            down[at, rows, :] = low[base + 4 * k + j, :FINE, :]
            up[at + POST + nx, rows, :] = high[base + 4 * k + 2 + j, r1 - FINE:, :]
            down[at + POST + nx, rows, :] = high[base + 4 * k + j, :FINE, :]
        at += 1

    def own(k):
        for j in range(2):
            rows, lanes = pl.ds(j * FINE, FINE), pl.ds(j * half, half)
            up[at + k, rows, :] = v[k, ny - FINE:, lanes]
            down[at + k, rows, :] = v[k, :FINE, lanes]

    planes(0, nx, own)


def coarse_pre_kernel(b1, c1, low, high, left, right,
                      v, wx, wy, wz, gain, scaled, send, field, c, w, total, upper, lower):
    n1, r1, lanes = b1.shape
    rows = r1 + 2 * COARSE
    count = rows // 8
    planes1 = n1 + 2 * COARSE
    scale = 0.25
    level = (wx, wy, wz, gain, scaled, total)

    def fill(target, own, base, offset, width):
        at = COARSE - width
        for k in range(n1 + 2 * width):
            target[at + k, r1:r1 + COARSE] = right[offset + k]
            target[at + k, r1 + COARSE:] = left[offset + k]
        for k in range(n1):
            target[COARSE + k, :r1] = own[k]
        for k in range(width):
            target[at + k, :r1] = low[base + k]
            target[COARSE + n1 + k, :r1] = high[base + k]

    def spaced(ref):
        return lambda p, j, t: ref[p, pl.ds(j, 8, stride=count), :]

    fill(field, b1, 0, 0, SOURCE)
    fill(c, c1, SOURCE, n1 + 2 * SOURCE, COARSE)
    for p in range(planes1):
        for j in range(count):
            w[p, j, 0] = spaced(c)(p, j, 0)
    weigh(reader(w), spaced(field), level, 1, planes1 - 1, lanes, False, scale, RELAX_WEIGHT)
    start(v, level, 1, planes1 - 1)
    sweep(reader(v), w, level, 2, planes1 - 2)
    sweep(reader(w), v, level, 3, planes1 - 3)

    n2, r2 = n1 // 2, r1 // 2
    half = n2 // 2

    def coarsen(value):
        matrix = jnp.concatenate((halve_lanes(lanes, LANES, value), halve_lanes(lanes, LANES, value, lanes // 2)), 0)
        return dot(jnp.concatenate((lower[...], upper[...]), 1), matrix).reshape(half, r2, LANES)

    for q in range(n2):
        one, two = (residual(reader(v), level, COARSE + 2 * q + k) for k in range(2))
        target = lower if q < half else upper
        for j in range(count // 2):
            value = (one[2 * j, 0] + two[2 * j, 0]) + (one[2 * j + 1, 0] + two[2 * j + 1, 0])
            target[pl.ds(q % half * r2 + j, r1 // count, stride=count // 2), :] = value[:r1 // count]
    b2 = coarsen(0.125 * 0.5 * scale)
    for q in range(n2):
        target = lower if q < half else upper
        field[q, :r1] = c1[2 * q] + c1[2 * q + 1]
        target[q % half * r2:(q % half + 1) * r2, :] = even_odd(field.at[q], r2)
    c2 = coarsen(0.125)
    for d in range(send.shape[0]):
        send[d, :half] = b2
        send[d, half:] = c2


def pads(ref, depth):
    last = ref.shape[0] - 1
    for j in range(ref.shape[1]):
        ref[0, j, 0] = roll(ref[last - 1, j, 0], depth, 1)
        ref[last, j, 0] = roll(ref[1, j, 0], -depth, 1)


def regroup(depth):
    source, target = iota((2 * LANES, LANES), 0), iota((2 * LANES, LANES), 1)
    group, lane = source // LANES, source % LANES
    block, z = lane // depth, lane % depth
    return (2 * block + group) * (depth // 2) + z // 2 == target


def solve_kernel(place_ref, gathered, v1, wx1, wy1, wz1, gain1, scaled1, v0, wx0, wy0, wz0, gain0, scaled0,
                 low, high, left, right, out,
                 c2, a2, y2, n2, l2x, l2y, l2z, l2g, l2s, l2t,
                 c3, b3, a3, y3, l3x, l3y, l3z, l3g, l3s, l3t,
                 c4, b4, y4, l4x, l4y, l4z, l4g, l4s,
                 u1, t1, e1, field, u0, t0, double, *, gx, gy):
    level2 = (l2x, l2y, l2z, l2g, l2s, l2t)
    level3 = (l3x, l3y, l3z, l3g, l3s, l3t)
    level4 = (l4x, l4y, l4z, l4g, l4s, None)
    half = gathered.shape[1] // 2
    r2 = gathered.shape[2]
    per = 2 * half
    m2, m3, m4 = c2.shape[0] - 2, c3.shape[0] - 2, c4.shape[0] - 2
    j2, j3, j4 = c2.shape[1], c3.shape[1], c4.shape[1]
    rows2 = 8 * j2
    depth2 = LANES // 2
    depth3, depth4 = depth2 // 2, depth2 // 4
    lane = iota((8, LANES), 1)

    def unpack(i):
        for j in range(gy):
            for k in range(half):
                for which in range(2):
                    one = gathered[i * gy + j, which * half + k]
                    two = gathered[(i + gx // 2) * gy + j, which * half + k]
                    here = pl.ds(j * r2, r2)
                    n2[which, i * per + k, here, :] = jnp.where(lane < depth2, one, roll(two, depth2, 1))
                    n2[which, i * per + half + k, here, :] = jnp.where(lane < depth2, roll(one, depth2, 1), two)

    planes(0, gx // 2, unpack)

    def spread(p):
        for j in range(j2):
            c2[1 + p, j, 0] = n2[1, p, pl.ds(j, 8, stride=j2), :]

    planes(0, m2, spread)

    def level_in(c, source, level, depth, scale, omega):
        last = c.shape[0] - 1
        lane = iota((8, LANES), 1)
        for j in range(c.shape[1]):
            c[0, j, 0] = jnp.where(lane < depth, 0.0, roll(c[last - 1, j, 0], depth, 1))
            c[last, j, 0] = jnp.where(lane >= LANES - depth, 0.0, roll(c[1, j, 0], -depth, 1))
        weigh(reader(c), source, level, 1, last, depth, True, scale, omega)
        wx = level[0]
        for j in range(c.shape[1]):
            wx[1, j, 0] = jnp.where(lane < depth, 0.0, wx[1, j, 0])
            wx[last, j, 0] = jnp.where(lane >= LANES - depth, 0.0, wx[last, j, 0])

    def smooth(first, other, level, depth, sweeps):
        for _ in range(sweeps):
            pads(first, depth)
            sweep(reader(first), other, level, 1, first.shape[0] - 1)
            first, other = other, first
        return first, other

    def down(fetch, count, rows, depth, out, value):
        def pair(m, g):
            at = g * (count // 2) + 2 * m + 1
            one, two = fetch(at), fetch(at + 1)
            return [(one[2 * j] + two[2 * j]) + (one[2 * j + 1] + two[2 * j + 1]) for j in range(rows // 2)]

        parts = [jnp.concatenate(both, 1) for m in range(count // 4) for both in zip(pair(m, 0), pair(m, 1))]
        matrix = jnp.where(regroup(depth), value, 0.0).astype(F32)
        found = dot(jnp.concatenate(parts, 0), matrix)
        at = 0
        for m in range(count // 4):
            for j in range(rows // 2):
                out[1 + m, j, 0] = found[at:at + 8]
                at += 8

    def up(coarse, fine, depth):
        count, rows = fine.shape[0] - 2, fine.shape[1]
        matrix = jnp.where(regroup(depth), 1.0, 0.0).astype(F32)
        x = jnp.concatenate([coarse[1 + m, j, 0] for m in range(count // 4) for j in range(rows // 2)], 0)
        x = lax.dot_general(x, matrix, (((1,), (1,)), ((), ())), precision=lax.Precision.HIGHEST,
                            preferred_element_type=F32)
        at = 0
        for m in range(count // 4):
            for j in range(rows // 2):
                for g in range(2):
                    value = x[at:at + 8, g * LANES:(g + 1) * LANES]
                    for k in range(2):
                        p = g * (count // 2) + 2 * m + 1 + k
                        for i in range(2):
                            fine[p, 2 * j + i, 0] = fine[p, 2 * j + i, 0] + value
                at += 8

    def rest(field, level):
        return lambda p: [value for _, value in sorted(residual(reader(field), level, p).items())]

    def whole(ref):
        return lambda p: [ref[p, j, 0] for j in range(ref.shape[1])]

    level_in(c2, lambda p, j, t: n2[0, p - 1, pl.ds(j, 8, stride=j2), :], level2, depth2, 0.25**2, RELAX_WEIGHT)
    start(a2, level2, 1, m2 + 1)
    x2, z2 = smooth(a2, y2, level2, depth2, SWEEPS - 1)
    pads(x2, depth2)
    down(whole(c2), m2, j2, depth2, c3, 0.125)
    down(rest(x2, level2), m2, j2, depth2, b3, 0.125 * 0.5 * 0.25**2)

    level_in(c3, reader(b3), level3, depth3, 0.25**3, RELAX_WEIGHT)
    start(a3, level3, 1, m3 + 1)
    x3, z3 = smooth(a3, y3, level3, depth3, SWEEPS - 1)
    pads(x3, depth3)
    down(whole(c3), m3, j3, depth3, c4, 0.125)
    down(rest(x3, level3), m3, j3, depth3, b4, 0.125 * 0.5 * 0.25**3)

    level_in(c4, reader(b4), level4, depth4, 0.25**4, 1.0)
    theta, delta = (CHEBY_UPPER + CHEBY_LOWER) / 2.0, (CHEBY_UPPER - CHEBY_LOWER) / 2.0
    sigma = theta / delta
    rho = 1.0 / sigma
    cells = [(1 + p, j) for p in range(m4) for j in range(j4)]
    res = {at: l4g[at[0], at[1], 0] * l4s[at[0], at[1], 0] for at in cells}
    direction = {at: res[at] / theta for at in cells}
    total = {at: jnp.zeros((8, LANES), F32) for at in cells}
    for _ in range(CHEB):
        for p, j in cells:
            total[p, j] = total[p, j] + direction[p, j]
            y4[p, j, 0] = direction[p, j]
        pads(y4, depth4)
        for p in range(1, m4 + 1):
            def finish(j, t, v, near):
                res[p, j] = res[p, j] - (v - l4g[p, j, 0] * near)

            around(reader(y4), level4, p, finish)
        rho_new = 1.0 / (2.0 * sigma - rho)
        direction = {at: rho_new * rho * direction[at] + (2.0 * rho_new / delta) * res[at] for at in cells}
        rho = rho_new
    for p, j in cells:
        b4[p, j, 0] = total[p, j]

    up(b4, x3, depth3)
    x3, z3 = smooth(x3, z3, level3, depth3, SWEEPS)
    up(x3, x2, depth2)
    x2, z2 = smooth(x2, z2, level2, depth2, SWEEPS)

    level1 = (wx1, wy1, wz1, gain1, scaled1, None)
    at_x, at_y = place_ref[0], place_ref[1]
    planes1, count1, _, _, lanes1 = v1.shape
    n1, r1 = planes1 - 2 * COARSE, 8 * count1 - 2 * COARSE
    sub = iota((8, LANES), 0)
    reach = SWEEPS + 2
    first, last = -((reach + 1) // 2), (n1 + reach + 1) // 2
    pad = rows2 + 8
    e1[0, :8] = jnp.zeros((8, LANES), F32)
    e1[0, pad:] = jnp.zeros((8, LANES), F32)
    window = []
    for t in range(first, last):
        x = at_x * per + t
        inside = (x >= 0) & (x < gx * per)
        x = jnp.clip(x, 0, gx * per - 1)
        block = x // m2
        slot = t - first
        for j in range(j2):
            value = x2[1 + x - block * m2, j, 0]
            value = jnp.where(block == 0, value, roll(value, depth2, 1))
            e1[0, pl.ds(8 + j, 8, stride=j2), :] = jnp.where(inside, value, 0.0)
        base = pl.multiple_of(at_y * r2, 8)
        above, here, after = (e1[0, pl.ds(base + 8 * k, 8), :] for k in range(3))
        t1[slot, 0, 0] = here
        t1[slot, 1, 0] = jnp.where(sub < 4, after, above)
    wide = jnp.concatenate([t1[slot, k, 0] for slot in range(last - first) for k in range(2)], 0)
    matrix = jnp.where(iota((LANES, lanes1), 0) == iota((LANES, lanes1), 1) // 2, 1.0, 0.0).astype(F32)
    double[0, :wide.shape[0]] = dot(wide, matrix)
    for t in range(first, last):
        part = [double[0, pl.ds(16 * (t - first) + j, 8, stride=2), :] for j in range(2)]
        for k in range(2):
            p = COARSE + 2 * t + k
            for j in range(count1):
                u1[p, j, 0] = v1[p, j, 0] + part[j // 2]
    sweep(reader(u1), t1, level1, COARSE - 4, COARSE + n1 + 4)
    sweep(reader(t1), u1, level1, COARSE - 3, COARSE + n1 + 3)
    sweep(reader(u1), t1, level1, COARSE - 2, COARSE + n1 + 2)

    level0 = (wx0, wy0, wz0, gain0, scaled0, None)
    nx, ny, nz = v0.shape
    pieces = nz // LANES
    rows0 = ny + 2 * FINE
    count0 = rows0 // 8

    wide = []
    for k in range(n1 + 4):
        for j in range(count1):
            e1[k, pl.ds(j, 8, stride=count1), :] = t1[COARSE - 2 + k, j, 0]
        wide.append(e1[k, :r1])
        wide.append(jnp.where(sub < 2, e1[k, r1:r1 + 8], roll(e1[k, r1 + 8:r1 + 16], 4, 0)))
    matrix = jnp.where(iota((lanes1, nz), 0) == iota((lanes1, nz), 1) // 2, 1.0, 0.0).astype(F32)
    wide = dot(jnp.concatenate(wide, 0), matrix)
    base = SOURCE + COARSE
    beyond = 2 * n1 + 2 * SOURCE + 2 * COARSE
    for k in range(n1 + 4):
        at = k * (r1 + 8)
        for t in range(pieces):
            lanes = slice(t * LANES, (t + 1) * LANES)
            for i in range(2):
                double[t, pl.ds(i, r1, stride=2), :] = wide[at:at + r1, lanes]
                double[t, pl.ds(ny + i, 4, stride=2), :] = wide[at + r1:at + r1 + 4, lanes]
            value = double[t, :rows0]
            for i in range(2):
                p = 2 * k + i
                q = p - FINE
                if p < FINE - POST or q >= nx + POST:
                    continue
                if 0 <= q < nx:
                    own = v0[q, :, lanes]
                else:
                    message, slot = (low, p - (FINE - POST)) if q < 0 else (high, q - nx)
                    own = jnp.concatenate([message[base + 4 * slot + 2 * h + t] for h in range(2)], 0)
                side = pl.ds(t * FINE, FINE)
                at_side = beyond + p - (FINE - POST)
                side = jnp.concatenate((right[at_side, side, :], left[at_side, side, :]), 0)
                field[p, t, :ny] = own + value[:ny]
                field[p, t, ny:] = side + value[ny:]

    def arrange(p):
        for j in range(count0):
            for t in range(pieces):
                u0[p, j, t] = field[p, t, pl.ds(j, 8, stride=count0), :]

    planes(FINE - POST, FINE + nx + POST, arrange)
    sweep(reader(u0), t0, level0, FINE - 2, FINE + nx + 2)
    sweep(reader(t0), u0, level0, FINE - 1, FINE + nx + 1)
    sweep(reader(u0), t0, level0, FINE, FINE + nx)

    def put(k):
        for t in range(pieces):
            for j in range(count0):
                field[k, t, pl.ds(j, 8, stride=count0), :] = t0[FINE + k, j, t]
            out[k, :, t * LANES:(t + 1) * LANES] = field[k, t, :ny]

    planes(0, nx, put)


def call(kernel, outs, scratch, *args, scalars=0):
    specs = [pl.BlockSpec(memory_space=pltpu.SMEM if k < scalars else pltpu.VMEM) for k in range(len(args))]
    return pl.pallas_call(
        kernel,
        out_shape=outs,
        in_specs=specs,
        out_specs=[pl.BlockSpec(memory_space=pltpu.VMEM) for _ in outs],
        scratch_shapes=scratch,
        compiler_params=pltpu.CompilerParams(vmem_limit_bytes=VMEM_LIMIT),
    )(*args)


def shape(*dims):
    return jax.ShapeDtypeStruct(dims, F32)


def exchange(up, down, axis):
    count = lax.axis_size(axis)
    forward = [(i, i + 1) for i in range(count - 1)]
    backward = [(target, source) for source, target in forward]
    return lax.ppermute(up, axis, forward), lax.ppermute(down, axis, backward)


def body(guess, right_side, coefficient):
    gx, gy = lax.axis_size("gx"), lax.axis_size("gy")
    nx, ny, nz = guess.shape
    fields = ((guess, FINE), (right_side, FINE - 1), (coefficient, FINE))
    low, high = exchange(
        jnp.concatenate([f[nx - k:] for f, k in fields], 0), jnp.concatenate([f[:k] for f, k in fields], 0), "gx"
    )

    def rows(cut):
        parts, at = [], 0
        for f, k in fields:
            parts += [cut(low[at:at + k]), cut(f), cut(high[at:at + k])]
            at += k
        return jnp.concatenate(parts, 0)

    left, right = exchange(rows(lambda f: f[:, ny - FINE:]), rows(lambda f: f[:, :FINE]), "gy")

    planes0, rows0, pieces = nx + 2 * FINE, ny + 2 * FINE, nz // LANES
    block0 = (planes0, rows0 // 8, pieces, 8, LANES)
    plain0 = (planes0, pieces, rows0, LANES)
    n1, r1, z1 = nx // 2, ny // 2, nz // 2
    message = (SOURCE + COARSE + 4 * POST, r1, z1)
    v0, *level0, up, down, b1, c1 = call(
        fine_pre_kernel,
        (shape(nx, ny, nz),) + (shape(*block0),) * 5 + (shape(*message),) * 2 + (shape(n1, r1, z1),) * 2,
        [vmem(*plain0)] * 3 + [vmem(*block0)] * 3 + [vmem(n1 * rows0, LANES)] * pieces,
        guess, right_side, coefficient, low, high, left, right,
    )
    low, high = exchange(up, down, "gx")
    count = 3 * n1 + 2 * SOURCE + 2 * COARSE + 2 * POST + n1
    up, down = call(rows_kernel, (shape(count, COARSE, z1),) * 2, (), b1, c1, v0, low, high)
    left, right = exchange(up, down, "gy")

    planes1, rows1 = n1 + 2 * COARSE, r1 + 2 * COARSE
    block1 = (planes1, rows1 // 8, 1, 8, z1)
    plain1 = (planes1, rows1, z1)
    n2, r2 = n1 // 2, r1 // 2
    v1, *level1, send = call(
        coarse_pre_kernel,
        (shape(*block1),) * 6 + (shape(gx * gy, n2, r2, LANES),),
        [vmem(*plain1)] * 2 + [vmem(*block1)] * 2 + [vmem(n2 // 2 * r2, LANES)] * 2,
        b1, c1, low, high, left, right,
    )
    gathered = lax.all_to_all(send, ("gx", "gy"), 0, 0)
    place_at = jnp.stack((lax.axis_index("gx"), lax.axis_index("gy"))).astype(jnp.int32)

    m2, rows2 = gx * n2 // 2, gy * r2
    m3, m4 = m2 // 4, m2 // 16
    block2, block3, block4 = ((m + 2, rows2 // part, 1, 8, LANES) for m, part in ((m2, 8), (m3, 16), (m4, 32)))
    scratch = (
        [vmem(*block2)] * 3 + [vmem(2, m2, rows2, LANES)] + [vmem(*block2)] * 6
        + [vmem(*block3)] * 10 + [vmem(*block4)] * 8
        + [vmem(*block1)] * 2 + [vmem(planes1, max(rows2 + 16, rows1), z1)]
        + [vmem(*plain0)] + [vmem(*block0)] * 2 + [vmem(pieces, 256, LANES)]
    )
    (out,) = call(
        partial(solve_kernel, gx=gx, gy=gy), (shape(nx, ny, nz),), scratch,
        place_at, gathered, v1, *level1, v0, *level0, low, high, left, right, scalars=1,
    )
    return out


def solution(mesh):
    return jax.shard_map(
        body,
        mesh=mesh,
        in_specs=(P("gx", "gy", None), P("gx", "gy", None), P("gx", "gy", None)),
        out_specs=P("gx", "gy", None),
        check_vma=False,
    )
```

```python
import math
from functools import partial

import jax
import jax.numpy as jnp
from jax import lax
from jax.experimental import pallas as pl
from jax.experimental.pallas import tpu as pltpu
from jax.sharding import PartitionSpec as P

LEVELS = 4
SWEEPS = 3
CHEB = 8

RELAX_WEIGHT = 0.7
CHEBY_LOWER = 0.08
CHEBY_UPPER = 2.0

F32 = jnp.float32
LANES = 128
FINE = SWEEPS + 1
COARSE = 8
SOURCE = COARSE - 1
POST = SWEEPS
BLOCK = 24
SPARE = 4 * 1024 * 1024


def dot(a, b):
    return jnp.dot(a, b, precision=lax.Precision.HIGHEST, preferred_element_type=F32)


def iota(shape, dim):
    return lax.broadcasted_iota(jnp.int32, shape, dim)


def vmem(*shape):
    return pltpu.VMEM(shape, F32)


def roll(x, by, axis):
    return pltpu.roll(x, by % x.shape[axis], axis)


def is_even(axis):
    return lax.axis_index(axis) % 2 == 0


class Sides:
    def __init__(self, axis, first, second):
        self.even, self.first, self.second = is_even(axis), first, second

    def low(self, *at):
        return jnp.where(self.even, self.second[at], self.first[at])

    def high(self, *at):
        return jnp.where(self.even, self.first[at], self.second[at])


def address(axis, first, second, write):
    even = is_even(axis)
    pl.when(even)(lambda: write(first, second))
    pl.when(jnp.logical_not(even))(lambda: write(second, first))


def planes(first, last, step):
    if last - first <= BLOCK:
        for p in range(first, last):
            step(p)
    else:
        lax.fori_loop(first, last, lambda p, carry: (step(p), carry)[1], 0, unroll=4)


def lane_before(x, t, lane):
    moved = roll(x[t], 1, 1)
    return moved if len(x) == 1 else jnp.where(lane == 0, roll(x[t - 1], 1, 1), moved)


def lane_after(x, t, lane):
    moved = roll(x[t], -1, 1)
    return moved if len(x) == 1 else jnp.where(lane == LANES - 1, roll(x[(t + 1) % len(x)], -1, 1), moved)


def weigh(fetch, source, level, first, last, depth, row_edges, scale, omega):
    wx, wy, wz, gain, scaled, total = level
    count, pieces = wy.shape[1:3]
    lane = iota((8, LANES), 1)
    front, back = lane % depth == 0, lane % depth == depth - 1
    top, bottom = iota((8, LANES), 0) == 0, iota((8, LANES), 0) == 7

    def step(p):
        for j in range(count):
            c = [fetch(p, j, t) for t in range(pieces)]
            for t in range(pieces):
                x = c[t]
                lower, upper = fetch(p - 1, j, t), fetch(p + 1, j, t)
                left = fetch(p, j - 1, t) if j else roll(fetch(p, count - 1, t), 1, 0)
                right = fetch(p, j + 1, t) if j < count - 1 else roll(fetch(p, 0, t), -1, 0)
                if row_edges and j == 0:
                    left = jnp.where(top, 0.0, left)
                if row_edges and j == count - 1:
                    right = jnp.where(bottom, 0.0, right)
                near, far = lane_before(c, t, lane), lane_after(c, t, lane)
                if t == 0:
                    near = jnp.where(front, 0.0, near)
                if t == pieces - 1:
                    far = jnp.where(back, 0.0, far)
                below, beside, before = x + lower, x + left, x + near
                s = (below + beside + before) + (3.0 * x + (upper + right + far))
                wx[p, j, t] = below
                if last is not None:
                    wx[p + 1, j, t] = x + upper
                wy[p, j, t] = jnp.where(top, 0.0, beside) if row_edges and j == 0 else beside
                wz[p, j, t] = jnp.where(front, 0.0, before) if t == 0 else before
                gain[p, j, t] = jnp.where(x > 0.0, omega / s, 0.0)
                scaled[p, j, t] = source(p, j, t) * (2.0 / scale)
                if total is not None:
                    total[p, j, t] = s

    planes(first, last, step)


def around(fetch, level, p, finish):
    wx, wy, wz = level[:3]
    count, pieces = wy.shape[1:3]
    lane = iota((8, LANES), 1)
    v = [[fetch(p, j, t) for t in range(pieces)] for j in range(count)]
    beside = [wy[p, 0, t] for t in range(pieces)]
    wrap = [roll(beside[t] * v[0][t], -1, 0) for t in range(pieces)]
    for j in range(count):
        ahead = [wy[p, j + 1, t] for t in range(pieces)] if j < count - 1 else None
        before = [wz[p, j, t] for t in range(pieces)]
        flow = [before[t] * v[j][t] for t in range(pieces)]
        for t in range(pieces):
            total = wx[p, j, t] * fetch(p - 1, j, t) + wx[p + 1, j, t] * fetch(p + 1, j, t)
            total += beside[t] * (v[j - 1][t] if j else roll(v[count - 1][t], 1, 0))
            total += ahead[t] * v[j + 1][t] if j < count - 1 else wrap[t]
            total += before[t] * lane_before(v[j], t, lane) + lane_after(flow, t, lane)
            finish(j, t, v[j][t], total)
        beside = ahead


def reader(ref):
    return lambda p, j, t: ref[p, j, t]


def sweep(fetch, out, level, first, last):
    gain, scaled = level[3:5]

    def step(p):
        def finish(j, t, v, total):
            out[p, j, t] = (1.0 - RELAX_WEIGHT) * v + gain[p, j, t] * (scaled[p, j, t] + total)

        around(fetch, level, p, finish)

    planes(first, last, step)


def start(out, level, first, last):
    gain, scaled = level[3:5]

    def step(p):
        for j in range(out.shape[1]):
            for t in range(out.shape[2]):
                out[p, j, t] = gain[p, j, t] * scaled[p, j, t]

    planes(first, last, step)


def residual(fetch, level, p):
    scaled, total = level[4:6]
    found = {}

    def finish(j, t, v, near):
        found[j, t] = (scaled[p, j, t] + near) - v * total[p, j, t]

    around(fetch, level, p, finish)
    return found


def halve_lanes(lanes, width, value, offset=0):
    return jnp.where(iota((lanes, width), 0) // 2 + offset == iota((lanes, width), 1), value, 0.0).astype(F32)


def pack_lanes(lanes, value):
    return jnp.concatenate((halve_lanes(lanes, LANES, value), halve_lanes(lanes, LANES, value, lanes // 2)), 0)


def even_odd(ref, count):
    return ref[pl.ds(0, count, stride=2), :] + ref[pl.ds(1, count, stride=2), :]


def edge_kernel(guess0, guess1, source0, source1, coef0, coef1, first, second):
    def write(up, down):
        at = 0
        for lower, upper, width in ((guess0, guess1, FINE), (source0, source1, FINE - 1), (coef0, coef1, FINE)):
            up[at:at + width] = upper[FINE - width:]
            down[at:at + width] = lower[:width]
            at += width

    address("gx", first, second, write)


def own_kernel(guess, source, coef, up, down, c1, send, *pairs):
    nx, ny, nz = guess.shape
    pieces = nz // LANES
    n1, r1 = nx // 2, ny // 2
    for which, field in enumerate((guess, source, coef)):
        def edges(k):
            up[which * nx + k] = field[k, ny - FINE:, :]
            down[which * nx + k] = field[k, :FINE, :]

        planes(0, nx, edges)
    for q in range(n1):
        for t in range(pieces):
            lanes = slice(t * LANES, (t + 1) * LANES)
            pairs[t][q * ny:(q + 1) * ny, :] = coef[2 * q, :, lanes] + coef[2 * q + 1, :, lanes]
    wide = jnp.concatenate([even_odd(pairs[t], n1 * r1) for t in range(pieces)], 1)
    c1[...] = dot(wide, halve_lanes(nz, nz // 2, 0.125)).reshape(n1, r1, nz // 2)

    n2, r2 = n1 // 2, r1 // 2
    for q in range(n2):
        pairs[0][q * r1:(q + 1) * r1, :] = c1[2 * q] + c1[2 * q + 1]
    narrow = even_odd(pairs[0], n2 * r2)
    wide = jnp.concatenate((narrow[:n2 * r2 // 2], narrow[n2 * r2 // 2:]), 1)
    c2 = dot(wide, pack_lanes(nz // 2, 0.125)).reshape(n2 // 2, r2, LANES)
    for d in range(send.shape[0]):
        send[d] = c2


def corner_kernel(own_up, own_down, one, two, first, second):
    nx = own_up.shape[0] // 3
    sides = Sides("gx", one, two)
    ny = one.shape[1]

    def write(up, down):
        at = base = 0
        for which, width in enumerate((FINE, FINE - 1, FINE)):
            for k in range(width):
                for message, slot in ((sides.low, at + k), (sides.high, at + width + nx + k)):
                    up[slot] = message(base + k, pl.ds(ny - FINE, FINE))
                    down[slot] = message(base + k, pl.ds(0, FINE))
            for k in range(nx):
                up[at + width + k] = own_up[which * nx + k]
                down[at + width + k] = own_down[which * nx + k]
            at += nx + 2 * width
            base += width

    address("gy", first, second, write)


def fine_pre_kernel(guess, source, coef, c1, one, two, three, four, done,
                    out, wx, wy, wz, gain, scaled, first, second, b1,
                    field, force, c, v, w, total, *pairs):
    nx, ny, nz = guess.shape
    across, beside = Sides("gx", one, two), Sides("gy", three, four)
    pieces = nz // LANES
    rows = ny + 2 * FINE
    count = rows // 8
    planes0 = nx + 2 * FINE
    level = (wx, wy, wz, gain, scaled, total)

    def fill(target, own, base, width):
        at = FINE - width
        offset = sum(nx + 2 * k for k in base)
        message = sum(base)

        def rest(k):
            side = jnp.concatenate((beside.high(offset + k), beside.low(offset + k)), 0)
            for t in range(pieces):
                target[at + k, t, ny:] = side[:, t * LANES:(t + 1) * LANES]

        planes(0, nx + 2 * width, rest)

        def main(k):
            for t in range(pieces):
                target[FINE + k, t, :ny] = own[k, :, t * LANES:(t + 1) * LANES]

        planes(0, nx, main)
        for k in range(width):
            for t in range(pieces):
                place = (message + k, slice(None), slice(t * LANES, (t + 1) * LANES))
                target[at + k, t, :ny] = across.low(*place)
                target[FINE + nx + k, t, :ny] = across.high(*place)

    def spaced(ref):
        return lambda p, j, t: ref[p, t, pl.ds(j, 8, stride=count), :]

    fill(field, guess, (), FINE)
    fill(force, source, (FINE,), FINE - 1)
    fill(c, coef, (FINE, FINE - 1), FINE)
    def arrange(p):
        for j in range(count):
            for t in range(pieces):
                w[p, j, t] = spaced(c)(p, j, t)

    planes(0, planes0, arrange)
    weigh(reader(w), spaced(force), level, 1, planes0 - 1, LANES, False, 1.0, RELAX_WEIGHT)

    def arrange_field(p):
        for j in range(count):
            for t in range(pieces):
                v[p, j, t] = spaced(field)(p, j, t)

    planes(0, planes0, arrange_field)
    sweep(reader(v), w, level, 1, planes0 - 1)
    sweep(reader(w), v, level, 2, planes0 - 2)
    sweep(reader(v), w, level, 3, planes0 - 3)

    def put(k):
        for t in range(pieces):
            for j in range(count):
                field[k, t, pl.ds(j, 8, stride=count), :] = w[FINE + k, j, t]
            out[k, :, t * LANES:(t + 1) * LANES] = field[k, t, :ny]

    planes(0, nx, put)

    n1, r1 = nx // 2, ny // 2

    def coarsen(value):
        wide = jnp.concatenate(
            [jnp.concatenate([even_odd(pairs[t].at[pl.ds(q * rows, ny)], r1) for t in range(pieces)], 1) for q in range(n1)], 0
        )
        return dot(wide, halve_lanes(nz, nz // 2, value)).reshape(n1, r1, nz // 2)

    def halve(q):
        one, two = (residual(reader(w), level, FINE + 2 * q + k) for k in range(2))
        for j in range(count):
            for t in range(pieces):
                pairs[t][pl.ds(q * rows + j, 8, stride=count), :] = one[j, t] + two[j, t]

    planes(0, n1, halve)
    b1[...] = coarsen(0.125 * 0.5)

    def write(up, down):
        up[:SOURCE] = b1[n1 - SOURCE:]
        down[:SOURCE] = b1[:SOURCE]
        up[SOURCE:SOURCE + COARSE] = c1[n1 - COARSE:]
        down[SOURCE:SOURCE + COARSE] = c1[:COARSE]
        at = SOURCE + COARSE
        for k in range(POST):
            for i in range(2):
                for j in range(2):
                    here, lanes = pl.ds(i * r1, r1), pl.ds(j * (nz // 2), nz // 2)
                    up[at] = out[nx - POST + k, here, lanes]
                    down[at] = out[k, here, lanes]
                    at += 1

    address("gx", first, second, write)


def rows_kernel(b1, c1, v, one, two, first, second):
    n1, r1, half = b1.shape
    nx, ny = 2 * n1, 2 * r1
    sides = Sides("gx", one, two)

    def write(up, down):
        def edge(take, at):
            up[at] = take(pl.ds(r1 - COARSE, COARSE))
            down[at] = take(pl.ds(0, COARSE))

        at = base = 0
        for own, width in ((b1, SOURCE), (c1, COARSE)):
            for k in range(width):
                edge(lambda rows: sides.low(base + k, rows), at + k)
                edge(lambda rows: sides.high(base + k, rows), at + width + n1 + k)
            for k in range(n1):
                edge(lambda rows: own[k, rows, :], at + width + k)
            at += n1 + 2 * width
            base += width
        for j in range(2):
            rows, lanes = pl.ds(j * FINE, FINE), pl.ds(j * half, half)
            last, start = pl.ds(r1 - FINE, FINE), pl.ds(0, FINE)
            for k in range(POST):
                for message, slot in ((sides.low, at + k), (sides.high, at + POST + nx + k)):
                    up[slot, rows, :] = message(base + 4 * k + 2 + j, last)
                    down[slot, rows, :] = message(base + 4 * k + j, start)
            for k in range(nx):
                up[at + POST + k, rows, :] = v[k, ny - FINE:, lanes]
                down[at + POST + k, rows, :] = v[k, :FINE, lanes]

    address("gy", first, second, write)


def coarse_pre_kernel(b1, c1, one, two, three, four,
                      v, wx, wy, wz, gain, scaled, send, field, c, w, total, upper, lower):
    n1, r1, lanes = b1.shape
    rows = r1 + 2 * COARSE
    count = rows // 8
    planes1 = n1 + 2 * COARSE
    scale = 0.25
    level = (wx, wy, wz, gain, scaled, total)
    across, beside = Sides("gx", one, two), Sides("gy", three, four)

    def fill(target, own, base, offset, width):
        at = COARSE - width
        for k in range(n1 + 2 * width):
            target[at + k, r1:r1 + COARSE] = beside.high(offset + k)
            target[at + k, r1 + COARSE:] = beside.low(offset + k)
        for k in range(n1):
            target[COARSE + k, :r1] = own[k]
        for k in range(width):
            target[at + k, :r1] = across.low(base + k)
            target[COARSE + n1 + k, :r1] = across.high(base + k)

    def spaced(ref):
        return lambda p, j, t: ref[p, pl.ds(j, 8, stride=count), :]

    fill(field, b1, 0, 0, SOURCE)
    fill(c, c1, SOURCE, n1 + 2 * SOURCE, COARSE)
    for p in range(planes1):
        for j in range(count):
            w[p, j, 0] = spaced(c)(p, j, 0)
    weigh(reader(w), spaced(field), level, 1, planes1 - 1, lanes, False, scale, RELAX_WEIGHT)
    start(v, level, 1, planes1 - 1)
    sweep(reader(v), w, level, 2, planes1 - 2)
    sweep(reader(w), v, level, 3, planes1 - 3)

    n2, r2 = n1 // 2, r1 // 2
    half = n2 // 2

    for q in range(n2):
        one, two = (residual(reader(v), level, COARSE + 2 * q + k) for k in range(2))
        target = lower if q < half else upper
        for j in range(count // 2):
            value = (one[2 * j, 0] + two[2 * j, 0]) + (one[2 * j + 1, 0] + two[2 * j + 1, 0])
            target[pl.ds(q % half * r2 + j, r1 // count, stride=count // 2), :] = value[:r1 // count]
    wide = jnp.concatenate((lower[...], upper[...]), 1)
    b2 = dot(wide, pack_lanes(lanes, 0.125 * 0.5 * scale)).reshape(half, r2, LANES)
    for d in range(send.shape[0]):
        send[d] = b2


def pads(ref, depth):
    last = ref.shape[0] - 1
    for j in range(ref.shape[1]):
        ref[0, j, 0] = roll(ref[last - 1, j, 0], depth, 1)
        ref[last, j, 0] = roll(ref[1, j, 0], -depth, 1)


def regroup(depth):
    source, target = iota((2 * LANES, LANES), 0), iota((2 * LANES, LANES), 1)
    group, lane = source // LANES, source % LANES
    block, z = lane // depth, lane % depth
    return (2 * block + group) * (depth // 2) + z // 2 == target


def solve_kernel(gathered_b, gathered_c, v1, wx1, wy1, wz1, gain1, scaled1, v0, wx0, wy0, wz0, gain0, scaled0,
                 one, two, three, four, out,
                 c2, a2, y2, n2, l2x, l2y, l2z, l2g, l2s, l2t,
                 c3, b3, a3, y3, l3x, l3y, l3z, l3g, l3s, l3t,
                 c4, b4, y4, l4x, l4y, l4z, l4g, l4s,
                 u1, t1, e1, field, u0, t0, double, *, gx, gy):
    level2 = (l2x, l2y, l2z, l2g, l2s, l2t)
    level3 = (l3x, l3y, l3z, l3g, l3s, l3t)
    level4 = (l4x, l4y, l4z, l4g, l4s, None)
    across, beside = Sides("gx", one, two), Sides("gy", three, four)
    half, r2 = gathered_b.shape[1:3]
    per = 2 * half
    m2, m3, m4 = c2.shape[0] - 2, c3.shape[0] - 2, c4.shape[0] - 2
    j2, j3, j4 = c2.shape[1], c3.shape[1], c4.shape[1]
    rows2 = 8 * j2
    depth2 = LANES // 2
    depth3, depth4 = depth2 // 2, depth2 // 4
    lane = iota((8, LANES), 1)

    def unpack(i):
        for j in range(gy):
            for k in range(half):
                for which, gathered in enumerate((gathered_b, gathered_c)):
                    near = gathered[i * gy + j, k]
                    far = gathered[(i + gx // 2) * gy + j, k]
                    here = pl.ds(j * r2, r2)
                    n2[which, i * per + k, here, :] = jnp.where(lane < depth2, near, roll(far, depth2, 1))
                    n2[which, i * per + half + k, here, :] = jnp.where(lane < depth2, roll(near, depth2, 1), far)

    planes(0, gx // 2, unpack)

    def spread(p):
        for j in range(j2):
            c2[1 + p, j, 0] = n2[1, p, pl.ds(j, 8, stride=j2), :]

    planes(0, m2, spread)

    def level_in(c, source, level, depth, scale, omega):
        last = c.shape[0] - 1
        lane = iota((8, LANES), 1)
        for j in range(c.shape[1]):
            c[0, j, 0] = jnp.where(lane < depth, 0.0, roll(c[last - 1, j, 0], depth, 1))
            c[last, j, 0] = jnp.where(lane >= LANES - depth, 0.0, roll(c[1, j, 0], -depth, 1))
        weigh(reader(c), source, level, 1, last, depth, True, scale, omega)
        wx = level[0]
        for j in range(c.shape[1]):
            wx[1, j, 0] = jnp.where(lane < depth, 0.0, wx[1, j, 0])
            wx[last, j, 0] = jnp.where(lane >= LANES - depth, 0.0, wx[last, j, 0])

    def smooth(first, other, level, depth, sweeps):
        for _ in range(sweeps):
            pads(first, depth)
            sweep(reader(first), other, level, 1, first.shape[0] - 1)
            first, other = other, first
        return first, other

    def down(fetch, count, rows, depth, out, value):
        def pair(m, g):
            at = g * (count // 2) + 2 * m + 1
            one, two = fetch(at), fetch(at + 1)
            return [(one[2 * j] + two[2 * j]) + (one[2 * j + 1] + two[2 * j + 1]) for j in range(rows // 2)]

        parts = [jnp.concatenate(both, 1) for m in range(count // 4) for both in zip(pair(m, 0), pair(m, 1))]
        matrix = jnp.where(regroup(depth), value, 0.0).astype(F32)
        found = dot(jnp.concatenate(parts, 0), matrix)
        at = 0
        for m in range(count // 4):
            for j in range(rows // 2):
                out[1 + m, j, 0] = found[at:at + 8]
                at += 8

    def up(coarse, fine, depth):
        count, rows = fine.shape[0] - 2, fine.shape[1]
        matrix = jnp.where(regroup(depth), 1.0, 0.0).astype(F32)
        x = jnp.concatenate([coarse[1 + m, j, 0] for m in range(count // 4) for j in range(rows // 2)], 0)
        x = lax.dot_general(x, matrix, (((1,), (1,)), ((), ())), precision=lax.Precision.HIGHEST,
                            preferred_element_type=F32)
        at = 0
        for m in range(count // 4):
            for j in range(rows // 2):
                for g in range(2):
                    value = x[at:at + 8, g * LANES:(g + 1) * LANES]
                    for k in range(2):
                        p = g * (count // 2) + 2 * m + 1 + k
                        for i in range(2):
                            fine[p, 2 * j + i, 0] = fine[p, 2 * j + i, 0] + value
                at += 8

    def rest(field, level):
        return lambda p: [value for _, value in sorted(residual(reader(field), level, p).items())]

    def whole(ref):
        return lambda p: [ref[p, j, 0] for j in range(ref.shape[1])]

    level_in(c2, lambda p, j, t: n2[0, p - 1, pl.ds(j, 8, stride=j2), :], level2, depth2, 0.25**2, RELAX_WEIGHT)
    start(a2, level2, 1, m2 + 1)
    x2, z2 = smooth(a2, y2, level2, depth2, SWEEPS - 1)
    pads(x2, depth2)
    down(whole(c2), m2, j2, depth2, c3, 0.125)
    down(rest(x2, level2), m2, j2, depth2, b3, 0.125 * 0.5 * 0.25**2)

    level_in(c3, reader(b3), level3, depth3, 0.25**3, RELAX_WEIGHT)
    start(a3, level3, 1, m3 + 1)
    x3, z3 = smooth(a3, y3, level3, depth3, SWEEPS - 1)
    pads(x3, depth3)
    down(whole(c3), m3, j3, depth3, c4, 0.125)
    down(rest(x3, level3), m3, j3, depth3, b4, 0.125 * 0.5 * 0.25**3)

    level_in(c4, reader(b4), level4, depth4, 0.25**4, 1.0)
    theta, delta = (CHEBY_UPPER + CHEBY_LOWER) / 2.0, (CHEBY_UPPER - CHEBY_LOWER) / 2.0
    sigma = theta / delta
    rho = 1.0 / sigma
    cells = [(1 + p, j) for p in range(m4) for j in range(j4)]
    res = {at: l4g[at[0], at[1], 0] * l4s[at[0], at[1], 0] for at in cells}
    direction = {at: res[at] / theta for at in cells}
    total = {at: jnp.zeros((8, LANES), F32) for at in cells}
    for _ in range(CHEB):
        for p, j in cells:
            total[p, j] = total[p, j] + direction[p, j]
            y4[p, j, 0] = direction[p, j]
        pads(y4, depth4)
        for p in range(1, m4 + 1):
            def finish(j, t, v, near):
                res[p, j] = res[p, j] - (v - l4g[p, j, 0] * near)

            around(reader(y4), level4, p, finish)
        rho_new = 1.0 / (2.0 * sigma - rho)
        direction = {at: rho_new * rho * direction[at] + (2.0 * rho_new / delta) * res[at] for at in cells}
        rho = rho_new
    for p, j in cells:
        b4[p, j, 0] = total[p, j]

    up(b4, x3, depth3)
    x3, z3 = smooth(x3, z3, level3, depth3, SWEEPS)
    up(x3, x2, depth2)
    x2, z2 = smooth(x2, z2, level2, depth2, SWEEPS)

    level1 = (wx1, wy1, wz1, gain1, scaled1, None)
    at_x, at_y = lax.axis_index("gx"), lax.axis_index("gy")
    planes1, count1, _, _, lanes1 = v1.shape
    n1, r1 = planes1 - 2 * COARSE, 8 * count1 - 2 * COARSE
    sub = iota((8, LANES), 0)
    reach = SWEEPS + 2
    first, last = -((reach + 1) // 2), (n1 + reach + 1) // 2
    pad = rows2 + 8
    e1[0, :8] = jnp.zeros((8, LANES), F32)
    e1[0, pad:] = jnp.zeros((8, LANES), F32)
    window = []
    for t in range(first, last):
        x = at_x * per + t
        inside = (x >= 0) & (x < gx * per)
        x = jnp.clip(x, 0, gx * per - 1)
        block = x // m2
        slot = t - first
        for j in range(j2):
            value = x2[1 + x - block * m2, j, 0]
            value = jnp.where(block == 0, value, roll(value, depth2, 1))
            e1[0, pl.ds(8 + j, 8, stride=j2), :] = jnp.where(inside, value, 0.0)
        base = pl.multiple_of(at_y * r2, 8)
        above, here, after = (e1[0, pl.ds(base + 8 * k, 8), :] for k in range(3))
        t1[slot, 0, 0] = here
        t1[slot, 1, 0] = jnp.where(sub < 4, after, above)
    wide = jnp.concatenate([t1[slot, k, 0] for slot in range(last - first) for k in range(2)], 0)
    matrix = jnp.where(iota((LANES, lanes1), 0) == iota((LANES, lanes1), 1) // 2, 1.0, 0.0).astype(F32)
    double[0, :wide.shape[0]] = dot(wide, matrix)
    for t in range(first, last):
        part = [double[0, pl.ds(16 * (t - first) + j, 8, stride=2), :] for j in range(2)]
        for k in range(2):
            p = COARSE + 2 * t + k
            for j in range(count1):
                u1[p, j, 0] = v1[p, j, 0] + part[j // 2]
    sweep(reader(u1), t1, level1, COARSE - 4, COARSE + n1 + 4)
    sweep(reader(t1), u1, level1, COARSE - 3, COARSE + n1 + 3)
    sweep(reader(u1), t1, level1, COARSE - 2, COARSE + n1 + 2)

    level0 = (wx0, wy0, wz0, gain0, scaled0, None)
    nx, ny, nz = v0.shape
    pieces = nz // LANES
    rows0 = ny + 2 * FINE
    count0 = rows0 // 8

    wide = []
    for k in range(n1 + 4):
        for j in range(count1):
            e1[k, pl.ds(j, 8, stride=count1), :] = t1[COARSE - 2 + k, j, 0]
        wide.append(e1[k, :r1])
        wide.append(jnp.where(sub < 2, e1[k, r1:r1 + 8], roll(e1[k, r1 + 8:r1 + 16], 4, 0)))
    matrix = jnp.where(iota((lanes1, nz), 0) == iota((lanes1, nz), 1) // 2, 1.0, 0.0).astype(F32)
    wide = dot(jnp.concatenate(wide, 0), matrix)
    base = SOURCE + COARSE
    beyond = 2 * n1 + 2 * SOURCE + 2 * COARSE
    for k in range(n1 + 4):
        at = k * (r1 + 8)
        for t in range(pieces):
            lanes = slice(t * LANES, (t + 1) * LANES)
            for i in range(2):
                double[t, pl.ds(i, r1, stride=2), :] = wide[at:at + r1, lanes]
                double[t, pl.ds(ny + i, 4, stride=2), :] = wide[at + r1:at + r1 + 4, lanes]
            value = double[t, :rows0]
            for i in range(2):
                p = 2 * k + i
                q = p - FINE
                if p < FINE - POST or q >= nx + POST:
                    continue
                if 0 <= q < nx:
                    own = v0[q, :, lanes]
                else:
                    message, slot = (across.low, p - (FINE - POST)) if q < 0 else (across.high, q - nx)
                    own = jnp.concatenate([message(base + 4 * slot + 2 * h + t) for h in range(2)], 0)
                side = pl.ds(t * FINE, FINE)
                at_side = beyond + p - (FINE - POST)
                side = jnp.concatenate((beside.high(at_side, side), beside.low(at_side, side)), 0)
                field[p, t, :ny] = own + value[:ny]
                field[p, t, ny:] = side + value[ny:]

    def arrange(p):
        for j in range(count0):
            for t in range(pieces):
                u0[p, j, t] = field[p, t, pl.ds(j, 8, stride=count0), :]

    planes(FINE - POST, FINE + nx + POST, arrange)
    sweep(reader(u0), t0, level0, FINE - 2, FINE + nx + 2)
    sweep(reader(t0), u0, level0, FINE - 1, FINE + nx + 1)
    sweep(reader(u0), t0, level0, FINE, FINE + nx)

    def put(k):
        for t in range(pieces):
            for j in range(count0):
                field[k, t, pl.ds(j, 8, stride=count0), :] = t0[FINE + k, j, t]
            out[k, :, t * LANES:(t + 1) * LANES] = field[k, t, :ny]

    planes(0, nx, put)


def limit(scratch, more):
    need = sum(4 * math.prod(x.inner_aval.shape) for x in scratch)
    return pltpu.CompilerParams(vmem_limit_bytes=SPARE + need + 2 * more)


def call(kernel, outs, scratch, *args, specs=None):
    if specs is None:
        specs = [None] * len(args)
    args = [x if spec and spec.memory_space == pl.ANY else pltpu.with_memory_space_constraint(x, pltpu.HBM if spec else pltpu.VMEM) for x, spec in zip(args, specs)]
    size = sum(4 * math.prod(x.shape) for x, spec in zip(args, specs) if spec)
    whole = pl.BlockSpec(memory_space=pltpu.VMEM)
    return pl.pallas_call(
        kernel,
        grid=(1,) if any(spec and spec.block_shape for spec in specs) else (),
        out_shape=outs,
        in_specs=[spec or whole for spec in specs],
        out_specs=[whole for _ in outs],
        scratch_shapes=scratch,
        compiler_params=limit(scratch, size),
    )(*args)


def shape(*dims):
    return pltpu.VMEM(dims, F32)


def swap(first, second, axis):
    count = lax.axis_size(axis)
    even = [(i, i ^ 1) for i in range(count) if i ^ 1 < count]
    odd = [(i, ((i + 1) ^ 1) - 1) for i in range(count) if 0 <= ((i + 1) ^ 1) - 1 < count]
    return lax.ppermute(first, axis, even), lax.ppermute(second, axis, odd)


def body(guess, right_side, coefficient):
    gx, gy = lax.axis_size("gx"), lax.axis_size("gy")
    nx, ny, nz = guess.shape
    n1, r1, z1 = nx // 2, ny // 2, nz // 2
    n2, r2 = n1 // 2, r1 // 2
    planes0, rows0, pieces = nx + 2 * FINE, ny + 2 * FINE, nz // LANES
    whole = pl.BlockSpec(memory_space=pltpu.VMEM)
    fields = (guess, right_side, coefficient)

    ends = [pl.BlockSpec((FINE, ny, nz), lambda i, at=at: (at, 0, 0)) for at in (0, nx // FINE - 1)]
    across = swap(*call(
        edge_kernel, (shape(3 * FINE - 1, ny, nz),) * 2, (), *(f for f in fields for _ in range(2)), specs=ends * 3
    ), "gx")
    own_up, own_down, c1, send = call(
        own_kernel,
        (shape(3 * nx, FINE, nz),) * 2 + (shape(n1, r1, z1), shape(gx * gy, n2 // 2, r2, LANES)),
        [vmem(n1 * ny, LANES)] * pieces,
        *fields, specs=[whole] * 3,
    )
    gathered_c = lax.all_to_all(send, ("gx", "gy"), 0, 0)
    corners = 3 * nx + 2 * (3 * FINE - 1)
    beside = swap(*call(corner_kernel, (shape(corners, FINE, nz),) * 2, (), own_up, own_down, *across), "gy")

    block0 = (planes0, rows0 // 8, pieces, 8, LANES)
    plain0 = (planes0, pieces, rows0, LANES)
    message = (SOURCE + COARSE + 4 * POST, r1, z1)
    v0, *level0, first, second, b1 = call(
        fine_pre_kernel,
        (shape(nx, ny, nz),) + (shape(*block0),) * 5 + (shape(*message),) * 2 + (shape(n1, r1, z1),),
        [vmem(*plain0)] * 3 + [vmem(*block0)] * 3 + [vmem(n1 * rows0, LANES)] * pieces,
        *fields, c1, *across, *beside, gathered_c, specs=[whole] * 3 + [None] * 5 + [pl.BlockSpec(memory_space=pl.ANY)],
    )
    across = swap(first, second, "gx")
    count = 3 * n1 + 2 * SOURCE + 2 * COARSE + 2 * POST + n1
    beside = swap(*call(rows_kernel, (shape(count, COARSE, z1),) * 2, (), b1, c1, v0, *across), "gy")

    planes1, rows1 = n1 + 2 * COARSE, r1 + 2 * COARSE
    block1 = (planes1, rows1 // 8, 1, 8, z1)
    plain1 = (planes1, rows1, z1)
    v1, *level1, send = call(
        coarse_pre_kernel,
        (shape(*block1),) * 6 + (shape(gx * gy, n2 // 2, r2, LANES),),
        [vmem(*plain1)] * 2 + [vmem(*block1)] * 2 + [vmem(n2 // 2 * r2, LANES)] * 2,
        b1, c1, *across, *beside,
    )
    gathered_b = lax.all_to_all(send, ("gx", "gy"), 0, 0)

    m2, rows2 = gx * n2 // 2, gy * r2
    m3, m4 = m2 // 4, m2 // 16
    block2, block3, block4 = ((m + 2, rows2 // part, 1, 8, LANES) for m, part in ((m2, 8), (m3, 16), (m4, 32)))
    scratch = (
        [vmem(*block2)] * 3 + [vmem(2, m2, rows2, LANES)] + [vmem(*block2)] * 6
        + [vmem(*block3)] * 10 + [vmem(*block4)] * 8
        + [vmem(*block1)] * 2 + [vmem(planes1, max(rows2 + 16, rows1), z1)]
        + [vmem(*plain0)] + [vmem(*block0)] * 2 + [vmem(pieces, 256, LANES)]
    )
    (out,) = pl.pallas_call(
        partial(solve_kernel, gx=gx, gy=gy),
        out_shape=(jax.ShapeDtypeStruct((nx, ny, nz), F32),),
        in_specs=[whole] * 18,
        out_specs=(whole,),
        scratch_shapes=scratch,
        compiler_params=limit(scratch, guess.size * 4),
    )(*(pltpu.with_memory_space_constraint(x, pltpu.VMEM)
        for x in (gathered_b, gathered_c, v1, *level1, v0, *level0, *across, *beside)))
    return out


def solution(mesh):
    return jax.shard_map(
        body,
        mesh=mesh,
        in_specs=(P("gx", "gy", None), P("gx", "gy", None), P("gx", "gy", None)),
        out_specs=P("gx", "gy", None),
        check_vma=False,
    )
```

```python
import math
from functools import partial

import jax
import jax.numpy as jnp
from jax import lax
from jax.experimental import pallas as pl
from jax.experimental.pallas import tpu as pltpu
from jax.sharding import Mesh, PartitionSpec as P

LEVELS = 4
SWEEPS = 3
CHEB = 8

RELAX_WEIGHT = 0.7
CHEBY_LOWER = 0.08
CHEBY_UPPER = 2.0

F32 = jnp.float32
LANES = 128
FINE = SWEEPS + 1
WIDTHS = (FINE - 1, FINE - 1, FINE)
COARSE = 8
SOURCE = COARSE - 1
POST = SWEEPS
SENT = POST - 1
BLOCK = 24
SPARE = 4 * 1024 * 1024


def dot(a, b):
    return jnp.dot(a, b, precision=lax.Precision.HIGHEST, preferred_element_type=F32)


def iota(shape, dim):
    return lax.broadcasted_iota(jnp.int32, shape, dim)


def vmem(*shape):
    return pltpu.VMEM(shape, F32)


def roll(x, by, axis):
    return pltpu.roll(x, by % x.shape[axis], axis)


GX, GY = "gx", ("gy_far", "gy_near")


def is_even(axis):
    return lax.axis_index(axis) % 2 == 0


class Sides:
    def __init__(self, axis, first, second):
        self.even, self.first, self.second = is_even(axis), first, second

    def low(self, *at):
        return jnp.where(self.even, self.second[at], self.first[at])

    def high(self, *at):
        return jnp.where(self.even, self.first[at], self.second[at])


def address(axis, first, second, write):
    even = is_even(axis)
    pl.when(even)(lambda: write(first, second))
    pl.when(jnp.logical_not(even))(lambda: write(second, first))


def planes(first, last, step):
    if last - first <= BLOCK:
        for p in range(first, last):
            step(p)
    else:
        lax.fori_loop(first, last, lambda p, carry: (step(p), carry)[1], 0, unroll=4)


def lane_before(x, t, lane):
    moved = roll(x[t], 1, 1)
    return moved if len(x) == 1 else jnp.where(lane == 0, roll(x[t - 1], 1, 1), moved)


def lane_after(x, t, lane):
    moved = roll(x[t], -1, 1)
    return moved if len(x) == 1 else jnp.where(lane == LANES - 1, roll(x[(t + 1) % len(x)], -1, 1), moved)


def weigh(fetch, source, level, first, last, depth, row_edges, scale, omega):
    wx, wy, wz, gain, scaled, total = level
    count, pieces = wy.shape[1:3]
    lane = iota((8, LANES), 1)
    front, back = lane % depth == 0, lane % depth == depth - 1
    top, bottom = iota((8, LANES), 0) == 0, iota((8, LANES), 0) == 7

    def step(p):
        for j in range(count):
            c = [fetch(p, j, t) for t in range(pieces)]
            for t in range(pieces):
                x = c[t]
                lower, upper = fetch(p - 1, j, t), fetch(p + 1, j, t)
                left = fetch(p, j - 1, t) if j else roll(fetch(p, count - 1, t), 1, 0)
                right = fetch(p, j + 1, t) if j < count - 1 else roll(fetch(p, 0, t), -1, 0)
                if row_edges and j == 0:
                    left = jnp.where(top, 0.0, left)
                if row_edges and j == count - 1:
                    right = jnp.where(bottom, 0.0, right)
                near, far = lane_before(c, t, lane), lane_after(c, t, lane)
                if t == 0:
                    near = jnp.where(front, 0.0, near)
                if t == pieces - 1:
                    far = jnp.where(back, 0.0, far)
                below, beside, before = x + lower, x + left, x + near
                s = (below + beside + before) + (3.0 * x + (upper + right + far))
                wx[p, j, t] = below
                if last is not None:
                    wx[p + 1, j, t] = x + upper
                wy[p, j, t] = jnp.where(top, 0.0, beside) if row_edges and j == 0 else beside
                wz[p, j, t] = jnp.where(front, 0.0, before) if t == 0 else before
                gain[p, j, t] = jnp.where(x > 0.0, omega / s, 0.0)
                scaled[p, j, t] = source(p, j, t) * (2.0 / scale)
                if total is not None:
                    total[p, j, t] = s

    planes(first, last, step)


def around(fetch, level, p, finish):
    wx, wy, wz = level[:3]
    count, pieces = wy.shape[1:3]
    lane = iota((8, LANES), 1)
    v = [[fetch(p, j, t) for t in range(pieces)] for j in range(count)]
    beside = [wy[p, 0, t] for t in range(pieces)]
    wrap = [roll(beside[t] * v[0][t], -1, 0) for t in range(pieces)]
    for j in range(count):
        ahead = [wy[p, j + 1, t] for t in range(pieces)] if j < count - 1 else None
        before = [wz[p, j, t] for t in range(pieces)]
        flow = [before[t] * v[j][t] for t in range(pieces)]
        for t in range(pieces):
            total = wx[p, j, t] * fetch(p - 1, j, t) + wx[p + 1, j, t] * fetch(p + 1, j, t)
            total += beside[t] * (v[j - 1][t] if j else roll(v[count - 1][t], 1, 0))
            total += ahead[t] * v[j + 1][t] if j < count - 1 else wrap[t]
            total += before[t] * lane_before(v[j], t, lane) + lane_after(flow, t, lane)
            finish(j, t, v[j][t], total)
        beside = ahead


def reader(ref):
    return lambda p, j, t: ref[p, j, t]


def sweep(fetch, out, level, first, last):
    gain, scaled = level[3:5]

    def step(p):
        def finish(j, t, v, total):
            out[p, j, t] = (1.0 - RELAX_WEIGHT) * v + gain[p, j, t] * (scaled[p, j, t] + total)

        around(fetch, level, p, finish)

    planes(first, last, step)


def start(out, level, first, last):
    gain, scaled = level[3:5]

    def step(p):
        for j in range(out.shape[1]):
            for t in range(out.shape[2]):
                out[p, j, t] = gain[p, j, t] * scaled[p, j, t]

    planes(first, last, step)


def residual(fetch, level, p):
    scaled, total = level[4:6]
    found = {}

    def finish(j, t, v, near):
        found[j, t] = (scaled[p, j, t] + near) - v * total[p, j, t]

    around(fetch, level, p, finish)
    return found


def halve_lanes(lanes, width, value, offset=0):
    return jnp.where(iota((lanes, width), 0) // 2 + offset == iota((lanes, width), 1), value, 0.0).astype(F32)


def pack_lanes(lanes, value):
    return jnp.concatenate((halve_lanes(lanes, LANES, value), halve_lanes(lanes, LANES, value, lanes // 2)), 0)


def even_odd(ref, count):
    return ref[pl.ds(0, count, stride=2), :] + ref[pl.ds(1, count, stride=2), :]


def edge_kernel(guess0, guess1, source0, source1, coef0, coef1, first, second):
    def write(up, down):
        at = 0
        for lower, upper, width in zip((guess0, source0, coef0), (guess1, source1, coef1), WIDTHS):
            up[at:at + width] = upper[FINE - width:]
            down[at:at + width] = lower[:width]
            at += width
        far = WIDTHS[0]
        up[far] = source1[1] + 0.5 * (coef1[1] + coef1[0]) * guess1[0]
        far += WIDTHS[1] - 1
        down[far] = source0[FINE - 2] + 0.5 * (coef0[FINE - 2] + coef0[FINE - 1]) * guess0[FINE - 1]

    address(GX, first, second, write)


def own_kernel(guess, source, coef, up, down, c1, send, *pairs):
    nx, ny, nz = guess.shape
    pieces = nz // LANES
    n1, r1 = nx // 2, ny // 2
    for which, field in enumerate((guess, source, coef)):
        def edges(k):
            up[which * nx + k] = field[k, ny - FINE:, :]
            down[which * nx + k] = field[k, :FINE, :]

        planes(0, nx, edges)
    for q in range(n1):
        for t in range(pieces):
            lanes = slice(t * LANES, (t + 1) * LANES)
            pairs[t][q * ny:(q + 1) * ny, :] = coef[2 * q, :, lanes] + coef[2 * q + 1, :, lanes]
    wide = jnp.concatenate([even_odd(pairs[t], n1 * r1) for t in range(pieces)], 1)
    c1[...] = dot(wide, halve_lanes(nz, nz // 2, 0.125)).reshape(n1, r1, nz // 2)

    n2, r2 = n1 // 2, r1 // 2
    for q in range(n2):
        pairs[0][q * r1:(q + 1) * r1, :] = c1[2 * q] + c1[2 * q + 1]
    narrow = even_odd(pairs[0], n2 * r2)
    wide = jnp.concatenate((narrow[:n2 * r2 // 2], narrow[n2 * r2 // 2:]), 1)
    c2 = dot(wide, pack_lanes(nz // 2, 0.125)).reshape(n2 // 2, r2, LANES)
    for d in range(send.shape[0]):
        send[d] = c2


def keep_kernel(guess, source, coef, *rest):
    guess_out, source_out, coef_out = rest[-3:]
    guess_out[...] = guess[...]
    source_out[...] = source[...]
    coef_out[...] = coef[...]


def corner_kernel(own_up, own_down, one, two, first, second):
    nx = own_up.shape[0] // 3
    sides = Sides(GX, one, two)
    ny = one.shape[1]

    def write(up, down):
        at = base = 0
        for which, width in enumerate(WIDTHS):
            for k in range(width):
                for message, slot in ((sides.low, at + k), (sides.high, at + width + nx + k)):
                    up[slot] = message(base + k, pl.ds(ny - FINE, FINE))
                    down[slot] = message(base + k, pl.ds(0, FINE))
            for k in range(nx):
                up[at + width + k] = own_up[which * nx + k]
                down[at + width + k] = own_down[which * nx + k]
            at += nx + 2 * width
            base += width

    address(GY, first, second, write)


def fine_pre_kernel(guess, source, coef, c1, one, two, three, four,
                    out, wx, wy, wz, gain, scaled, first, second, b1,
                    field, force, c, v, w, total, *pairs):
    nx, ny, nz = guess.shape
    across, beside = Sides(GX, one, two), Sides(GY, three, four)
    pieces = nz // LANES
    rows = ny + 2 * FINE
    count = rows // 8
    planes0 = nx + 2 * FINE
    level = (wx, wy, wz, gain, scaled, total)

    def fill(target, own, which):
        width = WIDTHS[which]
        at = FINE - width
        offset = sum(nx + 2 * k for k in WIDTHS[:which])
        message = sum(WIDTHS[:which])

        def rest(k):
            side = jnp.concatenate((beside.high(offset + k), beside.low(offset + k)), 0)
            for t in range(pieces):
                target[at + k, t, ny:] = side[:, t * LANES:(t + 1) * LANES]

        planes(0, nx + 2 * width, rest)

        def main(k):
            for t in range(pieces):
                target[FINE + k, t, :ny] = own[k, :, t * LANES:(t + 1) * LANES]

        planes(0, nx, main)
        for k in range(width):
            for t in range(pieces):
                place = (message + k, slice(None), slice(t * LANES, (t + 1) * LANES))
                target[at + k, t, :ny] = across.low(*place)
                target[FINE + nx + k, t, :ny] = across.high(*place)

    def spaced(ref):
        return lambda p, j, t: ref[p, t, pl.ds(j, 8, stride=count), :]

    fill(field, guess, 0)
    fill(force, source, 1)
    fill(c, coef, 2)
    def arrange(p):
        for j in range(count):
            for t in range(pieces):
                w[p, j, t] = spaced(c)(p, j, t)

    planes(0, planes0, arrange)
    weigh(reader(w), spaced(force), level, 1, planes0 - 1, LANES, False, 1.0, RELAX_WEIGHT)

    def arrange_field(p):
        for j in range(count):
            for t in range(pieces):
                v[p, j, t] = spaced(field)(p, j, t)

    planes(1, planes0 - 1, arrange_field)
    for p, face in ((0, 1), (planes0 - 1, planes0 - 1)):
        for j in range(count):
            for t in range(pieces):
                v[p, j, t] = jnp.zeros((8, LANES), F32)
                wx[face, j, t] = jnp.zeros((8, LANES), F32)
    sweep(reader(v), w, level, 1, planes0 - 1)
    sweep(reader(w), v, level, 2, planes0 - 2)
    sweep(reader(v), w, level, 3, planes0 - 3)

    def put(k):
        for t in range(pieces):
            for j in range(count):
                field[k, t, pl.ds(j, 8, stride=count), :] = w[FINE - 1 + k, j, t]
            out[k, :, t * LANES:(t + 1) * LANES] = field[k, t, :ny]

    planes(0, nx + 2, put)

    n1, r1 = nx // 2, ny // 2

    def coarsen(value):
        wide = jnp.concatenate(
            [jnp.concatenate([even_odd(pairs[t].at[pl.ds(q * rows, ny)], r1) for t in range(pieces)], 1) for q in range(n1)], 0
        )
        return dot(wide, halve_lanes(nz, nz // 2, value)).reshape(n1, r1, nz // 2)

    def halve(q):
        one, two = (residual(reader(w), level, FINE + 2 * q + k) for k in range(2))
        for j in range(count):
            for t in range(pieces):
                pairs[t][pl.ds(q * rows + j, 8, stride=count), :] = one[j, t] + two[j, t]

    planes(0, n1, halve)
    b1[...] = coarsen(0.125 * 0.5)

    def write(up, down):
        up[:SOURCE] = b1[n1 - SOURCE:]
        down[:SOURCE] = b1[:SOURCE]
        up[SOURCE:SOURCE + COARSE] = c1[n1 - COARSE:]
        down[SOURCE:SOURCE + COARSE] = c1[:COARSE]
        at = SOURCE + COARSE
        for k in range(SENT):
            for i in range(2):
                for j in range(2):
                    here, lanes = pl.ds(i * r1, r1), pl.ds(j * (nz // 2), nz // 2)
                    up[at] = out[nx - POST + 1 + k, here, lanes]
                    down[at] = out[2 + k, here, lanes]
                    at += 1

    address(GX, first, second, write)


def rows_kernel(b1, c1, v, one, two, first, second):
    n1, r1, half = b1.shape
    nx, ny = 2 * n1, 2 * r1
    sides = Sides(GX, one, two)

    def write(up, down):
        def edge(take, at):
            up[at] = take(pl.ds(r1 - COARSE, COARSE))
            down[at] = take(pl.ds(0, COARSE))

        at = base = 0
        for own, width in ((b1, SOURCE), (c1, COARSE)):
            for k in range(width):
                edge(lambda rows: sides.low(base + k, rows), at + k)
                edge(lambda rows: sides.high(base + k, rows), at + width + n1 + k)
            for k in range(n1):
                edge(lambda rows: own[k, rows, :], at + width + k)
            at += n1 + 2 * width
            base += width
        for j in range(2):
            rows, lanes = pl.ds(j * FINE, FINE), pl.ds(j * half, half)
            last, start = pl.ds(r1 - FINE, FINE), pl.ds(0, FINE)
            for k in range(SENT):
                for message, slot in ((sides.low, at + k), (sides.high, at + SENT + nx + 2 + k)):
                    up[slot, rows, :] = message(base + 4 * k + 2 + j, last)
                    down[slot, rows, :] = message(base + 4 * k + j, start)
            for k in range(nx + 2):
                up[at + SENT + k, rows, :] = v[k, ny - FINE:, lanes]
                down[at + SENT + k, rows, :] = v[k, :FINE, lanes]

    address(GY, first, second, write)


def coarse_pre_kernel(b1, c1, one, two, three, four,
                      v, wx, wy, wz, gain, scaled, send, field, c, w, total, upper, lower):
    n1, r1, lanes = b1.shape
    rows = r1 + 2 * COARSE
    count = rows // 8
    planes1 = n1 + 2 * COARSE
    scale = 0.25
    level = (wx, wy, wz, gain, scaled, total)
    across, beside = Sides(GX, one, two), Sides(GY, three, four)

    def fill(target, own, base, offset, width):
        at = COARSE - width
        for k in range(n1 + 2 * width):
            target[at + k, r1:r1 + COARSE] = beside.high(offset + k)
            target[at + k, r1 + COARSE:] = beside.low(offset + k)
        for k in range(n1):
            target[COARSE + k, :r1] = own[k]
        for k in range(width):
            target[at + k, :r1] = across.low(base + k)
            target[COARSE + n1 + k, :r1] = across.high(base + k)

    def spaced(ref):
        return lambda p, j, t: ref[p, pl.ds(j, 8, stride=count), :]

    fill(field, b1, 0, 0, SOURCE)
    fill(c, c1, SOURCE, n1 + 2 * SOURCE, COARSE)
    for p in range(planes1):
        for j in range(count):
            w[p, j, 0] = spaced(c)(p, j, 0)
    weigh(reader(w), spaced(field), level, 1, planes1 - 1, lanes, False, scale, RELAX_WEIGHT)
    start(v, level, 1, planes1 - 1)
    sweep(reader(v), w, level, 2, planes1 - 2)
    sweep(reader(w), v, level, 3, planes1 - 3)

    n2, r2 = n1 // 2, r1 // 2
    half = n2 // 2

    for q in range(n2):
        one, two = (residual(reader(v), level, COARSE + 2 * q + k) for k in range(2))
        target = lower if q < half else upper
        for j in range(count // 2):
            value = (one[2 * j, 0] + two[2 * j, 0]) + (one[2 * j + 1, 0] + two[2 * j + 1, 0])
            target[pl.ds(q % half * r2 + j, r1 // count, stride=count // 2), :] = value[:r1 // count]
    wide = jnp.concatenate((lower[...], upper[...]), 1)
    b2 = dot(wide, pack_lanes(lanes, 0.125 * 0.5 * scale)).reshape(half, r2, LANES)
    for d in range(send.shape[0]):
        send[d] = b2


def pads(ref, depth):
    last = ref.shape[0] - 1
    for j in range(ref.shape[1]):
        ref[0, j, 0] = roll(ref[last - 1, j, 0], depth, 1)
        ref[last, j, 0] = roll(ref[1, j, 0], -depth, 1)


def regroup(depth):
    source, target = iota((2 * LANES, LANES), 0), iota((2 * LANES, LANES), 1)
    group, lane = source // LANES, source % LANES
    block, z = lane // depth, lane % depth
    return (2 * block + group) * (depth // 2) + z // 2 == target


def solve_kernel(mine_b, other_b, mine_c, other_c, v1, wx1, wy1, wz1, gain1, scaled1, v0, wx0, wy0, wz0, gain0, scaled0,
                 one, two, three, four, out,
                 c2, a2, y2, n2, l2x, l2y, l2z, l2g, l2s, l2t,
                 c3, b3, a3, y3, l3x, l3y, l3z, l3g, l3s, l3t,
                 c4, b4, y4, l4x, l4y, l4z, l4g, l4s,
                 u1, t1, e1, field, u0, t0, double, *, gx, gy):
    level2 = (l2x, l2y, l2z, l2g, l2s, l2t)
    level3 = (l3x, l3y, l3z, l3g, l3s, l3t)
    level4 = (l4x, l4y, l4z, l4g, l4s, None)
    across, beside = Sides(GX, one, two), Sides(GY, three, four)
    half, r2 = mine_b.shape[1:3]
    per = 2 * half
    m2, m3, m4 = c2.shape[0] - 2, c3.shape[0] - 2, c4.shape[0] - 2
    j2, j3, j4 = c2.shape[1], c3.shape[1], c4.shape[1]
    rows2 = 8 * j2
    depth2 = LANES // 2
    depth3, depth4 = depth2 // 2, depth2 // 4
    lane = iota((8, LANES), 1)

    near_one = lax.axis_index(GY[1])

    def unpack(i):
        for j in range(gy):
            for k in range(half):
                for which, (mine, other) in enumerate(((mine_b, other_b), (mine_c, other_c))):
                    def block(x):
                        at = x * (gy // 2) + j // 2
                        return jnp.where(near_one == j % 2, mine[at, k], other[at, k])

                    near, far = block(i), block(i + gx // 2)
                    here = pl.ds(j * r2, r2)
                    n2[which, i * per + k, here, :] = jnp.where(lane < depth2, near, roll(far, depth2, 1))
                    n2[which, i * per + half + k, here, :] = jnp.where(lane < depth2, roll(near, depth2, 1), far)

    planes(0, gx // 2, unpack)

    def spread(p):
        for j in range(j2):
            c2[1 + p, j, 0] = n2[1, p, pl.ds(j, 8, stride=j2), :]

    planes(0, m2, spread)

    def level_in(c, source, level, depth, scale, omega):
        last = c.shape[0] - 1
        lane = iota((8, LANES), 1)
        for j in range(c.shape[1]):
            c[0, j, 0] = jnp.where(lane < depth, 0.0, roll(c[last - 1, j, 0], depth, 1))
            c[last, j, 0] = jnp.where(lane >= LANES - depth, 0.0, roll(c[1, j, 0], -depth, 1))
        weigh(reader(c), source, level, 1, last, depth, True, scale, omega)
        wx = level[0]
        for j in range(c.shape[1]):
            wx[1, j, 0] = jnp.where(lane < depth, 0.0, wx[1, j, 0])
            wx[last, j, 0] = jnp.where(lane >= LANES - depth, 0.0, wx[last, j, 0])

    def smooth(first, other, level, depth, sweeps):
        for _ in range(sweeps):
            pads(first, depth)
            sweep(reader(first), other, level, 1, first.shape[0] - 1)
            first, other = other, first
        return first, other

    def down(fetch, count, rows, depth, out, value):
        def pair(m, g):
            at = g * (count // 2) + 2 * m + 1
            one, two = fetch(at), fetch(at + 1)
            return [(one[2 * j] + two[2 * j]) + (one[2 * j + 1] + two[2 * j + 1]) for j in range(rows // 2)]

        parts = [jnp.concatenate(both, 1) for m in range(count // 4) for both in zip(pair(m, 0), pair(m, 1))]
        matrix = jnp.where(regroup(depth), value, 0.0).astype(F32)
        found = dot(jnp.concatenate(parts, 0), matrix)
        at = 0
        for m in range(count // 4):
            for j in range(rows // 2):
                out[1 + m, j, 0] = found[at:at + 8]
                at += 8

    def up(coarse, fine, depth):
        count, rows = fine.shape[0] - 2, fine.shape[1]
        matrix = jnp.where(regroup(depth), 1.0, 0.0).astype(F32)
        x = jnp.concatenate([coarse[1 + m, j, 0] for m in range(count // 4) for j in range(rows // 2)], 0)
        x = lax.dot_general(x, matrix, (((1,), (1,)), ((), ())), precision=lax.Precision.HIGHEST,
                            preferred_element_type=F32)
        at = 0
        for m in range(count // 4):
            for j in range(rows // 2):
                for g in range(2):
                    value = x[at:at + 8, g * LANES:(g + 1) * LANES]
                    for k in range(2):
                        p = g * (count // 2) + 2 * m + 1 + k
                        for i in range(2):
                            fine[p, 2 * j + i, 0] = fine[p, 2 * j + i, 0] + value
                at += 8

    def rest(field, level):
        return lambda p: [value for _, value in sorted(residual(reader(field), level, p).items())]

    def whole(ref):
        return lambda p: [ref[p, j, 0] for j in range(ref.shape[1])]

    level_in(c2, lambda p, j, t: n2[0, p - 1, pl.ds(j, 8, stride=j2), :], level2, depth2, 0.25**2, RELAX_WEIGHT)
    start(a2, level2, 1, m2 + 1)
    x2, z2 = smooth(a2, y2, level2, depth2, SWEEPS - 1)
    pads(x2, depth2)
    down(whole(c2), m2, j2, depth2, c3, 0.125)
    down(rest(x2, level2), m2, j2, depth2, b3, 0.125 * 0.5 * 0.25**2)

    level_in(c3, reader(b3), level3, depth3, 0.25**3, RELAX_WEIGHT)
    start(a3, level3, 1, m3 + 1)
    x3, z3 = smooth(a3, y3, level3, depth3, SWEEPS - 1)
    pads(x3, depth3)
    down(whole(c3), m3, j3, depth3, c4, 0.125)
    down(rest(x3, level3), m3, j3, depth3, b4, 0.125 * 0.5 * 0.25**3)

    level_in(c4, reader(b4), level4, depth4, 0.25**4, 1.0)
    theta, delta = (CHEBY_UPPER + CHEBY_LOWER) / 2.0, (CHEBY_UPPER - CHEBY_LOWER) / 2.0
    sigma = theta / delta
    rho = 1.0 / sigma
    cells = [(1 + p, j) for p in range(m4) for j in range(j4)]
    res = {at: l4g[at[0], at[1], 0] * l4s[at[0], at[1], 0] for at in cells}
    direction = {at: res[at] / theta for at in cells}
    total = {at: jnp.zeros((8, LANES), F32) for at in cells}
    for _ in range(CHEB):
        for p, j in cells:
            total[p, j] = total[p, j] + direction[p, j]
            y4[p, j, 0] = direction[p, j]
        pads(y4, depth4)
        for p in range(1, m4 + 1):
            def finish(j, t, v, near):
                res[p, j] = res[p, j] - (v - l4g[p, j, 0] * near)

            around(reader(y4), level4, p, finish)
        rho_new = 1.0 / (2.0 * sigma - rho)
        direction = {at: rho_new * rho * direction[at] + (2.0 * rho_new / delta) * res[at] for at in cells}
        rho = rho_new
    for p, j in cells:
        b4[p, j, 0] = total[p, j]

    up(b4, x3, depth3)
    x3, z3 = smooth(x3, z3, level3, depth3, SWEEPS)
    up(x3, x2, depth2)
    x2, z2 = smooth(x2, z2, level2, depth2, SWEEPS)

    level1 = (wx1, wy1, wz1, gain1, scaled1, None)
    at_x, at_y = lax.axis_index(GX), lax.axis_index(GY)
    planes1, count1, _, _, lanes1 = v1.shape
    n1, r1 = planes1 - 2 * COARSE, 8 * count1 - 2 * COARSE
    sub = iota((8, LANES), 0)
    reach = SWEEPS + 2
    first, last = -((reach + 1) // 2), (n1 + reach + 1) // 2
    pad = rows2 + 8
    e1[0, :8] = jnp.zeros((8, LANES), F32)
    e1[0, pad:] = jnp.zeros((8, LANES), F32)
    window = []
    for t in range(first, last):
        x = at_x * per + t
        inside = (x >= 0) & (x < gx * per)
        x = jnp.clip(x, 0, gx * per - 1)
        block = x // m2
        slot = t - first
        for j in range(j2):
            value = x2[1 + x - block * m2, j, 0]
            value = jnp.where(block == 0, value, roll(value, depth2, 1))
            e1[0, pl.ds(8 + j, 8, stride=j2), :] = jnp.where(inside, value, 0.0)
        base = pl.multiple_of(at_y * r2, 8)
        above, here, after = (e1[0, pl.ds(base + 8 * k, 8), :] for k in range(3))
        t1[slot, 0, 0] = here
        t1[slot, 1, 0] = jnp.where(sub < 4, after, above)
    wide = jnp.concatenate([t1[slot, k, 0] for slot in range(last - first) for k in range(2)], 0)
    matrix = jnp.where(iota((LANES, lanes1), 0) == iota((LANES, lanes1), 1) // 2, 1.0, 0.0).astype(F32)
    double[0, :wide.shape[0]] = dot(wide, matrix)
    for t in range(first, last):
        part = [double[0, pl.ds(16 * (t - first) + j, 8, stride=2), :] for j in range(2)]
        for k in range(2):
            p = COARSE + 2 * t + k
            for j in range(count1):
                u1[p, j, 0] = v1[p, j, 0] + part[j // 2]
    sweep(reader(u1), t1, level1, COARSE - 4, COARSE + n1 + 4)
    sweep(reader(t1), u1, level1, COARSE - 3, COARSE + n1 + 3)
    sweep(reader(u1), t1, level1, COARSE - 2, COARSE + n1 + 2)

    level0 = (wx0, wy0, wz0, gain0, scaled0, None)
    nx, ny, nz = out.shape
    pieces = nz // LANES
    rows0 = ny + 2 * FINE
    count0 = rows0 // 8

    wide = []
    for k in range(n1 + 4):
        for j in range(count1):
            e1[k, pl.ds(j, 8, stride=count1), :] = t1[COARSE - 2 + k, j, 0]
        wide.append(e1[k, :r1])
        wide.append(jnp.where(sub < 2, e1[k, r1:r1 + 8], roll(e1[k, r1 + 8:r1 + 16], 4, 0)))
    matrix = jnp.where(iota((lanes1, nz), 0) == iota((lanes1, nz), 1) // 2, 1.0, 0.0).astype(F32)
    wide = dot(jnp.concatenate(wide, 0), matrix)
    base = SOURCE + COARSE
    beyond = 2 * n1 + 2 * SOURCE + 2 * COARSE
    for k in range(n1 + 4):
        at = k * (r1 + 8)
        for t in range(pieces):
            lanes = slice(t * LANES, (t + 1) * LANES)
            for i in range(2):
                double[t, pl.ds(i, r1, stride=2), :] = wide[at:at + r1, lanes]
                double[t, pl.ds(ny + i, 4, stride=2), :] = wide[at + r1:at + r1 + 4, lanes]
            value = double[t, :rows0]
            for i in range(2):
                p = 2 * k + i
                q = p - FINE
                if p < FINE - POST or q >= nx + POST:
                    continue
                if -1 <= q <= nx:
                    own = v0[q + 1, :, lanes]
                else:
                    message, slot = (across.low, q + POST) if q < 0 else (across.high, q - nx - 1)
                    own = jnp.concatenate([message(base + 4 * slot + 2 * h + t) for h in range(2)], 0)
                side = pl.ds(t * FINE, FINE)
                at_side = beyond + p - (FINE - POST)
                side = jnp.concatenate((beside.high(at_side, side), beside.low(at_side, side)), 0)
                field[p, t, :ny] = own + value[:ny]
                field[p, t, ny:] = side + value[ny:]

    def arrange(p):
        for j in range(count0):
            for t in range(pieces):
                u0[p, j, t] = field[p, t, pl.ds(j, 8, stride=count0), :]

    planes(FINE - POST, FINE + nx + POST, arrange)
    sweep(reader(u0), t0, level0, FINE - 2, FINE + nx + 2)
    sweep(reader(t0), u0, level0, FINE - 1, FINE + nx + 1)
    sweep(reader(u0), t0, level0, FINE, FINE + nx)

    def put(k):
        for t in range(pieces):
            for j in range(count0):
                field[k, t, pl.ds(j, 8, stride=count0), :] = t0[FINE + k, j, t]
            out[k, :, t * LANES:(t + 1) * LANES] = field[k, t, :ny]

    planes(0, nx, put)


def limit(scratch, more):
    need = sum(4 * math.prod(x.inner_aval.shape) for x in scratch)
    return pltpu.CompilerParams(vmem_limit_bytes=SPARE + need + 2 * more)


def call(kernel, outs, scratch, *args, specs=None):
    if specs is None:
        specs = [None] * len(args)
    args = [x if spec and spec.memory_space == pl.ANY else pltpu.with_memory_space_constraint(x, pltpu.HBM if spec else pltpu.VMEM) for x, spec in zip(args, specs)]
    size = sum(4 * math.prod(x.shape) for x, spec in zip(args, specs) if spec)
    whole = pl.BlockSpec(memory_space=pltpu.VMEM)
    return pl.pallas_call(
        kernel,
        grid=(1,) if any(spec and spec.block_shape for spec in specs) else (),
        out_shape=outs,
        in_specs=[spec or whole for spec in specs],
        out_specs=[whole for _ in outs],
        scratch_shapes=scratch,
        compiler_params=limit(scratch, size),
    )(*args)


def shape(*dims):
    return pltpu.VMEM(dims, F32)


def swap(first, second, axis):
    count = lax.axis_size(axis)
    even = [(i, i ^ 1) for i in range(count) if i ^ 1 < count]
    odd = [(i, ((i + 1) ^ 1) - 1) for i in range(count) if 0 <= ((i + 1) ^ 1) - 1 < count]
    return lax.ppermute(first, axis, even), lax.ppermute(second, axis, odd)


def spread(send):
    found = lax.all_to_all(send, (GX, GY[0]), 0, 0)
    return found, lax.ppermute(found, GY[1], [(0, 1), (1, 0)])


def body(guess, right_side, coefficient):
    gx, gy = lax.axis_size(GX), lax.axis_size(GY)
    nx, ny, nz = guess.shape
    n1, r1, z1 = nx // 2, ny // 2, nz // 2
    n2, r2 = n1 // 2, r1 // 2
    planes0, rows0, pieces = nx + 2 * FINE, ny + 2 * FINE, nz // LANES
    whole = pl.BlockSpec(memory_space=pltpu.VMEM)
    fields = (guess, right_side, coefficient)

    ends = [pl.BlockSpec((FINE, ny, nz), lambda i, at=at: (at, 0, 0)) for at in (0, nx // FINE - 1)]
    across = swap(*call(
        edge_kernel, (shape(sum(WIDTHS), ny, nz),) * 2, (), *(f for f in fields for _ in range(2)), specs=ends * 3
    ), GX)
    own_up, own_down, c1, send = call(
        own_kernel,
        (shape(3 * nx, FINE, nz),) * 2 + (shape(n1, r1, z1), shape(gx * gy // 2, n2 // 2, r2, LANES)),
        [vmem(n1 * ny, LANES)] * pieces,
        *fields, specs=[whole] * 3,
    )
    gathered_c = spread(send)
    corners = 3 * nx + 2 * sum(WIDTHS)
    rows = call(corner_kernel, (shape(corners, FINE, nz),) * 2, (), own_up, own_down, *across)
    beside = swap(*rows, GY)
    fields = call(
        keep_kernel, (shape(nx, ny, nz),) * 3, (), *fields, gathered_c[1], rows[0],
        specs=[whole] * 3 + [pl.BlockSpec(memory_space=pl.ANY)] * 2,
    )

    block0 = (planes0, rows0 // 8, pieces, 8, LANES)
    plain0 = (planes0, pieces, rows0, LANES)
    message = (SOURCE + COARSE + 4 * SENT, r1, z1)
    v0, *level0, first, second, b1 = call(
        fine_pre_kernel,
        (shape(nx + 2, ny, nz),) + (shape(*block0),) * 5 + (shape(*message),) * 2 + (shape(n1, r1, z1),),
        [vmem(*plain0)] * 3 + [vmem(*block0)] * 3 + [vmem(n1 * rows0, LANES)] * pieces,
        *fields, c1, *across, *beside, specs=[None] * 8,
    )
    across = swap(first, second, GX)
    count = 3 * n1 + 2 * SOURCE + 2 * COARSE + 2 * POST + n1
    beside = swap(*call(rows_kernel, (shape(count, COARSE, z1),) * 2, (), b1, c1, v0, *across), GY)

    planes1, rows1 = n1 + 2 * COARSE, r1 + 2 * COARSE
    block1 = (planes1, rows1 // 8, 1, 8, z1)
    plain1 = (planes1, rows1, z1)
    v1, *level1, send = call(
        coarse_pre_kernel,
        (shape(*block1),) * 6 + (shape(gx * gy // 2, n2 // 2, r2, LANES),),
        [vmem(*plain1)] * 2 + [vmem(*block1)] * 2 + [vmem(n2 // 2 * r2, LANES)] * 2,
        b1, c1, *across, *beside,
    )
    gathered_b = spread(send)

    m2, rows2 = gx * n2 // 2, gy * r2
    m3, m4 = m2 // 4, m2 // 16
    block2, block3, block4 = ((m + 2, rows2 // part, 1, 8, LANES) for m, part in ((m2, 8), (m3, 16), (m4, 32)))
    scratch = (
        [vmem(*block2)] * 3 + [vmem(2, m2, rows2, LANES)] + [vmem(*block2)] * 6
        + [vmem(*block3)] * 10 + [vmem(*block4)] * 8
        + [vmem(*block1)] * 2 + [vmem(planes1, max(rows2 + 16, rows1), z1)]
        + [vmem(*plain0)] + [vmem(*block0)] * 2 + [vmem(pieces, 256, LANES)]
    )
    (out,) = pl.pallas_call(
        partial(solve_kernel, gx=gx, gy=gy),
        out_shape=(jax.ShapeDtypeStruct((nx, ny, nz), F32),),
        in_specs=[whole] * 20,
        out_specs=(whole,),
        scratch_shapes=scratch,
        compiler_params=limit(scratch, guess.size * 4),
    )(*(pltpu.with_memory_space_constraint(x, pltpu.VMEM)
        for x in (*gathered_b, *gathered_c, v1, *level1, v0, *level0, *across, *beside)))
    return out


def solution(mesh):
    gx, gy = mesh.devices.shape
    mesh = Mesh(mesh.devices.reshape(gx, gy // 2, 2), (GX, *GY))
    return jax.shard_map(
        body,
        mesh=mesh,
        in_specs=(P(GX, GY, None),) * 3,
        out_specs=P(GX, GY, None),
        check_vma=False,
    )
```

```python
import math
from functools import partial

import jax
import jax.numpy as jnp
from jax import lax
from jax.experimental import pallas as pl
from jax.experimental.pallas import tpu as pltpu
from jax.sharding import Mesh, PartitionSpec as P

LEVELS = 4
SWEEPS = 3
CHEB = 8

RELAX_WEIGHT = 0.7
CHEBY_LOWER = 0.08
CHEBY_UPPER = 2.0

F32 = jnp.float32
LANES = 128
PARTS = 2
FINE = SWEEPS + 1
WIDTHS = (FINE - 1, FINE - 1, FINE)
COARSE = 8
SOURCE = COARSE - 1
LOCAL = FINE // 2
POST = SWEEPS
SENT = POST - 1
BLOCK = 24
SPARE = 4 * 1024 * 1024


def dot(a, b):
    b = b.astype(jnp.bfloat16)
    parts = []
    for _ in range(PARTS):
        parts.append(a.astype(jnp.bfloat16))
        a = a - parts[-1].astype(F32)
    found = [jnp.dot(part, b, preferred_element_type=F32) for part in reversed(parts)]
    return sum(found[1:], found[0])


def iota(shape, dim):
    return lax.broadcasted_iota(jnp.int32, shape, dim)


def vmem(*shape):
    return pltpu.VMEM(shape, F32)


def roll(x, by, axis):
    return pltpu.roll(x, by % x.shape[axis], axis)


GX, GY = "gx", ("gy_far", "gy_near")


def is_even(axis):
    return lax.axis_index(axis) % 2 == 0


class Sides:
    def __init__(self, axis, first, second):
        self.even, self.first, self.second = is_even(axis), first, second

    def low(self, *at):
        return jnp.where(self.even, self.second[at], self.first[at])

    def high(self, *at):
        return jnp.where(self.even, self.first[at], self.second[at])


def address(axis, first, second, write):
    even = is_even(axis)
    pl.when(even)(lambda: write(first, second))
    pl.when(jnp.logical_not(even))(lambda: write(second, first))


def planes(first, last, step):
    if last - first <= BLOCK:
        for p in range(first, last):
            step(p)
    else:
        lax.fori_loop(first, last, lambda p, carry: (step(p), carry)[1], 0, unroll=4)


def lane_before(x, t, lane):
    moved = roll(x[t], 1, 1)
    return moved if len(x) == 1 else jnp.where(lane == 0, roll(x[t - 1], 1, 1), moved)


def lane_after(x, t, lane):
    moved = roll(x[t], -1, 1)
    return moved if len(x) == 1 else jnp.where(lane == LANES - 1, roll(x[(t + 1) % len(x)], -1, 1), moved)


def weigh(fetch, source, level, first, last, depth, row_edges, scale, omega):
    wx, wy, wz, gain, scaled, total = level
    count, pieces = wy.shape[1:3]
    lane = iota((8, LANES), 1)
    front, back = lane % depth == 0, lane % depth == depth - 1
    top, bottom = iota((8, LANES), 0) == 0, iota((8, LANES), 0) == 7

    def step(p):
        for j in range(count):
            c = [fetch(p, j, t) for t in range(pieces)]
            for t in range(pieces):
                x = c[t]
                lower, upper = fetch(p - 1, j, t), fetch(p + 1, j, t)
                left = fetch(p, j - 1, t) if j else roll(fetch(p, count - 1, t), 1, 0)
                right = fetch(p, j + 1, t) if j < count - 1 else roll(fetch(p, 0, t), -1, 0)
                if row_edges and j == 0:
                    left = jnp.where(top, 0.0, left)
                if row_edges and j == count - 1:
                    right = jnp.where(bottom, 0.0, right)
                near, far = lane_before(c, t, lane), lane_after(c, t, lane)
                if t == 0:
                    near = jnp.where(front, 0.0, near)
                if t == pieces - 1:
                    far = jnp.where(back, 0.0, far)
                below, beside, before = x + lower, x + left, x + near
                s = (below + beside + before) + (3.0 * x + (upper + right + far))
                wx[p, j, t] = below
                if last is not None:
                    wx[p + 1, j, t] = x + upper
                wy[p, j, t] = jnp.where(top, 0.0, beside) if row_edges and j == 0 else beside
                wz[p, j, t] = jnp.where(front, 0.0, before) if t == 0 else before
                gain[p, j, t] = jnp.where(x > 0.0, omega / s, 0.0)
                scaled[p, j, t] = source(p, j, t) * (2.0 / scale)
                if total is not None:
                    total[p, j, t] = s

    planes(first, last, step)


def around(fetch, level, p, finish):
    wx, wy, wz = level[:3]
    count, pieces = wy.shape[1:3]
    lane = iota((8, LANES), 1)
    v = [[fetch(p, j, t) for t in range(pieces)] for j in range(count)]
    beside = [wy[p, 0, t] for t in range(pieces)]
    wrap = [roll(beside[t] * v[0][t], -1, 0) for t in range(pieces)]
    for j in range(count):
        ahead = [wy[p, j + 1, t] for t in range(pieces)] if j < count - 1 else None
        before = [wz[p, j, t] for t in range(pieces)]
        flow = [before[t] * v[j][t] for t in range(pieces)]
        for t in range(pieces):
            total = wx[p, j, t] * fetch(p - 1, j, t) + wx[p + 1, j, t] * fetch(p + 1, j, t)
            total += beside[t] * (v[j - 1][t] if j else roll(v[count - 1][t], 1, 0))
            total += ahead[t] * v[j + 1][t] if j < count - 1 else wrap[t]
            total += before[t] * lane_before(v[j], t, lane) + lane_after(flow, t, lane)
            finish(j, t, v[j][t], total)
        beside = ahead


def reader(ref):
    return lambda p, j, t: ref[p, j, t]


def sweep(fetch, out, level, first, last):
    gain, scaled = level[3:5]

    def step(p):
        def finish(j, t, v, total):
            out[p, j, t] = (1.0 - RELAX_WEIGHT) * v + gain[p, j, t] * (scaled[p, j, t] + total)

        around(fetch, level, p, finish)

    planes(first, last, step)


def start(out, level, first, last):
    gain, scaled = level[3:5]

    def step(p):
        for j in range(out.shape[1]):
            for t in range(out.shape[2]):
                out[p, j, t] = gain[p, j, t] * scaled[p, j, t]

    planes(first, last, step)


def residual(fetch, level, p):
    scaled, total = level[4:6]
    found = {}

    def finish(j, t, v, near):
        found[j, t] = (scaled[p, j, t] + near) - v * total[p, j, t]

    around(fetch, level, p, finish)
    return found


def halve_lanes(lanes, width, value, offset=0):
    return jnp.where(iota((lanes, width), 0) // 2 + offset == iota((lanes, width), 1), value, 0.0).astype(F32)


def pack_lanes(lanes, value):
    return jnp.concatenate((halve_lanes(lanes, LANES, value), halve_lanes(lanes, LANES, value, lanes // 2)), 0)


def even_odd(ref, count):
    return ref[pl.ds(0, count, stride=2), :] + ref[pl.ds(1, count, stride=2), :]


def edge_kernel(guess0, guess1, source0, source1, coef0, coef1, first, second):
    def write(up, down):
        at = 0
        for lower, upper, width in zip((guess0, source0, coef0), (guess1, source1, coef1), WIDTHS):
            up[at:at + width] = upper[FINE - width:]
            down[at:at + width] = lower[:width]
            at += width
        far = WIDTHS[0]
        up[far] = source1[1] + 0.5 * (coef1[1] + coef1[0]) * guess1[0]
        far += WIDTHS[1] - 1
        down[far] = source0[FINE - 2] + 0.5 * (coef0[FINE - 2] + coef0[FINE - 1]) * guess0[FINE - 1]

    address(GX, first, second, write)


def own_kernel(guess, source, coef, up, down, c1, send, *pairs):
    nx, ny, nz = guess.shape
    pieces = nz // LANES
    n1, r1 = nx // 2, ny // 2
    for which, field in enumerate((guess, source, coef)):
        def edges(k):
            up[which * nx + k] = field[k, ny - FINE:, :]
            down[which * nx + k] = field[k, :FINE, :]

        planes(0, nx, edges)
    for q in range(n1):
        for t in range(pieces):
            lanes = slice(t * LANES, (t + 1) * LANES)
            pairs[t][q * ny:(q + 1) * ny, :] = coef[2 * q, :, lanes] + coef[2 * q + 1, :, lanes]
    wide = jnp.concatenate([even_odd(pairs[t], n1 * r1) for t in range(pieces)], 1)
    c1[...] = dot(wide, halve_lanes(nz, nz // 2, 0.125)).reshape(n1, r1, nz // 2)

    n2, r2 = n1 // 2, r1 // 2
    for q in range(n2):
        pairs[0][q * r1:(q + 1) * r1, :] = c1[2 * q] + c1[2 * q + 1]
    narrow = even_odd(pairs[0], n2 * r2)
    wide = jnp.concatenate((narrow[:n2 * r2 // 2], narrow[n2 * r2 // 2:]), 1)
    c2 = dot(wide, pack_lanes(nz // 2, 0.125)).reshape(n2 // 2, r2, LANES)
    for d in range(send.shape[0]):
        send[d] = c2


def keep_kernel(guess, source, coef, *rest):
    guess_out, source_out, coef_out = rest[-3:]
    guess_out[...] = guess[...]
    source_out[...] = source[...]
    coef_out[...] = coef[...]


def corner_kernel(own_up, own_down, one, two, first, second):
    nx = own_up.shape[0] // 3
    sides = Sides(GX, one, two)
    ny = one.shape[1]

    def write(up, down):
        at = base = 0
        for which, width in enumerate(WIDTHS):
            for k in range(width):
                for message, slot in ((sides.low, at + k), (sides.high, at + width + nx + k)):
                    up[slot] = message(base + k, pl.ds(ny - FINE, FINE))
                    down[slot] = message(base + k, pl.ds(0, FINE))
            for k in range(nx):
                up[at + width + k] = own_up[which * nx + k]
                down[at + width + k] = own_down[which * nx + k]
            at += nx + 2 * width
            base += width

    address(GY, first, second, write)


def fine_pre_kernel(guess, source, coef, c1, one, two, three, four,
                    out, wx, wy, wz, gain, scaled, first, second, b1, local,
                    field, force, c, v, w, total, *pairs):
    nx, ny, nz = guess.shape
    across, beside = Sides(GX, one, two), Sides(GY, three, four)
    pieces = nz // LANES
    rows = ny + 2 * FINE
    count = rows // 8
    planes0 = nx + 2 * FINE
    level = (wx, wy, wz, gain, scaled, total)

    def fill(target, own, which):
        width = WIDTHS[which]
        at = FINE - width
        offset = sum(nx + 2 * k for k in WIDTHS[:which])
        message = sum(WIDTHS[:which])

        def rest(k):
            side = jnp.concatenate((beside.high(offset + k), beside.low(offset + k)), 0)
            for t in range(pieces):
                target[at + k, t, ny:] = side[:, t * LANES:(t + 1) * LANES]

        planes(0, nx + 2 * width, rest)

        def main(k):
            for t in range(pieces):
                target[FINE + k, t, :ny] = own[k, :, t * LANES:(t + 1) * LANES]

        planes(0, nx, main)
        for k in range(width):
            for t in range(pieces):
                place = (message + k, slice(None), slice(t * LANES, (t + 1) * LANES))
                target[at + k, t, :ny] = across.low(*place)
                target[FINE + nx + k, t, :ny] = across.high(*place)

    def spaced(ref):
        return lambda p, j, t: ref[p, t, pl.ds(j, 8, stride=count), :]

    fill(field, guess, 0)
    fill(force, source, 1)
    fill(c, coef, 2)
    def arrange(p):
        for j in range(count):
            for t in range(pieces):
                w[p, j, t] = spaced(c)(p, j, t)

    planes(0, planes0, arrange)
    weigh(reader(w), spaced(force), level, 1, planes0 - 1, LANES, False, 1.0, RELAX_WEIGHT)

    def arrange_field(p):
        for j in range(count):
            for t in range(pieces):
                v[p, j, t] = spaced(field)(p, j, t)

    planes(1, planes0 - 1, arrange_field)
    for p, face in ((0, 1), (planes0 - 1, planes0 - 1)):
        for j in range(count):
            for t in range(pieces):
                v[p, j, t] = jnp.zeros((8, LANES), F32)
                wx[face, j, t] = jnp.zeros((8, LANES), F32)
    sweep(reader(v), w, level, 1, planes0 - 1)
    sweep(reader(w), v, level, 2, planes0 - 2)
    sweep(reader(v), w, level, 3, planes0 - 3)

    def put(k):
        for t in range(pieces):
            for j in range(count):
                field[k, t, pl.ds(j, 8, stride=count), :] = w[FINE - 1 + k, j, t]
            out[k, :, t * LANES:(t + 1) * LANES] = field[k, t, :ny]

    planes(0, nx + 2, put)

    n1, r1 = nx // 2, ny // 2

    def coarsen(value, number):
        wide = jnp.concatenate(
            [jnp.concatenate([even_odd(pairs[t].at[pl.ds(q * rows, ny)], r1) for t in range(pieces)], 1) for q in range(number)], 0
        )
        return dot(wide, halve_lanes(nz, nz // 2, value)).reshape(number, r1, nz // 2)

    for k in range(2 * LOCAL):
        p = 2 * k if k < LOCAL else nx + 2 * k
        for t in range(pieces):
            pairs[t][k * rows:k * rows + ny, :] = c[p, t, :ny] + c[p + 1, t, :ny]
    local[...] = coarsen(0.125, 2 * LOCAL)

    def halve(q):
        one, two = (residual(reader(w), level, FINE + 2 * q + k) for k in range(2))
        for j in range(count):
            for t in range(pieces):
                pairs[t][pl.ds(q * rows + j, 8, stride=count), :] = one[j, t] + two[j, t]

    planes(0, n1, halve)
    b1[...] = coarsen(0.125 * 0.5, n1)

    def write(up, down):
        up[:SOURCE] = b1[n1 - SOURCE:]
        down[:SOURCE] = b1[:SOURCE]
        at = SOURCE + COARSE - LOCAL
        up[SOURCE:at] = c1[n1 - COARSE:n1 - LOCAL]
        down[SOURCE:at] = c1[LOCAL:COARSE]
        for k in range(SENT):
            for i in range(2):
                for j in range(2):
                    here, lanes = pl.ds(i * r1, r1), pl.ds(j * (nz // 2), nz // 2)
                    up[at] = out[nx - POST + 1 + k, here, lanes]
                    down[at] = out[2 + k, here, lanes]
                    at += 1

    address(GX, first, second, write)


def rows_kernel(b1, c1, local, v, one, two, first, second):
    n1, r1, half = b1.shape
    nx, ny = 2 * n1, 2 * r1
    sides = Sides(GX, one, two)

    def write(up, down):
        def edge(take, at):
            up[at] = take(pl.ds(r1 - COARSE, COARSE))
            down[at] = take(pl.ds(0, COARSE))

        at = base = 0
        for own, width, known in ((b1, SOURCE, 0), (c1, COARSE, LOCAL)):
            for k in range(width - known):
                edge(lambda rows: sides.low(base + k, rows), at + k)
                edge(lambda rows: sides.high(base + k, rows), at + width + n1 + known + k)
            for k in range(known):
                edge(lambda rows: local[k, rows, :], at + width - known + k)
                edge(lambda rows: local[known + k, rows, :], at + width + n1 + k)
            for k in range(n1):
                edge(lambda rows: own[k, rows, :], at + width + k)
            at += n1 + 2 * width
            base += width - known
        for j in range(2):
            rows, lanes = pl.ds(j * FINE, FINE), pl.ds(j * half, half)
            last, start = pl.ds(r1 - FINE, FINE), pl.ds(0, FINE)
            for k in range(SENT):
                for message, slot in ((sides.low, at + k), (sides.high, at + SENT + nx + 2 + k)):
                    up[slot, rows, :] = message(base + 4 * k + 2 + j, last)
                    down[slot, rows, :] = message(base + 4 * k + j, start)
            for k in range(nx + 2):
                up[at + SENT + k, rows, :] = v[k, ny - FINE:, lanes]
                down[at + SENT + k, rows, :] = v[k, :FINE, lanes]

    address(GY, first, second, write)


def coarse_pre_kernel(b1, c1, local, one, two, three, four, sent,
                      v, wx, wy, wz, gain, scaled, send, field, c, w, total, upper, lower):
    n1, r1, lanes = b1.shape
    rows = r1 + 2 * COARSE
    count = rows // 8
    planes1 = n1 + 2 * COARSE
    scale = 0.25
    level = (wx, wy, wz, gain, scaled, total)
    across, beside = Sides(GX, one, two), Sides(GY, three, four)

    def fill(target, own, base, offset, width, known):
        at = COARSE - width
        for k in range(n1 + 2 * width):
            target[at + k, r1:r1 + COARSE] = beside.high(offset + k)
            target[at + k, r1 + COARSE:] = beside.low(offset + k)
        for k in range(n1):
            target[COARSE + k, :r1] = own[k]
        for k in range(width - known):
            target[at + k, :r1] = across.low(base + k)
            target[COARSE + n1 + known + k, :r1] = across.high(base + k)
        for k in range(known):
            target[COARSE - known + k, :r1] = local[k]
            target[COARSE + n1 + k, :r1] = local[known + k]

    def spaced(ref):
        return lambda p, j, t: ref[p, pl.ds(j, 8, stride=count), :]

    fill(field, b1, 0, 0, SOURCE, 0)
    fill(c, c1, SOURCE, n1 + 2 * SOURCE, COARSE, LOCAL)
    for p in range(planes1):
        for j in range(count):
            w[p, j, 0] = spaced(c)(p, j, 0)
    weigh(reader(w), spaced(field), level, 1, planes1 - 1, lanes, False, scale, RELAX_WEIGHT)
    start(v, level, 1, planes1 - 1)
    sweep(reader(v), w, level, 2, planes1 - 2)
    sweep(reader(w), v, level, 3, planes1 - 3)

    n2, r2 = n1 // 2, r1 // 2
    half = n2 // 2

    for q in range(n2):
        one, two = (residual(reader(v), level, COARSE + 2 * q + k) for k in range(2))
        target = lower if q < half else upper
        for j in range(count // 2):
            value = (one[2 * j, 0] + two[2 * j, 0]) + (one[2 * j + 1, 0] + two[2 * j + 1, 0])
            target[pl.ds(q % half * r2 + j, r1 // count, stride=count // 2), :] = value[:r1 // count]
    wide = jnp.concatenate((lower[...], upper[...]), 1)
    b2 = dot(wide, pack_lanes(lanes, 0.125 * 0.5 * scale)).reshape(half, r2, LANES)
    for d in range(send.shape[0]):
        send[d] = b2


def pads(ref, depth):
    last = ref.shape[0] - 1
    for j in range(ref.shape[1]):
        ref[0, j, 0] = roll(ref[last - 1, j, 0], depth, 1)
        ref[last, j, 0] = roll(ref[1, j, 0], -depth, 1)


def regroup(depth, back=False):
    dims = (LANES, 2 * LANES) if back else (2 * LANES, LANES)
    source, target = iota(dims, int(back)), iota(dims, 1 - int(back))
    group, lane = source // LANES, source % LANES
    block, z = lane // depth, lane % depth
    return (2 * block + group) * (depth // 2) + z // 2 == target


def solve_kernel(mine_b, other_b, mine_c, other_c, v1, wx1, wy1, wz1, gain1, scaled1, v0, wx0, wy0, wz0, gain0, scaled0,
                 one, two, three, four, out,
                 c2, a2, y2, n2, l2x, l2y, l2z, l2g, l2s, l2t,
                 c3, b3, a3, y3, l3x, l3y, l3z, l3g, l3s, l3t,
                 c4, b4, y4, l4x, l4y, l4z, l4g, l4s,
                 u1, t1, e1, field, u0, t0, double, *, gx, gy):
    level2 = (l2x, l2y, l2z, l2g, l2s, l2t)
    level3 = (l3x, l3y, l3z, l3g, l3s, l3t)
    level4 = (l4x, l4y, l4z, l4g, l4s, None)
    across, beside = Sides(GX, one, two), Sides(GY, three, four)
    half, r2 = mine_b.shape[1:3]
    per = 2 * half
    m2, m3, m4 = c2.shape[0] - 2, c3.shape[0] - 2, c4.shape[0] - 2
    j2, j3, j4 = c2.shape[1], c3.shape[1], c4.shape[1]
    rows2 = 8 * j2
    depth2 = LANES // 2
    depth3, depth4 = depth2 // 2, depth2 // 4
    lane = iota((8, LANES), 1)

    near_one = lax.axis_index(GY[1])

    def unpack(i):
        for j in range(gy):
            for k in range(half):
                for which, (mine, other) in enumerate(((mine_b, other_b), (mine_c, other_c))):
                    def block(x):
                        at = x * (gy // 2) + j // 2
                        return jnp.where(near_one == j % 2, mine[at, k], other[at, k])

                    near, far = block(i), block(i + gx // 2)
                    here = pl.ds(j * r2, r2)
                    n2[which, i * per + k, here, :] = jnp.where(lane < depth2, near, roll(far, depth2, 1))
                    n2[which, i * per + half + k, here, :] = jnp.where(lane < depth2, roll(near, depth2, 1), far)

    planes(0, gx // 2, unpack)

    def spread(p):
        for j in range(j2):
            c2[1 + p, j, 0] = n2[1, p, pl.ds(j, 8, stride=j2), :]

    planes(0, m2, spread)

    def level_in(c, source, level, depth, scale, omega):
        last = c.shape[0] - 1
        lane = iota((8, LANES), 1)
        for j in range(c.shape[1]):
            c[0, j, 0] = jnp.where(lane < depth, 0.0, roll(c[last - 1, j, 0], depth, 1))
            c[last, j, 0] = jnp.where(lane >= LANES - depth, 0.0, roll(c[1, j, 0], -depth, 1))
        weigh(reader(c), source, level, 1, last, depth, True, scale, omega)
        wx = level[0]
        for j in range(c.shape[1]):
            wx[1, j, 0] = jnp.where(lane < depth, 0.0, wx[1, j, 0])
            wx[last, j, 0] = jnp.where(lane >= LANES - depth, 0.0, wx[last, j, 0])

    def smooth(first, other, level, depth, sweeps):
        for _ in range(sweeps):
            pads(first, depth)
            sweep(reader(first), other, level, 1, first.shape[0] - 1)
            first, other = other, first
        return first, other

    def down(fetch, count, rows, depth, out, value):
        def pair(m, g):
            at = g * (count // 2) + 2 * m + 1
            one, two = fetch(at), fetch(at + 1)
            return [(one[2 * j] + two[2 * j]) + (one[2 * j + 1] + two[2 * j + 1]) for j in range(rows // 2)]

        parts = [jnp.concatenate(both, 1) for m in range(count // 4) for both in zip(pair(m, 0), pair(m, 1))]
        matrix = jnp.where(regroup(depth), value, 0.0).astype(F32)
        found = dot(jnp.concatenate(parts, 0), matrix)
        at = 0
        for m in range(count // 4):
            for j in range(rows // 2):
                out[1 + m, j, 0] = found[at:at + 8]
                at += 8

    def up(coarse, fine, depth):
        count, rows = fine.shape[0] - 2, fine.shape[1]
        matrix = jnp.where(regroup(depth, True), 1.0, 0.0).astype(F32)
        x = jnp.concatenate([coarse[1 + m, j, 0] for m in range(count // 4) for j in range(rows // 2)], 0)
        x = dot(x, matrix)
        at = 0
        for m in range(count // 4):
            for j in range(rows // 2):
                for g in range(2):
                    value = x[at:at + 8, g * LANES:(g + 1) * LANES]
                    for k in range(2):
                        p = g * (count // 2) + 2 * m + 1 + k
                        for i in range(2):
                            fine[p, 2 * j + i, 0] = fine[p, 2 * j + i, 0] + value
                at += 8

    def rest(field, level):
        return lambda p: [value for _, value in sorted(residual(reader(field), level, p).items())]

    def whole(ref):
        return lambda p: [ref[p, j, 0] for j in range(ref.shape[1])]

    level_in(c2, lambda p, j, t: n2[0, p - 1, pl.ds(j, 8, stride=j2), :], level2, depth2, 0.25**2, RELAX_WEIGHT)
    start(a2, level2, 1, m2 + 1)
    x2, z2 = smooth(a2, y2, level2, depth2, SWEEPS - 1)
    pads(x2, depth2)
    down(whole(c2), m2, j2, depth2, c3, 0.125)
    down(rest(x2, level2), m2, j2, depth2, b3, 0.125 * 0.5 * 0.25**2)

    level_in(c3, reader(b3), level3, depth3, 0.25**3, RELAX_WEIGHT)
    start(a3, level3, 1, m3 + 1)
    x3, z3 = smooth(a3, y3, level3, depth3, SWEEPS - 1)
    pads(x3, depth3)
    down(whole(c3), m3, j3, depth3, c4, 0.125)
    down(rest(x3, level3), m3, j3, depth3, b4, 0.125 * 0.5 * 0.25**3)

    level_in(c4, reader(b4), level4, depth4, 0.25**4, 1.0)
    theta, delta = (CHEBY_UPPER + CHEBY_LOWER) / 2.0, (CHEBY_UPPER - CHEBY_LOWER) / 2.0
    sigma = theta / delta
    rho = 1.0 / sigma
    cells = [(1 + p, j) for p in range(m4) for j in range(j4)]
    res = {at: l4g[at[0], at[1], 0] * l4s[at[0], at[1], 0] for at in cells}
    direction = {at: res[at] / theta for at in cells}
    total = {at: jnp.zeros((8, LANES), F32) for at in cells}
    for _ in range(CHEB):
        for p, j in cells:
            total[p, j] = total[p, j] + direction[p, j]
            y4[p, j, 0] = direction[p, j]
        pads(y4, depth4)
        for p in range(1, m4 + 1):
            def finish(j, t, v, near):
                res[p, j] = res[p, j] - (v - l4g[p, j, 0] * near)

            around(reader(y4), level4, p, finish)
        rho_new = 1.0 / (2.0 * sigma - rho)
        direction = {at: rho_new * rho * direction[at] + (2.0 * rho_new / delta) * res[at] for at in cells}
        rho = rho_new
    for p, j in cells:
        b4[p, j, 0] = total[p, j]

    up(b4, x3, depth3)
    x3, z3 = smooth(x3, z3, level3, depth3, SWEEPS)
    up(x3, x2, depth2)
    x2, z2 = smooth(x2, z2, level2, depth2, SWEEPS)

    level1 = (wx1, wy1, wz1, gain1, scaled1, None)
    at_x, at_y = lax.axis_index(GX), lax.axis_index(GY)
    planes1, count1, _, _, lanes1 = v1.shape
    n1, r1 = planes1 - 2 * COARSE, 8 * count1 - 2 * COARSE
    sub = iota((8, LANES), 0)
    reach = SWEEPS + 2
    first, last = -((reach + 1) // 2), (n1 + reach + 1) // 2
    pad = rows2 + 8
    e1[0, :8] = jnp.zeros((8, LANES), F32)
    e1[0, pad:] = jnp.zeros((8, LANES), F32)
    window = []
    for t in range(first, last):
        x = at_x * per + t
        inside = (x >= 0) & (x < gx * per)
        x = jnp.clip(x, 0, gx * per - 1)
        block = x // m2
        slot = t - first
        for j in range(j2):
            value = x2[1 + x - block * m2, j, 0]
            value = jnp.where(block == 0, value, roll(value, depth2, 1))
            e1[0, pl.ds(8 + j, 8, stride=j2), :] = jnp.where(inside, value, 0.0)
        base = pl.multiple_of(at_y * r2, 8)
        above, here, after = (e1[0, pl.ds(base + 8 * k, 8), :] for k in range(3))
        t1[slot, 0, 0] = here
        t1[slot, 1, 0] = jnp.where(sub < 4, after, above)
    wide = jnp.concatenate([t1[slot, k, 0] for slot in range(last - first) for k in range(2)], 0)
    matrix = jnp.where(iota((LANES, lanes1), 0) == iota((LANES, lanes1), 1) // 2, 1.0, 0.0).astype(F32)
    double[0, :wide.shape[0]] = dot(wide, matrix)
    for t in range(first, last):
        part = [double[0, pl.ds(16 * (t - first) + j, 8, stride=2), :] for j in range(2)]
        for k in range(2):
            p = COARSE + 2 * t + k
            for j in range(count1):
                u1[p, j, 0] = v1[p, j, 0] + part[j // 2]
    sweep(reader(u1), t1, level1, COARSE - 4, COARSE + n1 + 4)
    sweep(reader(t1), u1, level1, COARSE - 3, COARSE + n1 + 3)
    sweep(reader(u1), t1, level1, COARSE - 2, COARSE + n1 + 2)

    level0 = (wx0, wy0, wz0, gain0, scaled0, None)
    nx, ny, nz = out.shape
    pieces = nz // LANES
    rows0 = ny + 2 * FINE
    count0 = rows0 // 8

    wide = []
    for k in range(n1 + 4):
        for j in range(count1):
            e1[k, pl.ds(j, 8, stride=count1), :] = t1[COARSE - 2 + k, j, 0]
        wide.append(e1[k, :r1])
        wide.append(jnp.where(sub < 2, e1[k, r1:r1 + 8], roll(e1[k, r1 + 8:r1 + 16], 4, 0)))
    matrix = jnp.where(iota((lanes1, nz), 0) == iota((lanes1, nz), 1) // 2, 1.0, 0.0).astype(F32)
    wide = dot(jnp.concatenate(wide, 0), matrix)
    base = SOURCE + COARSE - LOCAL
    beyond = 2 * n1 + 2 * SOURCE + 2 * COARSE
    for k in range(n1 + 4):
        at = k * (r1 + 8)
        for t in range(pieces):
            lanes = slice(t * LANES, (t + 1) * LANES)
            for i in range(2):
                double[t, pl.ds(i, r1, stride=2), :] = wide[at:at + r1, lanes]
                double[t, pl.ds(ny + i, 4, stride=2), :] = wide[at + r1:at + r1 + 4, lanes]
            value = double[t, :rows0]
            for i in range(2):
                p = 2 * k + i
                q = p - FINE
                if p < FINE - POST or q >= nx + POST:
                    continue
                if -1 <= q <= nx:
                    own = v0[q + 1, :, lanes]
                else:
                    message, slot = (across.low, q + POST) if q < 0 else (across.high, q - nx - 1)
                    own = jnp.concatenate([message(base + 4 * slot + 2 * h + t) for h in range(2)], 0)
                side = pl.ds(t * FINE, FINE)
                at_side = beyond + p - (FINE - POST)
                side = jnp.concatenate((beside.high(at_side, side), beside.low(at_side, side)), 0)
                field[p, t, :ny] = own + value[:ny]
                field[p, t, ny:] = side + value[ny:]

    def arrange(p):
        for j in range(count0):
            for t in range(pieces):
                u0[p, j, t] = field[p, t, pl.ds(j, 8, stride=count0), :]

    planes(FINE - POST, FINE + nx + POST, arrange)
    sweep(reader(u0), t0, level0, FINE - 2, FINE + nx + 2)
    sweep(reader(t0), u0, level0, FINE - 1, FINE + nx + 1)
    sweep(reader(u0), t0, level0, FINE, FINE + nx)

    def put(k):
        for t in range(pieces):
            for j in range(count0):
                field[k, t, pl.ds(j, 8, stride=count0), :] = t0[FINE + k, j, t]
            out[k, :, t * LANES:(t + 1) * LANES] = field[k, t, :ny]

    planes(0, nx, put)


def limit(scratch, more):
    need = sum(4 * math.prod(x.inner_aval.shape) for x in scratch)
    return pltpu.CompilerParams(vmem_limit_bytes=SPARE + need + 2 * more)


def call(kernel, outs, scratch, *args, specs=None):
    if specs is None:
        specs = [None] * len(args)
    args = [x if spec and spec.memory_space == pl.ANY else pltpu.with_memory_space_constraint(x, pltpu.HBM if spec else pltpu.VMEM) for x, spec in zip(args, specs)]
    size = sum(4 * math.prod(x.shape) for x, spec in zip(args, specs) if spec)
    whole = pl.BlockSpec(memory_space=pltpu.VMEM)
    return pl.pallas_call(
        kernel,
        grid=(1,) if any(spec and spec.block_shape for spec in specs) else (),
        out_shape=outs,
        in_specs=[spec or whole for spec in specs],
        out_specs=[whole for _ in outs],
        scratch_shapes=scratch,
        compiler_params=limit(scratch, size),
    )(*args)


def shape(*dims):
    return pltpu.VMEM(dims, F32)


def swap(first, second, axis):
    count = lax.axis_size(axis)
    even = [(i, i ^ 1) for i in range(count) if i ^ 1 < count]
    odd = [(i, ((i + 1) ^ 1) - 1) for i in range(count) if 0 <= ((i + 1) ^ 1) - 1 < count]
    return lax.ppermute(first, axis, even), lax.ppermute(second, axis, odd)


def spread(send):
    found = lax.all_to_all(send, (GX, GY[0]), 0, 0)
    return found, lax.ppermute(found, GY[1], [(0, 1), (1, 0)])


def body(guess, right_side, coefficient):
    gx, gy = lax.axis_size(GX), lax.axis_size(GY)
    nx, ny, nz = guess.shape
    n1, r1, z1 = nx // 2, ny // 2, nz // 2
    n2, r2 = n1 // 2, r1 // 2
    planes0, rows0, pieces = nx + 2 * FINE, ny + 2 * FINE, nz // LANES
    whole = pl.BlockSpec(memory_space=pltpu.VMEM)
    fields = (guess, right_side, coefficient)

    ends = [pl.BlockSpec((FINE, ny, nz), lambda i, at=at: (at, 0, 0)) for at in (0, nx // FINE - 1)]
    across = swap(*call(
        edge_kernel, (shape(sum(WIDTHS), ny, nz),) * 2, (), *(f for f in fields for _ in range(2)), specs=ends * 3
    ), GX)
    own_up, own_down, c1, send = call(
        own_kernel,
        (shape(3 * nx, FINE, nz),) * 2 + (shape(n1, r1, z1), shape(gx * gy // 2, n2 // 2, r2, LANES)),
        [vmem(n1 * ny, LANES)] * pieces,
        *fields, specs=[whole] * 3,
    )
    gathered_c = spread(send)
    corners = 3 * nx + 2 * sum(WIDTHS)
    rows = call(corner_kernel, (shape(corners, FINE, nz),) * 2, (), own_up, own_down, *across)
    beside = swap(*rows, GY)
    fields = call(
        keep_kernel, (shape(nx, ny, nz),) * 3, (), *fields, gathered_c[1], rows[0],
        specs=[whole] * 3 + [pl.BlockSpec(memory_space=pl.ANY)] * 2,
    )

    block0 = (planes0, rows0 // 8, pieces, 8, LANES)
    plain0 = (planes0, pieces, rows0, LANES)
    message = (SOURCE + COARSE - LOCAL + 4 * SENT, r1, z1)
    v0, *level0, first, second, b1, local = call(
        fine_pre_kernel,
        (shape(nx + 2, ny, nz),) + (shape(*block0),) * 5 + (shape(*message),) * 2 + (shape(n1, r1, z1), shape(2 * LOCAL, r1, z1)),
        [vmem(*plain0)] * 3 + [vmem(*block0)] * 3 + [vmem(n1 * rows0, LANES)] * pieces,
        *fields, c1, *across, *beside, specs=[None] * 8,
    )
    across = swap(first, second, GX)
    count = 3 * n1 + 2 * SOURCE + 2 * COARSE + 2 * POST + n1
    rows = call(rows_kernel, (shape(count, COARSE, z1),) * 2, (), b1, c1, local, v0, *across)
    beside = swap(*rows, GY)

    planes1, rows1 = n1 + 2 * COARSE, r1 + 2 * COARSE
    block1 = (planes1, rows1 // 8, 1, 8, z1)
    plain1 = (planes1, rows1, z1)
    v1, *level1, send = call(
        coarse_pre_kernel,
        (shape(*block1),) * 6 + (shape(gx * gy // 2, n2 // 2, r2, LANES),),
        [vmem(*plain1)] * 2 + [vmem(*block1)] * 2 + [vmem(n2 // 2 * r2, LANES)] * 2,
        b1, c1, local, *across, *beside, rows[0],
        specs=[None] * 7 + [pl.BlockSpec(memory_space=pl.ANY)],
    )
    gathered_b = spread(send)

    m2, rows2 = gx * n2 // 2, gy * r2
    m3, m4 = m2 // 4, m2 // 16
    block2, block3, block4 = ((m + 2, rows2 // part, 1, 8, LANES) for m, part in ((m2, 8), (m3, 16), (m4, 32)))
    scratch = (
        [vmem(*block2)] * 3 + [vmem(2, m2, rows2, LANES)] + [vmem(*block2)] * 6
        + [vmem(*block3)] * 10 + [vmem(*block4)] * 8
        + [vmem(*block1)] * 2 + [vmem(planes1, max(rows2 + 16, rows1), z1)]
        + [vmem(*plain0)] + [vmem(*block0)] * 2 + [vmem(pieces, 256, LANES)]
    )
    (out,) = pl.pallas_call(
        partial(solve_kernel, gx=gx, gy=gy),
        out_shape=(jax.ShapeDtypeStruct((nx, ny, nz), F32),),
        in_specs=[whole] * 20,
        out_specs=(whole,),
        scratch_shapes=scratch,
        compiler_params=limit(scratch, guess.size * 4),
    )(*(pltpu.with_memory_space_constraint(x, pltpu.VMEM)
        for x in (*gathered_b, *gathered_c, v1, *level1, v0, *level0, *across, *beside)))
    return out


def solution(mesh):
    gx, gy = mesh.devices.shape
    mesh = Mesh(mesh.devices.reshape(gx, gy // 2, 2), (GX, *GY))
    return jax.shard_map(
        body,
        mesh=mesh,
        in_specs=(P(GX, GY, None),) * 3,
        out_specs=P(GX, GY, None),
        check_vma=False,
    )
```

```python
import math
from functools import partial

import jax
import jax.numpy as jnp
from jax import lax
from jax.experimental import pallas as pl
from jax.experimental.pallas import tpu as pltpu
from jax.sharding import Mesh, PartitionSpec as P

LEVELS = 4
SWEEPS = 3
CHEB = 8

RELAX_WEIGHT = 0.7
CHEBY_LOWER = 0.08
CHEBY_UPPER = 2.0

F32 = jnp.float32
LANES = 128
PARTS = 2
FINE = SWEEPS + 1
WIDTHS = (FINE - 1, FINE - 1, FINE)
COARSE = 8
SOURCE = COARSE - 1
LOCAL = FINE // 2
POST = SWEEPS
SENT = POST - 1
BLOCK = 24
SPARE = 4 * 1024 * 1024


def dot(a, b):
    b = b.astype(jnp.bfloat16)
    parts = []
    for _ in range(PARTS):
        parts.append(a.astype(jnp.bfloat16))
        a = a - parts[-1].astype(F32)
    found = [jnp.dot(part, b, preferred_element_type=F32) for part in reversed(parts)]
    return sum(found[1:], found[0])


def iota(shape, dim):
    return lax.broadcasted_iota(jnp.int32, shape, dim)


def vmem(*shape):
    return pltpu.VMEM(shape, F32)


def roll(x, by, axis):
    return pltpu.roll(x, by % x.shape[axis], axis)


GX, GY = "gx", ("gy_far", "gy_near")


def is_even(axis):
    return lax.axis_index(axis) % 2 == 0


class Sides:
    def __init__(self, axis, first, second):
        self.even, self.first, self.second = is_even(axis), first, second

    def low(self, *at):
        return jnp.where(self.even, self.second[at], self.first[at])

    def high(self, *at):
        return jnp.where(self.even, self.first[at], self.second[at])


def address(axis, first, second, write):
    even = is_even(axis)
    pl.when(even)(lambda: write(first, second))
    pl.when(jnp.logical_not(even))(lambda: write(second, first))


def planes(first, last, step):
    if last - first <= BLOCK:
        for p in range(first, last):
            step(p)
    else:
        lax.fori_loop(first, last, lambda p, carry: (step(p), carry)[1], 0, unroll=4)


def lane_before(x, t, lane):
    moved = roll(x[t], 1, 1)
    return moved if len(x) == 1 else jnp.where(lane == 0, roll(x[t - 1], 1, 1), moved)


def lane_after(x, t, lane):
    moved = roll(x[t], -1, 1)
    return moved if len(x) == 1 else jnp.where(lane == LANES - 1, roll(x[(t + 1) % len(x)], -1, 1), moved)


def weigh(fetch, source, level, first, last, depth, row_edges, scale, omega):
    wx, wy, wz, gain, scaled, total = level
    count, pieces = wy.shape[1:3]
    lane = iota((8, LANES), 1)
    front, back = lane % depth == 0, lane % depth == depth - 1
    top, bottom = iota((8, LANES), 0) == 0, iota((8, LANES), 0) == 7

    def step(p):
        for j in range(count):
            c = [fetch(p, j, t) for t in range(pieces)]
            for t in range(pieces):
                x = c[t]
                lower, upper = fetch(p - 1, j, t), fetch(p + 1, j, t)
                left = fetch(p, j - 1, t) if j else roll(fetch(p, count - 1, t), 1, 0)
                right = fetch(p, j + 1, t) if j < count - 1 else roll(fetch(p, 0, t), -1, 0)
                if row_edges and j == 0:
                    left = jnp.where(top, 0.0, left)
                if row_edges and j == count - 1:
                    right = jnp.where(bottom, 0.0, right)
                near, far = lane_before(c, t, lane), lane_after(c, t, lane)
                if t == 0:
                    near = jnp.where(front, 0.0, near)
                if t == pieces - 1:
                    far = jnp.where(back, 0.0, far)
                below, beside, before = x + lower, x + left, x + near
                s = (below + beside + before) + (3.0 * x + (upper + right + far))
                wx[p, j, t] = below
                if last is not None:
                    wx[p + 1, j, t] = x + upper
                wy[p, j, t] = jnp.where(top, 0.0, beside) if row_edges and j == 0 else beside
                wz[p, j, t] = jnp.where(front, 0.0, before) if t == 0 else before
                gain[p, j, t] = jnp.where(x > 0.0, omega / s, 0.0)
                scaled[p, j, t] = source(p, j, t) * (2.0 / scale)
                if total is not None:
                    total[p, j, t] = s

    planes(first, last, step)


def around(fetch, level, p, finish):
    wx, wy, wz = level[:3]
    count, pieces = wy.shape[1:3]
    lane = iota((8, LANES), 1)
    v = [[fetch(p, j, t) for t in range(pieces)] for j in range(count)]
    beside = [wy[p, 0, t] for t in range(pieces)]
    wrap = [roll(beside[t] * v[0][t], -1, 0) for t in range(pieces)]
    for j in range(count):
        ahead = [wy[p, j + 1, t] for t in range(pieces)] if j < count - 1 else None
        before = [wz[p, j, t] for t in range(pieces)]
        flow = [before[t] * v[j][t] for t in range(pieces)]
        for t in range(pieces):
            total = wx[p, j, t] * fetch(p - 1, j, t) + wx[p + 1, j, t] * fetch(p + 1, j, t)
            total += beside[t] * (v[j - 1][t] if j else roll(v[count - 1][t], 1, 0))
            total += ahead[t] * v[j + 1][t] if j < count - 1 else wrap[t]
            total += before[t] * lane_before(v[j], t, lane) + lane_after(flow, t, lane)
            finish(j, t, v[j][t], total)
        beside = ahead


def reader(ref):
    return lambda p, j, t: ref[p, j, t]


def sweep(fetch, out, level, first, last):
    gain, scaled = level[3:5]

    def step(p):
        def finish(j, t, v, total):
            out[p, j, t] = (1.0 - RELAX_WEIGHT) * v + gain[p, j, t] * (scaled[p, j, t] + total)

        around(fetch, level, p, finish)

    planes(first, last, step)


def start(out, level, first, last):
    gain, scaled = level[3:5]

    def step(p):
        for j in range(out.shape[1]):
            for t in range(out.shape[2]):
                out[p, j, t] = gain[p, j, t] * scaled[p, j, t]

    planes(first, last, step)


def residual(fetch, level, p):
    scaled, total = level[4:6]
    found = {}

    def finish(j, t, v, near):
        found[j, t] = (scaled[p, j, t] + near) - v * total[p, j, t]

    around(fetch, level, p, finish)
    return found


def halve_lanes(lanes, width, value, offset=0):
    return jnp.where(iota((lanes, width), 0) // 2 + offset == iota((lanes, width), 1), value, 0.0).astype(F32)


def pack_lanes(lanes, value):
    return jnp.concatenate((halve_lanes(lanes, LANES, value), halve_lanes(lanes, LANES, value, lanes // 2)), 0)


def even_odd(ref, count):
    return ref[pl.ds(0, count, stride=2), :] + ref[pl.ds(1, count, stride=2), :]


def edge_kernel(guess0, guess1, source0, source1, coef0, coef1, first, second):
    def write(up, down):
        at = 0
        for lower, upper, width in zip((guess0, source0, coef0), (guess1, source1, coef1), WIDTHS):
            up[at:at + width] = upper[FINE - width:]
            down[at:at + width] = lower[:width]
            at += width
        far = WIDTHS[0]
        up[far] = source1[1] + 0.5 * (coef1[1] + coef1[0]) * guess1[0]
        far += WIDTHS[1] - 1
        down[far] = source0[FINE - 2] + 0.5 * (coef0[FINE - 2] + coef0[FINE - 1]) * guess0[FINE - 1]

    address(GX, first, second, write)


def own_kernel(guess, source, coef, up, down, c1, send, *pairs):
    nx, ny, nz = guess.shape
    pieces = nz // LANES
    n1, r1 = nx // 2, ny // 2
    for which, field in enumerate((guess, source, coef)):
        def edges(k):
            up[which * nx + k] = field[k, ny - FINE:, :]
            down[which * nx + k] = field[k, :FINE, :]

        planes(0, nx, edges)
    for q in range(n1):
        for t in range(pieces):
            lanes = slice(t * LANES, (t + 1) * LANES)
            pairs[t][q * ny:(q + 1) * ny, :] = coef[2 * q, :, lanes] + coef[2 * q + 1, :, lanes]
    wide = jnp.concatenate([even_odd(pairs[t], n1 * r1) for t in range(pieces)], 1)
    c1[...] = dot(wide, halve_lanes(nz, nz // 2, 0.125)).reshape(n1, r1, nz // 2)

    n2, r2 = n1 // 2, r1 // 2
    for q in range(n2):
        pairs[0][q * r1:(q + 1) * r1, :] = c1[2 * q] + c1[2 * q + 1]
    narrow = even_odd(pairs[0], n2 * r2)
    wide = jnp.concatenate((narrow[:n2 * r2 // 2], narrow[n2 * r2 // 2:]), 1)
    c2 = dot(wide, pack_lanes(nz // 2, 0.125)).reshape(n2 // 2, r2, LANES)
    for d in range(send.shape[0]):
        send[d] = c2


def keep_kernel(guess, source, coef, *rest):
    guess_out, source_out, coef_out = rest[-3:]
    guess_out[...] = guess[...]
    source_out[...] = source[...]
    coef_out[...] = coef[...]


def corner_kernel(own_up, own_down, one, two, first, second):
    nx = own_up.shape[0] // 3
    sides = Sides(GX, one, two)
    ny = one.shape[1]

    def write(up, down):
        at = base = 0
        for which, width in enumerate(WIDTHS):
            for k in range(width):
                for message, slot in ((sides.low, at + k), (sides.high, at + width + nx + k)):
                    up[slot] = message(base + k, pl.ds(ny - FINE, FINE))
                    down[slot] = message(base + k, pl.ds(0, FINE))
            for k in range(nx):
                up[at + width + k] = own_up[which * nx + k]
                down[at + width + k] = own_down[which * nx + k]
            at += nx + 2 * width
            base += width

    address(GY, first, second, write)


def fine_pre_kernel(guess, source, coef, c1, one, two, three, four,
                    out, wx, wy, wz, gain, scaled, first, second, b1, local,
                    field, force, c, v, w, total, *pairs):
    nx, ny, nz = guess.shape
    across, beside = Sides(GX, one, two), Sides(GY, three, four)
    pieces = nz // LANES
    rows = ny + 2 * FINE
    count = rows // 8
    planes0 = nx + 2 * FINE
    level = (wx, wy, wz, gain, scaled, total)

    def fill(target, own, which):
        width = WIDTHS[which]
        at = FINE - width
        offset = sum(nx + 2 * k for k in WIDTHS[:which])
        message = sum(WIDTHS[:which])

        def rest(k):
            side = jnp.concatenate((beside.high(offset + k), beside.low(offset + k)), 0)
            for t in range(pieces):
                target[at + k, t, ny:] = side[:, t * LANES:(t + 1) * LANES]

        planes(0, nx + 2 * width, rest)

        def main(k):
            for t in range(pieces):
                target[FINE + k, t, :ny] = own[k, :, t * LANES:(t + 1) * LANES]

        planes(0, nx, main)
        for k in range(width):
            for t in range(pieces):
                place = (message + k, slice(None), slice(t * LANES, (t + 1) * LANES))
                target[at + k, t, :ny] = across.low(*place)
                target[FINE + nx + k, t, :ny] = across.high(*place)

    def spaced(ref):
        return lambda p, j, t: ref[p, t, pl.ds(j, 8, stride=count), :]

    fill(field, guess, 0)
    fill(force, source, 1)
    fill(c, coef, 2)
    def arrange(p):
        for j in range(count):
            for t in range(pieces):
                w[p, j, t] = spaced(c)(p, j, t)

    planes(0, planes0, arrange)
    weigh(reader(w), spaced(force), level, 1, planes0 - 1, LANES, False, 1.0, RELAX_WEIGHT)

    def arrange_field(p):
        for j in range(count):
            for t in range(pieces):
                v[p, j, t] = spaced(field)(p, j, t)

    planes(1, planes0 - 1, arrange_field)
    for p, face in ((0, 1), (planes0 - 1, planes0 - 1)):
        for j in range(count):
            for t in range(pieces):
                v[p, j, t] = jnp.zeros((8, LANES), F32)
                wx[face, j, t] = jnp.zeros((8, LANES), F32)
    sweep(reader(v), w, level, 1, planes0 - 1)
    sweep(reader(w), v, level, 2, planes0 - 2)
    sweep(reader(v), w, level, 3, planes0 - 3)

    def put(k):
        for t in range(pieces):
            for j in range(count):
                field[k, t, pl.ds(j, 8, stride=count), :] = w[FINE - 1 + k, j, t]
            out[k, :, t * LANES:(t + 1) * LANES] = field[k, t, :ny]

    planes(0, nx + 2, put)

    n1, r1 = nx // 2, ny // 2

    def coarsen(value, number):
        wide = jnp.concatenate(
            [jnp.concatenate([even_odd(pairs[t].at[pl.ds(q * rows, ny)], r1) for t in range(pieces)], 1) for q in range(number)], 0
        )
        return dot(wide, halve_lanes(nz, nz // 2, value)).reshape(number, r1, nz // 2)

    for k in range(2 * LOCAL):
        p = 2 * k if k < LOCAL else nx + 2 * k
        for t in range(pieces):
            pairs[t][k * rows:k * rows + ny, :] = c[p, t, :ny] + c[p + 1, t, :ny]
    local[...] = coarsen(0.125, 2 * LOCAL)

    def halve(q):
        one, two = (residual(reader(w), level, FINE + 2 * q + k) for k in range(2))
        for j in range(count):
            for t in range(pieces):
                pairs[t][pl.ds(q * rows + j, 8, stride=count), :] = one[j, t] + two[j, t]

    planes(0, n1, halve)
    b1[...] = coarsen(0.125 * 0.5, n1)

    def write(up, down):
        up[:SOURCE] = b1[n1 - SOURCE:]
        down[:SOURCE] = b1[:SOURCE]
        at = SOURCE + COARSE - LOCAL
        up[SOURCE:at] = c1[n1 - COARSE:n1 - LOCAL]
        down[SOURCE:at] = c1[LOCAL:COARSE]
        for k in range(SENT):
            for i in range(2):
                for j in range(2):
                    here, lanes = pl.ds(i * r1, r1), pl.ds(j * (nz // 2), nz // 2)
                    up[at] = out[nx - POST + 1 + k, here, lanes]
                    down[at] = out[2 + k, here, lanes]
                    at += 1

    address(GX, first, second, write)


def rows_kernel(b1, c1, local, v, one, two, first, second):
    n1, r1, half = b1.shape
    nx, ny = 2 * n1, 2 * r1
    sides = Sides(GX, one, two)

    def write(up, down):
        def edge(take, at):
            up[at] = take(pl.ds(r1 - COARSE, COARSE))
            down[at] = take(pl.ds(0, COARSE))

        at = base = 0
        for own, width, known in ((b1, SOURCE, 0), (c1, COARSE, LOCAL)):
            near = width - 1
            for k in range(near - known):
                edge(lambda rows: sides.low(base + 1 + k, rows), at + k)
                edge(lambda rows: sides.high(base + k, rows), at + near + n1 + known + k)
            for k in range(known):
                edge(lambda rows: local[k, rows, :], at + near - known + k)
                edge(lambda rows: local[known + k, rows, :], at + near + n1 + k)
            for k in range(n1):
                edge(lambda rows: own[k, rows, :], at + near + k)
            at += n1 + 2 * near
            base += width - known
        for j in range(2):
            rows, lanes = pl.ds(j * FINE, FINE), pl.ds(j * half, half)
            last, start = pl.ds(r1 - FINE, FINE), pl.ds(0, FINE)
            for k in range(SENT):
                for message, slot in ((sides.low, at + k), (sides.high, at + SENT + nx + 2 + k)):
                    up[slot, rows, :] = message(base + 4 * k + 2 + j, last)
                    down[slot, rows, :] = message(base + 4 * k + j, start)
            for k in range(nx + 2):
                up[at + SENT + k, rows, :] = v[k, ny - FINE:, lanes]
                down[at + SENT + k, rows, :] = v[k, :FINE, lanes]

    address(GY, first, second, write)


def coarse_pre_kernel(b1, c1, local, one, two, three, four, sent,
                      v, wx, wy, wz, gain, scaled, send, field, c, w, total, upper, lower):
    n1, r1, lanes = b1.shape
    rows = r1 + 2 * COARSE
    count = rows // 8
    planes1 = n1 + 2 * COARSE
    scale = 0.25
    level = (wx, wy, wz, gain, scaled, total)
    across, beside = Sides(GX, one, two), Sides(GY, three, four)

    def fill(target, own, base, offset, width, known):
        at = COARSE - width
        for k in range(n1 + 2 * width - 2):
            target[at + 1 + k, r1:r1 + COARSE] = beside.high(offset + k)
            target[at + 1 + k, r1 + COARSE:] = beside.low(offset + k)
        for p in (at, COARSE + n1 + width - 1):
            target[p, r1:] = jnp.zeros((2 * COARSE, lanes), F32)
        for k in range(n1):
            target[COARSE + k, :r1] = own[k]
        for k in range(width - known):
            target[at + k, :r1] = across.low(base + k)
            target[COARSE + n1 + known + k, :r1] = across.high(base + k)
        for k in range(known):
            target[COARSE - known + k, :r1] = local[k]
            target[COARSE + n1 + k, :r1] = local[known + k]

    def spaced(ref):
        return lambda p, j, t: ref[p, pl.ds(j, 8, stride=count), :]

    fill(field, b1, 0, 0, SOURCE, 0)
    fill(c, c1, SOURCE, n1 + 2 * SOURCE - 2, COARSE, LOCAL)
    for p in range(planes1):
        for j in range(count):
            w[p, j, 0] = spaced(c)(p, j, 0)
    weigh(reader(w), spaced(field), level, 1, planes1 - 1, lanes, False, scale, RELAX_WEIGHT)
    start(v, level, 1, planes1 - 1)
    sweep(reader(v), w, level, 2, planes1 - 2)
    sweep(reader(w), v, level, 3, planes1 - 3)

    n2, r2 = n1 // 2, r1 // 2
    half = n2 // 2

    for q in range(n2):
        one, two = (residual(reader(v), level, COARSE + 2 * q + k) for k in range(2))
        target = lower if q < half else upper
        for j in range(count // 2):
            value = (one[2 * j, 0] + two[2 * j, 0]) + (one[2 * j + 1, 0] + two[2 * j + 1, 0])
            target[pl.ds(q % half * r2 + j, r1 // count, stride=count // 2), :] = value[:r1 // count]
    wide = jnp.concatenate((lower[...], upper[...]), 1)
    b2 = dot(wide, pack_lanes(lanes, 0.125 * 0.5 * scale)).reshape(half, r2, LANES)
    for d in range(send.shape[0]):
        send[d] = b2


def pads(ref, depth):
    last = ref.shape[0] - 1
    for j in range(ref.shape[1]):
        ref[0, j, 0] = roll(ref[last - 1, j, 0], depth, 1)
        ref[last, j, 0] = roll(ref[1, j, 0], -depth, 1)


def regroup(depth, back=False):
    dims = (LANES, 2 * LANES) if back else (2 * LANES, LANES)
    source, target = iota(dims, int(back)), iota(dims, 1 - int(back))
    group, lane = source // LANES, source % LANES
    block, z = lane // depth, lane % depth
    return (2 * block + group) * (depth // 2) + z // 2 == target


def solve_kernel(mine_b, other_b, mine_c, other_c, v1, wx1, wy1, wz1, gain1, scaled1, v0, wx0, wy0, wz0, gain0, scaled0,
                 one, two, three, four, out,
                 c2, a2, y2, n2, l2x, l2y, l2z, l2g, l2s, l2t,
                 c3, b3, a3, y3, l3x, l3y, l3z, l3g, l3s, l3t,
                 c4, b4, y4, l4x, l4y, l4z, l4g, l4s,
                 u1, t1, e1, field, u0, t0, double, *, gx, gy):
    level2 = (l2x, l2y, l2z, l2g, l2s, l2t)
    level3 = (l3x, l3y, l3z, l3g, l3s, l3t)
    level4 = (l4x, l4y, l4z, l4g, l4s, None)
    across, beside = Sides(GX, one, two), Sides(GY, three, four)
    half, r2 = mine_b.shape[1:3]
    per = 2 * half
    m2, m3, m4 = c2.shape[0] - 2, c3.shape[0] - 2, c4.shape[0] - 2
    j2, j3, j4 = c2.shape[1], c3.shape[1], c4.shape[1]
    rows2 = 8 * j2
    depth2 = LANES // 2
    depth3, depth4 = depth2 // 2, depth2 // 4
    lane = iota((8, LANES), 1)

    near_one = lax.axis_index(GY[1])

    def unpack(i):
        for j in range(gy):
            for k in range(half):
                for which, (mine, other) in enumerate(((mine_b, other_b), (mine_c, other_c))):
                    def block(x):
                        at = x * (gy // 2) + j // 2
                        return jnp.where(near_one == j % 2, mine[at, k], other[at, k])

                    near, far = block(i), block(i + gx // 2)
                    here = pl.ds(j * r2, r2)
                    n2[which, i * per + k, here, :] = jnp.where(lane < depth2, near, roll(far, depth2, 1))
                    n2[which, i * per + half + k, here, :] = jnp.where(lane < depth2, roll(near, depth2, 1), far)

    planes(0, gx // 2, unpack)

    def spread(p):
        for j in range(j2):
            c2[1 + p, j, 0] = n2[1, p, pl.ds(j, 8, stride=j2), :]

    planes(0, m2, spread)

    def level_in(c, source, level, depth, scale, omega):
        last = c.shape[0] - 1
        lane = iota((8, LANES), 1)
        for j in range(c.shape[1]):
            c[0, j, 0] = jnp.where(lane < depth, 0.0, roll(c[last - 1, j, 0], depth, 1))
            c[last, j, 0] = jnp.where(lane >= LANES - depth, 0.0, roll(c[1, j, 0], -depth, 1))
        weigh(reader(c), source, level, 1, last, depth, True, scale, omega)
        wx = level[0]
        for j in range(c.shape[1]):
            wx[1, j, 0] = jnp.where(lane < depth, 0.0, wx[1, j, 0])
            wx[last, j, 0] = jnp.where(lane >= LANES - depth, 0.0, wx[last, j, 0])

    def smooth(first, other, level, depth, sweeps):
        for _ in range(sweeps):
            pads(first, depth)
            sweep(reader(first), other, level, 1, first.shape[0] - 1)
            first, other = other, first
        return first, other

    def down(fetch, count, rows, depth, out, value):
        def pair(m, g):
            at = g * (count // 2) + 2 * m + 1
            one, two = fetch(at), fetch(at + 1)
            return [(one[2 * j] + two[2 * j]) + (one[2 * j + 1] + two[2 * j + 1]) for j in range(rows // 2)]

        parts = [jnp.concatenate(both, 1) for m in range(count // 4) for both in zip(pair(m, 0), pair(m, 1))]
        matrix = jnp.where(regroup(depth), value, 0.0).astype(F32)
        found = dot(jnp.concatenate(parts, 0), matrix)
        at = 0
        for m in range(count // 4):
            for j in range(rows // 2):
                out[1 + m, j, 0] = found[at:at + 8]
                at += 8

    def up(coarse, fine, depth):
        count, rows = fine.shape[0] - 2, fine.shape[1]
        matrix = jnp.where(regroup(depth, True), 1.0, 0.0).astype(F32)
        x = jnp.concatenate([coarse[1 + m, j, 0] for m in range(count // 4) for j in range(rows // 2)], 0)
        x = dot(x, matrix)
        at = 0
        for m in range(count // 4):
            for j in range(rows // 2):
                for g in range(2):
                    value = x[at:at + 8, g * LANES:(g + 1) * LANES]
                    for k in range(2):
                        p = g * (count // 2) + 2 * m + 1 + k
                        for i in range(2):
                            fine[p, 2 * j + i, 0] = fine[p, 2 * j + i, 0] + value
                at += 8

    def rest(field, level):
        return lambda p: [value for _, value in sorted(residual(reader(field), level, p).items())]

    def whole(ref):
        return lambda p: [ref[p, j, 0] for j in range(ref.shape[1])]

    level_in(c2, lambda p, j, t: n2[0, p - 1, pl.ds(j, 8, stride=j2), :], level2, depth2, 0.25**2, RELAX_WEIGHT)
    start(a2, level2, 1, m2 + 1)
    x2, z2 = smooth(a2, y2, level2, depth2, SWEEPS - 1)
    pads(x2, depth2)
    down(whole(c2), m2, j2, depth2, c3, 0.125)
    down(rest(x2, level2), m2, j2, depth2, b3, 0.125 * 0.5 * 0.25**2)

    level_in(c3, reader(b3), level3, depth3, 0.25**3, RELAX_WEIGHT)
    start(a3, level3, 1, m3 + 1)
    x3, z3 = smooth(a3, y3, level3, depth3, SWEEPS - 1)
    pads(x3, depth3)
    down(whole(c3), m3, j3, depth3, c4, 0.125)
    down(rest(x3, level3), m3, j3, depth3, b4, 0.125 * 0.5 * 0.25**3)

    level_in(c4, reader(b4), level4, depth4, 0.25**4, 1.0)
    theta, delta = (CHEBY_UPPER + CHEBY_LOWER) / 2.0, (CHEBY_UPPER - CHEBY_LOWER) / 2.0
    sigma = theta / delta
    rho = 1.0 / sigma
    cells = [(1 + p, j) for p in range(m4) for j in range(j4)]
    res = {at: l4g[at[0], at[1], 0] * l4s[at[0], at[1], 0] for at in cells}
    direction = {at: res[at] / theta for at in cells}
    total = {at: jnp.zeros((8, LANES), F32) for at in cells}
    for _ in range(CHEB):
        for p, j in cells:
            total[p, j] = total[p, j] + direction[p, j]
            y4[p, j, 0] = direction[p, j]
        pads(y4, depth4)
        for p in range(1, m4 + 1):
            def finish(j, t, v, near):
                res[p, j] = res[p, j] - (v - l4g[p, j, 0] * near)

            around(reader(y4), level4, p, finish)
        rho_new = 1.0 / (2.0 * sigma - rho)
        direction = {at: rho_new * rho * direction[at] + (2.0 * rho_new / delta) * res[at] for at in cells}
        rho = rho_new
    for p, j in cells:
        b4[p, j, 0] = total[p, j]

    up(b4, x3, depth3)
    x3, z3 = smooth(x3, z3, level3, depth3, SWEEPS)
    up(x3, x2, depth2)
    x2, z2 = smooth(x2, z2, level2, depth2, SWEEPS)

    level1 = (wx1, wy1, wz1, gain1, scaled1, None)
    at_x, at_y = lax.axis_index(GX), lax.axis_index(GY)
    planes1, count1, _, _, lanes1 = v1.shape
    n1, r1 = planes1 - 2 * COARSE, 8 * count1 - 2 * COARSE
    sub = iota((8, LANES), 0)
    reach = SWEEPS + 2
    first, last = -((reach + 1) // 2), (n1 + reach + 1) // 2
    pad = rows2 + 8
    e1[0, :8] = jnp.zeros((8, LANES), F32)
    e1[0, pad:] = jnp.zeros((8, LANES), F32)
    window = []
    for t in range(first, last):
        x = at_x * per + t
        inside = (x >= 0) & (x < gx * per)
        x = jnp.clip(x, 0, gx * per - 1)
        block = x // m2
        slot = t - first
        for j in range(j2):
            value = x2[1 + x - block * m2, j, 0]
            value = jnp.where(block == 0, value, roll(value, depth2, 1))
            e1[0, pl.ds(8 + j, 8, stride=j2), :] = jnp.where(inside, value, 0.0)
        base = pl.multiple_of(at_y * r2, 8)
        above, here, after = (e1[0, pl.ds(base + 8 * k, 8), :] for k in range(3))
        t1[slot, 0, 0] = here
        t1[slot, 1, 0] = jnp.where(sub < 4, after, above)
    wide = jnp.concatenate([t1[slot, k, 0] for slot in range(last - first) for k in range(2)], 0)
    matrix = jnp.where(iota((LANES, lanes1), 0) == iota((LANES, lanes1), 1) // 2, 1.0, 0.0).astype(F32)
    double[0, :wide.shape[0]] = dot(wide, matrix)
    for t in range(first, last):
        part = [double[0, pl.ds(16 * (t - first) + j, 8, stride=2), :] for j in range(2)]
        for k in range(2):
            p = COARSE + 2 * t + k
            for j in range(count1):
                u1[p, j, 0] = v1[p, j, 0] + part[j // 2]
    sweep(reader(u1), t1, level1, COARSE - 4, COARSE + n1 + 4)
    sweep(reader(t1), u1, level1, COARSE - 3, COARSE + n1 + 3)
    sweep(reader(u1), t1, level1, COARSE - 2, COARSE + n1 + 2)

    level0 = (wx0, wy0, wz0, gain0, scaled0, None)
    nx, ny, nz = out.shape
    pieces = nz // LANES
    rows0 = ny + 2 * FINE
    count0 = rows0 // 8

    wide = []
    for k in range(n1 + 4):
        for j in range(count1):
            e1[k, pl.ds(j, 8, stride=count1), :] = t1[COARSE - 2 + k, j, 0]
        wide.append(e1[k, :r1])
        wide.append(jnp.where(sub < 2, e1[k, r1:r1 + 8], roll(e1[k, r1 + 8:r1 + 16], 4, 0)))
    matrix = jnp.where(iota((lanes1, nz), 0) == iota((lanes1, nz), 1) // 2, 1.0, 0.0).astype(F32)
    wide = dot(jnp.concatenate(wide, 0), matrix)
    base = SOURCE + COARSE - LOCAL
    beyond = 2 * n1 + 2 * (SOURCE - 1) + 2 * (COARSE - 1)
    for k in range(n1 + 4):
        at = k * (r1 + 8)
        for t in range(pieces):
            lanes = slice(t * LANES, (t + 1) * LANES)
            for i in range(2):
                double[t, pl.ds(i, r1, stride=2), :] = wide[at:at + r1, lanes]
                double[t, pl.ds(ny + i, 4, stride=2), :] = wide[at + r1:at + r1 + 4, lanes]
            value = double[t, :rows0]
            for i in range(2):
                p = 2 * k + i
                q = p - FINE
                if p < FINE - POST or q >= nx + POST:
                    continue
                if -1 <= q <= nx:
                    own = v0[q + 1, :, lanes]
                else:
                    message, slot = (across.low, q + POST) if q < 0 else (across.high, q - nx - 1)
                    own = jnp.concatenate([message(base + 4 * slot + 2 * h + t) for h in range(2)], 0)
                side = pl.ds(t * FINE, FINE)
                at_side = beyond + p - (FINE - POST)
                side = jnp.concatenate((beside.high(at_side, side), beside.low(at_side, side)), 0)
                field[p, t, :ny] = own + value[:ny]
                field[p, t, ny:] = side + value[ny:]

    def arrange(p):
        for j in range(count0):
            for t in range(pieces):
                u0[p, j, t] = field[p, t, pl.ds(j, 8, stride=count0), :]

    planes(FINE - POST, FINE + nx + POST, arrange)
    sweep(reader(u0), t0, level0, FINE - 2, FINE + nx + 2)
    sweep(reader(t0), u0, level0, FINE - 1, FINE + nx + 1)

    def put(k):
        def finish(j, t, v, total):
            value = (1.0 - RELAX_WEIGHT) * v + gain0[FINE + k, j, t] * (scaled0[FINE + k, j, t] + total)
            field[k, t, pl.ds(j, 8, stride=count0), :] = value

        around(reader(u0), level0, FINE + k, finish)
        for t in range(pieces):
            out[k, :, t * LANES:(t + 1) * LANES] = field[k, t, :ny]

    planes(0, nx, put)


def limit(scratch, more):
    need = sum(4 * math.prod(x.inner_aval.shape) for x in scratch)
    return pltpu.CompilerParams(vmem_limit_bytes=SPARE + need + 2 * more)


def call(kernel, outs, scratch, *args, specs=None):
    if specs is None:
        specs = [None] * len(args)
    args = [x if spec and spec.memory_space == pl.ANY else pltpu.with_memory_space_constraint(x, pltpu.HBM if spec else pltpu.VMEM) for x, spec in zip(args, specs)]
    size = sum(4 * math.prod(x.shape) for x, spec in zip(args, specs) if spec)
    whole = pl.BlockSpec(memory_space=pltpu.VMEM)
    return pl.pallas_call(
        kernel,
        grid=(1,) if any(spec and spec.block_shape for spec in specs) else (),
        out_shape=outs,
        in_specs=[spec or whole for spec in specs],
        out_specs=[whole for _ in outs],
        scratch_shapes=scratch,
        compiler_params=limit(scratch, size),
    )(*args)


def shape(*dims):
    return pltpu.VMEM(dims, F32)


def swap(first, second, axis):
    count = lax.axis_size(axis)
    even = [(i, i ^ 1) for i in range(count) if i ^ 1 < count]
    odd = [(i, ((i + 1) ^ 1) - 1) for i in range(count) if 0 <= ((i + 1) ^ 1) - 1 < count]
    return lax.ppermute(first, axis, even), lax.ppermute(second, axis, odd)


def spread(send):
    found = lax.all_to_all(send, (GX, GY[0]), 0, 0)
    return found, lax.ppermute(found, GY[1], [(0, 1), (1, 0)])


def body(guess, right_side, coefficient):
    gx, gy = lax.axis_size(GX), lax.axis_size(GY)
    nx, ny, nz = guess.shape
    n1, r1, z1 = nx // 2, ny // 2, nz // 2
    n2, r2 = n1 // 2, r1 // 2
    planes0, rows0, pieces = nx + 2 * FINE, ny + 2 * FINE, nz // LANES
    whole = pl.BlockSpec(memory_space=pltpu.VMEM)
    fields = (guess, right_side, coefficient)

    ends = [pl.BlockSpec((FINE, ny, nz), lambda i, at=at: (at, 0, 0)) for at in (0, nx // FINE - 1)]
    across = swap(*call(
        edge_kernel, (shape(sum(WIDTHS), ny, nz),) * 2, (), *(f for f in fields for _ in range(2)), specs=ends * 3
    ), GX)
    own_up, own_down, c1, send = call(
        own_kernel,
        (shape(3 * nx, FINE, nz),) * 2 + (shape(n1, r1, z1), shape(gx * gy // 2, n2 // 2, r2, LANES)),
        [vmem(n1 * ny, LANES)] * pieces,
        *fields, specs=[whole] * 3,
    )
    gathered_c = spread(send)
    corners = 3 * nx + 2 * sum(WIDTHS)
    rows = call(corner_kernel, (shape(corners, FINE, nz),) * 2, (), own_up, own_down, *across)
    beside = swap(*rows, GY)
    fields = call(
        keep_kernel, (shape(nx, ny, nz),) * 3, (), *fields, gathered_c[1], rows[0],
        specs=[whole] * 3 + [pl.BlockSpec(memory_space=pl.ANY)] * 2,
    )

    block0 = (planes0, rows0 // 8, pieces, 8, LANES)
    plain0 = (planes0, pieces, rows0, LANES)
    message = (SOURCE + COARSE - LOCAL + 4 * SENT, r1, z1)
    v0, *level0, first, second, b1, local = call(
        fine_pre_kernel,
        (shape(nx + 2, ny, nz),) + (shape(*block0),) * 5 + (shape(*message),) * 2 + (shape(n1, r1, z1), shape(2 * LOCAL, r1, z1)),
        [vmem(*plain0)] * 3 + [vmem(*block0)] * 3 + [vmem(n1 * rows0, LANES)] * pieces,
        *fields, c1, *across, *beside, specs=[None] * 8,
    )
    across = swap(first, second, GX)
    count = 4 * n1 + 2 * (SOURCE - 1) + 2 * (COARSE - 1) + 2 * POST
    rows = call(rows_kernel, (shape(count, COARSE, z1),) * 2, (), b1, c1, local, v0, *across)
    beside = swap(*rows, GY)

    planes1, rows1 = n1 + 2 * COARSE, r1 + 2 * COARSE
    block1 = (planes1, rows1 // 8, 1, 8, z1)
    plain1 = (planes1, rows1, z1)
    v1, *level1, send = call(
        coarse_pre_kernel,
        (shape(*block1),) * 6 + (shape(gx * gy // 2, n2 // 2, r2, LANES),),
        [vmem(*plain1)] * 2 + [vmem(*block1)] * 2 + [vmem(n2 // 2 * r2, LANES)] * 2,
        b1, c1, local, *across, *beside, rows[0],
        specs=[None] * 7 + [pl.BlockSpec(memory_space=pl.ANY)],
    )
    gathered_b = spread(send)

    m2, rows2 = gx * n2 // 2, gy * r2
    m3, m4 = m2 // 4, m2 // 16
    block2, block3, block4 = ((m + 2, rows2 // part, 1, 8, LANES) for m, part in ((m2, 8), (m3, 16), (m4, 32)))
    scratch = (
        [vmem(*block2)] * 3 + [vmem(2, m2, rows2, LANES)] + [vmem(*block2)] * 6
        + [vmem(*block3)] * 10 + [vmem(*block4)] * 8
        + [vmem(*block1)] * 2 + [vmem(planes1, max(rows2 + 16, rows1), z1)]
        + [vmem(*plain0)] + [vmem(*block0)] * 2 + [vmem(pieces, 256, LANES)]
    )
    (out,) = pl.pallas_call(
        partial(solve_kernel, gx=gx, gy=gy),
        out_shape=(jax.ShapeDtypeStruct((nx, ny, nz), F32),),
        in_specs=[whole] * 20,
        out_specs=(whole,),
        scratch_shapes=scratch,
        compiler_params=limit(scratch, guess.size * 4),
    )(*(pltpu.with_memory_space_constraint(x, pltpu.VMEM)
        for x in (*gathered_b, *gathered_c, v1, *level1, v0, *level0, *across, *beside)))
    return out


def solution(mesh):
    gx, gy = mesh.devices.shape
    mesh = Mesh(mesh.devices.reshape(gx, gy // 2, 2), (GX, *GY))
    return jax.shard_map(
        body,
        mesh=mesh,
        in_specs=(P(GX, GY, None),) * 3,
        out_specs=P(GX, GY, None),
        check_vma=False,
    )
```
